32 devices in a mesh: rep: 4 (over x, core), shard: 8 (over z, y).
Axes of the slice: x: 2, y: 2, z: 4, core: 2. Of those that a mesh axis runs over, the one named last changes fastest.
Arguments:
- tokens: bfloat16 [256, 197, 384], P(('rep', 'shard')), may hold values from -6 to 6
- weights: float32 [2, 384, 4608], P(None, 'shard')
- vectors: float32 [2, 12, 384], P(None, None, 'shard')
- moment_one: float32 [2, 384, 4608], P(None, 'shard'), may hold values from -60 to 60
- moment_two: float32 [2, 384, 4608], P(None, 'shard'), may hold values from 1 to 100
- vector_one: float32 [2, 12, 384], P(None, None, 'shard'), may hold values from -60 to 60
- vector_two: float32 [2, 12, 384], P(None, None, 'shard'), may hold values from 1 to 100
- images: int32 [32], P(('rep', 'shard')), may hold values from 4 to 8, as said below
- cotangent: bfloat16 [256, 197, 384], P(('rep', 'shard')), may hold values from -6 to 6
Outputs:
- output: float32 [256, 197, 384], P(('rep', 'shard'))
- input_grad: float32 [256, 197, 384], P(('rep', 'shard'))
- weight_grad: float32 [2, 384, 4608], P(None, 'shard')
- vector_grad: float32 [2, 12, 384], P(None, None, 'shard')
- moment_one_new: float32 [2, 384, 4608], P(None, 'shard')
- moment_two_new: float32 [2, 384, 4608], P(None, 'shard')
- vector_one_new: float32 [2, 12, 384], P(None, None, 'shard')
- vector_two_new: float32 [2, 12, 384], P(None, None, 'shard')
- update: float32 [2, 384, 4608], P(None, 'shard')
- vector_update: float32 [2, 12, 384], P(None, None, 'shard')
The draws below stay inside these ranges and needn't reach their ends.
Inputs may be any that keep to these rules, and one draw needn't show every extreme that they name: `images`: live image slots of each device; some device has all 8.
All inputs are finite; a program needn't handle non-finite values.
Results may differ from the reference program's by a relative error of at most 0.022.
The reference program's roundings to bfloat16 on the way count: a program that leaves them out, or rounds other values in their place, can miss the bound.
Values may be sent and summed in bfloat16 or wider, within the bound.
No kernel may reach another device: no remote copies, remote signals or barrier semaphores. Data moves between devices by JAX's collectives and lax.ppermute only.
A program may use at most 192 MiB of HBM per device.

```python
import math
import jax
import jax.numpy as jnp
from jax import lax

D = 384
HEADS = 6
HEAD = 64
FF = 1536
SEQ = 197
LAYERS = 2
STEP = 10
IMGS_DEV = 8
IMAGES = 256
COLS = 4608
VROWS = 12
DEVICES = 32


def draw_weights(key, part):
    layers = []
    for index in range(LAYERS):
        keys = jax.random.split(jax.random.fold_in(key, index + 11), 4)
        blocks = [1.0 / math.sqrt(D) * jax.random.truncated_normal(keys[0], -4.0, 4.0, (D, 3 * D), jnp.float32), 4.0 / math.sqrt(D) * jax.random.truncated_normal(keys[1], -4.0, 4.0, (D, D), jnp.float32), 1.0 / math.sqrt(D) * jax.random.truncated_normal(keys[2], -4.0, 4.0, (D, FF), jnp.float32), 1.0 / math.sqrt(FF) * jax.random.truncated_normal(keys[3], -4.0, 4.0, (D, FF), jnp.float32)]
        layers.append(jnp.concatenate(blocks, axis=1))
    return jnp.stack(layers)


def draw_vectors(key, part):
    layers = []
    for index in range(LAYERS):
        keys = jax.random.split(jax.random.fold_in(key, index + 41), 9)

        def gain_draw(subkey, count):
            return 1.0 + 0.1 * jax.random.truncated_normal(subkey, -3.0, 3.0, (count,), jnp.float32)

        def bias_draw(subkey, count):
            return 0.1 * jax.random.truncated_normal(subkey, -4.0, 4.0, (count,), jnp.float32)
        pieces = [gain_draw(keys[0], D), bias_draw(keys[1], D), bias_draw(keys[2], D), bias_draw(keys[3], D), bias_draw(keys[4], D), gain_draw(keys[5], D), bias_draw(keys[6], D), bias_draw(keys[7], D), bias_draw(keys[8], FF)]
        layers.append(jnp.concatenate(pieces).reshape(8 + FF // D, D))
    return jnp.stack(layers)


def draw_images(key, part):
    counts = jax.random.randint(jax.random.fold_in(key, 3), (DEVICES,), (IMGS_DEV + 1) // 2, IMGS_DEV + 1)
    where = jax.random.randint(jax.random.fold_in(key, 7), (), 0, DEVICES)
    return counts.at[where].set(IMGS_DEV).astype(jnp.int32)


def steps_of(rng, shape, cuts, low, largest):
    def one(position, parts):
        heights = jax.random.uniform(jax.random.fold_in(jax.random.fold_in(rng, 6), position), (parts,), jnp.float32, low / len(cuts), largest / len(cuts))
        return jnp.repeat(jnp.exp(heights), shape[position] // parts).reshape((-1,) + (1,) * (len(shape) - position - 1))

    factor_of = one(*cuts[0])
    for cut in cuts[1:]:
        factor_of = factor_of * one(*cut)
    return factor_of


def scatter_about(stream_key, shape, spread, bound, shards=(), kind=jnp.bfloat16):
    array = spread * jax.random.normal(stream_key, shape, jnp.float32)
    if shards:
        array = array * steps_of(stream_key, shape, shards, -0.22, 0.18)
    return jnp.clip(array, -bound, bound).astype(kind)


def setup_inputs(seed: int = 0) -> dict:
    streams_of = jax.random.split(jax.random.key(seed), 10)
    return {
        "tokens": scatter_about(streams_of[0], (IMAGES, SEQ, D), 1.0, 6.0, ((0, 32),)),
        "weights": draw_weights(jax.random.fold_in(streams_of[9], 71), 0),
        "vectors": draw_vectors(jax.random.fold_in(streams_of[9], 71), 0),
        "moment_one": scatter_about(streams_of[3], (LAYERS, D, COLS), 10.0, 60.0, ((1, 8),), jnp.float32),
        "moment_two": jnp.clip(jnp.exp(math.log(100.0) - 4.6051702 * jax.random.uniform(streams_of[4], (LAYERS, D, COLS), jnp.float32) ** steps_of(streams_of[4], (LAYERS, D, COLS), ((1, 8),), -0.2, 0.2)), 1.0, 100.0),
        "vector_one": scatter_about(streams_of[5], (LAYERS, VROWS, D), 10.0, 60.0, ((2, 8),), jnp.float32),
        "vector_two": jnp.clip(jnp.exp(math.log(100.0) - 4.6051702 * jax.random.uniform(streams_of[6], (LAYERS, VROWS, D), jnp.float32) ** steps_of(streams_of[6], (LAYERS, VROWS, D), ((2, 8),), -0.2, 0.2)), 1.0, 100.0),
        "images": draw_images(jax.random.fold_in(streams_of[9], 71), 0),
        "cotangent": scatter_about(streams_of[8], (IMAGES, SEQ, D), 1.0, 6.0, ((0, 32),)),
    }


@jax.custom_vjp
def low(v):
    return lax.optimization_barrier(v.astype(jnp.bfloat16)).astype(jnp.float32)

@jax.custom_vjp
def low_back(v):
    return v

def low_keep(v):
    return (low(v), None)

def low_pass(kept, grad):
    return (grad,)

def back_keep(v):
    return (v, None)

def back_low(kept, grad):
    return (low(grad),)
low.defvjp(low_keep, low_pass)
low_back.defvjp(back_keep, back_low)

def rounded(value):
    return low_back(low(value))

def layer_norm(values, gain, offset):
    center = values - lax.optimization_barrier(jnp.mean(values, -1, keepdims=True))
    scale = lax.rsqrt(lax.optimization_barrier(jnp.mean(center * center, -1, keepdims=True)) + 1e-06)
    return center * scale * gain + offset

def matmul(left, right):
    return jnp.einsum('bsd,de->bse', left, right, precision=lax.Precision.HIGHEST)

def attend(query, key_part, value):
    scores = jnp.einsum('bshd,bthd->bhst', query, key_part, precision=lax.Precision.HIGHEST) / 8.0
    scores = low_back(scores)
    probs = jax.nn.softmax(scores, axis=-1)
    return jnp.einsum('bhst,bthd->bshd', low(probs), value, precision=lax.Precision.HIGHEST)

def layer(values, matrix, vector):
    matrix = low(matrix)
    vector = low(vector)
    w_qkv = matrix[:, :3 * D]
    w_out = matrix[:, 3 * D:4 * D]
    w_up = matrix[:, 4 * D:4 * D + FF]
    w_down_t = matrix[:, 4 * D + FF:]
    gain1 = vector[0]
    shift1 = vector[1]
    bias_q = vector[2]
    bias_v = vector[3]
    bias_out = vector[4]
    gain2 = vector[5]
    shift2 = vector[6]
    bias_down = vector[7]
    bias_up = vector[8:].reshape(-1)
    images, length, width = values.shape
    hidden = rounded(layer_norm(values, gain1, shift1))
    bias_all = jnp.concatenate([bias_q, jnp.zeros((width,), jnp.float32), bias_v])
    qkv = matmul(hidden, w_qkv) + bias_all
    query = rounded(qkv[..., :width]).reshape(images, length, HEADS, HEAD)
    key_part = rounded(qkv[..., width:2 * width]).reshape(images, length, HEADS, HEAD)
    value = rounded(qkv[..., 2 * width:]).reshape(images, length, HEADS, HEAD)
    mixed = jax.checkpoint(attend)(query, key_part, value).reshape(images, length, width)
    mixed = rounded(mixed)
    first = values + low_back(matmul(mixed, w_out) + bias_out)
    hidden2 = rounded(layer_norm(first, gain2, shift2))
    inner = low_back(matmul(hidden2, w_up) + bias_up)
    active = rounded(0.5 * inner * (1.0 + jax.scipy.special.erf(inner / math.sqrt(2.0))))
    down = jnp.einsum('bsf,df->bsd', active, w_down_t, precision=lax.Precision.HIGHEST)
    return first + low_back(down + bias_down)

def adamw(grad, first, second, old):
    first_new = 0.9 * first + 0.1 * grad
    second_new = 0.999 * second + 0.001 * grad * grad
    first_hat = first_new / (1.0 - 0.9 ** STEP)
    second_hat = second_new / (1.0 - 0.999 ** STEP)
    change = -0.01 * (first_hat / (jnp.sqrt(second_hat) + 1e-08) + 0.05 * old)
    return (first_new, second_new, change)

def reference(tokens, weights, vectors, moment_one, moment_two, vector_one, vector_two, images, cotangent):
    slots = jnp.arange(IMGS_DEV, dtype=jnp.int32)
    live = (slots[None, :] < images[:, None]).astype(jnp.float32).reshape(-1)
    start_values = tokens.astype(jnp.float32)

    def forward(values, matrices, vector_all):
        for index in range(LAYERS):
            values = layer(values, matrices[index], vector_all[index])
        return values
    output, pullback = jax.vjp(forward, start_values, weights, vectors)
    start_grad = cotangent.astype(jnp.float32) * live[:, None, None]
    input_grad, weight_grad, vector_grad = pullback(start_grad)
    moment_one_new, moment_two_new, update = adamw(weight_grad, moment_one, moment_two, weights)
    vector_one_new, vector_two_new, vector_update = adamw(vector_grad, vector_one, vector_two, vectors)
    return (output, input_grad, weight_grad, vector_grad, moment_one_new, moment_two_new, vector_one_new, vector_two_new, update, vector_update)
```

```python
import functools
import math

import jax
import jax.numpy as jnp
from jax import lax
from jax.experimental import pallas as pl
from jax.experimental.pallas import tpu as pltpu
from jax.sharding import PartitionSpec as P

HEAD = 64
FF = 1536
STEP = 10
PAIR = 2
TILE = 128
NEG = -1e30
F32 = jnp.float32
BF16 = jnp.bfloat16
VMEM_LIMIT = 60 * 1024 * 1024


def dot(left, right):
    return jnp.dot(left, right, preferred_element_type=F32)


def dot_nt(left, right):
    return lax.dot_general(left, right, (((1,), (1,)), ((), ())), preferred_element_type=F32)


def dot_tn(left, right):
    return lax.dot_general(left, right, (((0,), (0,)), ((), ())), preferred_element_type=F32)


def norm(values):
    center = values - jnp.mean(values, -1, keepdims=True)
    scale = lax.rsqrt(jnp.mean(center * center, -1, keepdims=True) + 1e-06)
    return center * scale, scale


def norm_back(grad, normed, scale, gain):
    inner = grad * gain
    return scale * (
        inner
        - jnp.mean(inner, -1, keepdims=True)
        - normed * jnp.mean(inner * normed, -1, keepdims=True)
    )


def gelu_parts(u):
    size = jnp.abs(u)
    t = 1.0 / (1.0 + (0.3275911 / math.sqrt(2.0)) * size)
    e = jnp.exp(-0.5 * (u * u))
    poly = t * (
        0.5 * 0.254829592
        + t
        * (
            0.5 * -0.284496736
            + t * (0.5 * 1.421413741 + t * (0.5 * -1.453152027 + t * (0.5 * 1.061405429)))
        )
    )
    tail = poly * e
    phi = jnp.where(u < 0.0, tail, 1.0 - tail)
    slope = phi + u * (e * (1.0 / math.sqrt(2.0 * math.pi)))
    return u * phi, slope


def join_halves(core, mine_ref, other_ref, whole_ref):
    half = mine_ref.shape[1]

    @pl.when(core == 0)
    def _():
        whole_ref[:, :half] = mine_ref[...]
        whole_ref[:, half:] = other_ref[...]

    @pl.when(core != 0)
    def _():
        whole_ref[:, :half] = other_ref[...]
        whole_ref[:, half:] = mine_ref[...]


def attn_forward(first, seq, rows, *refs):
    if first:
        core_ref, x_ref, mine_ref, other_ref, qkv_ref, o_ref, lse_ref, vec_ref, xp_ref, w_ref = refs
    else:
        core_ref, x_ref, mine_ref, other_ref, qkv_ref, o_ref, lse_ref, vec_ref, w_ref = refs
        xp_ref = x_ref
    width = o_ref.shape[1]
    heads = width // HEAD

    @pl.when(pl.program_id(0) == 0)
    def _():
        join_halves(core_ref[0], mine_ref, other_ref, w_ref)
        turned = w_ref[:, 3 * width : 3 * width + TILE].astype(F32).T
        vec_ref[...] = turned[: vec_ref.shape[0]]

    if first:
        for i in range(PAIR):
            xp_ref[i * rows : i * rows + seq, :] = x_ref[i].astype(F32)
            xp_ref[i * rows + seq : (i + 1) * rows, :] = jnp.zeros((rows - seq, width), F32)

    normed, _ = norm(xp_ref[...])
    hidden = (normed * vec_ref[0:1, :] + vec_ref[1:2, :]).astype(BF16)
    q = dot(hidden, w_ref[:, :width]) + vec_ref[2:3, :]
    qkv_ref[:, :width] = (q.astype(BF16).astype(F32) * 0.125).astype(BF16)
    qkv_ref[:, width : 2 * width] = dot(hidden, w_ref[:, width : 2 * width]).astype(BF16)
    v = dot(hidden, w_ref[:, 2 * width : 3 * width]) + vec_ref[3:4, :]
    qkv_ref[:, 2 * width :] = v.astype(BF16)

    edge = seq // 16 * 16
    alive = lax.broadcasted_iota(jnp.int32, (rows - edge, rows), 0) < seq - edge
    lane = lax.broadcasted_iota(jnp.int32, (rows, TILE), 1)
    for i in range(PAIR):
        span = slice(i * rows, (i + 1) * rows)
        turned_v = qkv_ref[span, 2 * width :].T
        outs = []
        for h in range(heads):
            tile = (h * HEAD) // TILE * TILE
            mine = (lane < HEAD) if h * HEAD % TILE == 0 else (lane >= HEAD)
            query = jnp.where(mine, qkv_ref[span, tile : tile + TILE], jnp.zeros((), BF16))
            scores = dot_nt(qkv_ref[span, width + tile : width + tile + TILE], query)
            low = scores[:edge]
            high = jnp.where(alive, scores[edge:], NEG)
            top = jnp.maximum(jnp.max(low, 0, keepdims=True), jnp.max(high, 0, keepdims=True))
            low = jnp.exp(low - top)
            high = jnp.exp(high - top)
            total = jnp.sum(low, 0, keepdims=True) + jnp.sum(high, 0, keepdims=True)
            lse_ref[i, h : h + 1, :rows] = top + jnp.log(total)
            share = 1.0 / total
            probs = jnp.concatenate([(low * share).astype(BF16), (high * share).astype(BF16)], 0)
            outs.append(dot(turned_v[h * HEAD : (h + 1) * HEAD], probs).astype(BF16))
        o_ref[span, :] = jnp.concatenate(outs, 0).T


def mlp_forward(last, seq, rows, *refs):
    core_ref, x_ref, o_ref, mine_ref, other_ref, vec_ref, x1_ref, act_ref, slope_ref, out_ref, w_ref = refs
    width = x_ref.shape[1]

    @pl.when(pl.program_id(0) == 0)
    def _():
        join_halves(core_ref[0], mine_ref, other_ref, w_ref)

    x1 = x_ref[...] + dot(o_ref[...], w_ref[:, :width]) + vec_ref[4:5, :]
    x1_ref[...] = x1
    normed, _ = norm(x1)
    hidden = (normed * vec_ref[5:6, :] + vec_ref[6:7, :]).astype(BF16)
    total = x1 + vec_ref[7:8, :]
    for j in range(FF // width):
        cols = slice(j * width, (j + 1) * width)
        u = dot(hidden, w_ref[:, (1 + j) * width : (2 + j) * width]) + vec_ref[8 + j : 9 + j, :]
        act, slope = gelu_parts(u)
        act = act.astype(BF16)
        act_ref[:, cols] = act
        slope_ref[:, cols] = slope
        start = width + FF + j * width
        total = total + dot_nt(act, w_ref[:, start : start + width])
    if last:
        for i in range(PAIR):
            out_ref[i] = total[i * rows : i * rows + seq]
    else:
        out_ref[...] = total


def put_grads(core, first_of, second_of, keep_ref, send_ref):
    @pl.when(core == 0)
    def _():
        first_of(keep_ref)
        second_of(send_ref)

    @pl.when(core != 0)
    def _():
        first_of(send_ref)
        second_of(keep_ref)


def put_vectors(acc_ref, ref):
    size = acc_ref.shape[0]
    padded = jnp.concatenate(
        [acc_ref[...], jnp.zeros((TILE - size, acc_ref.shape[1]), F32)], 0
    )
    ref[:, ref.shape[1] - TILE :] = padded.T.astype(BF16)


def column_sum(values):
    return jnp.sum(values, 0, keepdims=True)


def mlp_backward(last, seq, rows, *refs):
    (core_ref, live_ref, g_ref, x1_ref, act_ref, slope_ref, mine_ref, other_ref, vec_ref,
     gx1_ref, keep_ref, send_ref, w_ref, up_ref, down_ref, acc_ref, gp_ref) = refs
    width = x1_ref.shape[1]
    step = pl.program_id(0)

    @pl.when(step == 0)
    def _():
        join_halves(core_ref[0], mine_ref, other_ref, w_ref)
        up_ref[...] = jnp.zeros_like(up_ref)
        down_ref[...] = jnp.zeros_like(down_ref)
        acc_ref[...] = jnp.zeros_like(acc_ref)

    if last:
        for i in range(PAIR):
            keep = (step * PAIR + i < live_ref[0]).astype(F32)
            gp_ref[i * rows : i * rows + seq, :] = g_ref[i].astype(F32) * keep
            gp_ref[i * rows + seq : (i + 1) * rows, :] = jnp.zeros((rows - seq, width), F32)
        g = gp_ref[...]
    else:
        g = g_ref[...]
    low = g.astype(BF16)
    turned = low.T
    normed, scale = norm(x1_ref[...])
    hidden = (normed * vec_ref[5:6, :] + vec_ref[6:7, :]).astype(BF16)
    turned_h = hidden.T
    acc_ref[2:3, :] += column_sum(low.astype(F32))
    total = jnp.zeros_like(g)
    for j in range(FF // width):
        cols = slice(j * width, (j + 1) * width)
        down_ref[:, cols] += dot(turned, act_ref[:, cols])
        start = width + FF + j * width
        ga = dot(low, w_ref[:, start : start + width]).astype(BF16).astype(F32)
        gu = (ga * slope_ref[:, cols]).astype(BF16)
        up_ref[:, cols] += dot(turned_h, gu)
        acc_ref[3 + j : 4 + j, :] += column_sum(gu.astype(F32))
        total = total + dot_nt(gu, w_ref[:, (1 + j) * width : (2 + j) * width])
    gh2 = total.astype(BF16).astype(F32)
    acc_ref[0:1, :] += column_sum(gh2 * normed)
    acc_ref[1:2, :] += column_sum(gh2)
    gx1_ref[...] = g + norm_back(gh2, normed, scale, vec_ref[5:6, :])

    @pl.when(step == pl.num_programs(0) - 1)
    def _():
        def up(ref):
            ref[:, :FF] = up_ref[...].astype(BF16)
            put_vectors(acc_ref, ref)

        def down(ref):
            ref[:, :FF] = down_ref[...].astype(BF16)
            ref[:, FF:] = jnp.zeros((width, TILE), BF16)

        put_grads(core_ref[0], up, down, keep_ref, send_ref)


def attn_backward(first, seq, rows, *refs):
    (core_ref, g_ref, x_ref, qkv_ref, lse_ref, o_ref, qmine_ref, qother_ref, wout_ref, vec_ref,
     gx_ref, keep_ref, send_ref, w_ref, gw_ref, gout_ref, acc_ref, gqkv_ref, go_ref) = refs
    width = x_ref.shape[1]
    heads = width // HEAD
    step = pl.program_id(0)

    @pl.when(step == 0)
    def _():
        join_halves(core_ref[0], qmine_ref, qother_ref, w_ref)
        gw_ref[...] = jnp.zeros_like(gw_ref)
        gout_ref[...] = jnp.zeros_like(gout_ref)
        acc_ref[...] = jnp.zeros_like(acc_ref)

    low = g_ref[...].astype(BF16)
    gout_ref[...] += dot(o_ref[...].T, low)
    acc_ref[4:5, :] += column_sum(low.astype(F32))
    go_ref[...] = dot_nt(low, wout_ref[...]).astype(BF16)

    edge = seq // 16 * 16
    alive = lax.broadcasted_iota(jnp.int32, (rows - edge, rows), 0) < seq - edge
    lane = lax.broadcasted_iota(jnp.int32, (rows, TILE), 1)
    zero = jnp.zeros((), BF16)
    for i in range(PAIR):
        span = slice(i * rows, (i + 1) * rows)
        turned_k = qkv_ref[span, width : 2 * width].T
        turned_gq = []
        for pair in range(heads // 2):
            tile = pair * TILE
            query = qkv_ref[span, tile : tile + TILE]
            key_part = qkv_ref[span, width + tile : width + tile + TILE]
            value = qkv_ref[span, 2 * width + tile : 2 * width + tile + TILE]
            go = go_ref[span, tile : tile + TILE]
            gks, gvs = [], []
            for e in range(2):
                h = 2 * pair + e
                mine = (lane < HEAD) if e == 0 else (lane >= HEAD)
                scores = dot_nt(key_part, jnp.where(mine, query, zero)) - lse_ref[i, h : h + 1, :rows]
                gp = dot_nt(value, jnp.where(mine, go, zero))
                p_low = jnp.exp(scores[:edge])
                p_high = jnp.where(alive, jnp.exp(scores[edge:]), 0.0)
                probs = jnp.concatenate([p_low.astype(BF16), p_high.astype(BF16)], 0)
                gp_low, gp_high = gp[:edge], gp[edge:]
                mean = column_sum(gp_low * p_low) + column_sum(gp_high * p_high)
                gs = jnp.concatenate(
                    [
                        (p_low * (gp_low - mean)).astype(BF16),
                        (p_high * (gp_high - mean)).astype(BF16),
                    ],
                    0,
                )
                gvs.append(dot(probs, go))
                gks.append(dot(gs, query))
                turned_gq.append((dot(turned_k[h * HEAD : (h + 1) * HEAD], gs) * 0.125).astype(BF16))
            gqkv_ref[span, width + tile : width + tile + TILE] = jnp.where(
                lane < HEAD, gks[0], gks[1]
            ).astype(BF16)
            gqkv_ref[span, 2 * width + tile : 2 * width + tile + TILE] = jnp.where(
                lane < HEAD, gvs[0], gvs[1]
            ).astype(BF16)
        gqkv_ref[span, :width] = jnp.concatenate(turned_gq, 0).T

    normed, scale = norm(x_ref[...])
    hidden = (normed * vec_ref[0:1, :] + vec_ref[1:2, :]).astype(BF16)
    turned_h = hidden.T
    total = jnp.zeros((PAIR * rows, width), F32)
    for j in range(3):
        cols = slice(j * width, (j + 1) * width)
        part = gqkv_ref[:, cols]
        gw_ref[:, cols] += dot(turned_h, part)
        total = total + dot_nt(part, w_ref[:, cols])
        if j != 1:
            at = 2 if j == 0 else 3
            acc_ref[at : at + 1, :] += column_sum(part.astype(F32))
    gh = total.astype(BF16).astype(F32)
    acc_ref[0:1, :] += column_sum(gh * normed)
    acc_ref[1:2, :] += column_sum(gh)
    gx = g_ref[...] + norm_back(gh, normed, scale, vec_ref[0:1, :])
    if first:
        for i in range(PAIR):
            gx_ref[i] = gx[i * rows : i * rows + seq]
    else:
        gx_ref[...] = gx

    @pl.when(step == pl.num_programs(0) - 1)
    def _():
        def one(ref):
            ref[:, : 2 * width] = gw_ref[:, : 2 * width].astype(BF16)
            put_vectors(acc_ref, ref)

        def two(ref):
            ref[:, :width] = gw_ref[:, 2 * width :].astype(BF16)
            ref[:, width : 2 * width] = gout_ref[...].astype(BF16)
            ref[:, 2 * width :] = jnp.zeros((width, TILE), BF16)

        put_grads(core_ref[0], one, two, keep_ref, send_ref)


def adamw(grad, first, second, old):
    first_new = 0.9 * first + 0.1 * grad
    second_new = 0.999 * second + 0.001 * grad * grad
    first_hat = first_new / (1.0 - 0.9**STEP)
    second_hat = second_new / (1.0 - 0.999**STEP)
    change = -0.01 * (first_hat / (jnp.sqrt(second_hat) + 1e-08) + 0.05 * old)
    return (first_new, second_new, change)


def step_kernel(aliased, core_ref, mine_ref, other_ref, one_ref, two_ref, old_ref, *refs):
    grad_ref, one_new_ref, two_new_ref, change_ref = refs[-4:]
    cols = grad_ref.shape[2]

    def put(from_ref):
        grad = from_ref[:, :cols].astype(F32)
        grad_ref[0] = grad
        one_new_ref[0], two_new_ref[0], change_ref[0] = adamw(grad, one_ref[0], two_ref[0], old_ref[0])

    @pl.when(core_ref[0] == pl.program_id(0))
    def _():
        put(mine_ref)

    @pl.when(core_ref[0] != pl.program_id(0))
    def _():
        put(other_ref)


def smem():
    return pl.BlockSpec(memory_space=pltpu.SMEM)


def whole(shape):
    zeros = (0,) * len(shape)
    return pl.BlockSpec(shape, lambda i: zeros)


def cost(flops, moved, exps):
    return pl.CostEstimate(flops=int(flops), bytes_accessed=int(moved), transcendentals=int(exps))


def params():
    return pltpu.CompilerParams(
        dimension_semantics=("arbitrary",), vmem_limit_bytes=VMEM_LIMIT
    )


def struct(shape, kind):
    return jax.ShapeDtypeStruct(shape, kind)


class Layers:
    def __init__(self, images, seq, width):
        self.images, self.seq, self.width = images, seq, width
        self.rows = -(-seq // 16) * 16
        self.grid = (images // PAIR,)
        self.total = images * self.rows
        self.block = PAIR * self.rows

    def tall(self, cols):
        return pl.BlockSpec((self.block, cols), lambda i: (i, 0))

    def images_spec(self):
        return pl.BlockSpec((PAIR, self.seq, self.width), lambda i: (i, 0, 0))

    def attn_forward(self, core, x, mine, other, first):
        w, t = self.width, self.total
        outs = [
            (self.tall(3 * w), struct((t, 3 * w), BF16)),
            (self.tall(w), struct((t, w), BF16)),
            (pl.BlockSpec((PAIR, 8, 256), lambda i: (i, 0, 0)), struct((self.images, 8, 256), F32)),
            (whole((16, w)), struct((16, w), F32)),
        ]
        if first:
            outs.append((self.tall(w), struct((t, w), F32)))
        return pl.pallas_call(
            functools.partial(attn_forward, first, self.seq, self.rows),
            grid=self.grid,
            in_specs=[
                smem(),
                self.images_spec() if first else self.tall(w),
                whole(mine.shape),
                whole(other.shape),
            ],
            out_specs=[o[0] for o in outs],
            out_shape=[o[1] for o in outs],
            scratch_shapes=[pltpu.VMEM((w, 2 * mine.shape[1]), BF16)],
            compiler_params=params(),
            cost_estimate=cost(8e9, 2e7, 3e6),
        )(core, x, mine, other)

    def mlp_forward(self, core, x, o, mine, other, vec, last):
        w, t = self.width, self.total
        outs = [
            (self.tall(w), struct((t, w), F32)),
            (self.tall(FF), struct((t, FF), BF16)),
            (self.tall(FF), struct((t, FF), F32)),
            (self.images_spec(), struct((self.images, self.seq, w), F32))
            if last
            else (self.tall(w), struct((t, w), F32)),
        ]
        return pl.pallas_call(
            functools.partial(mlp_forward, last, self.seq, self.rows),
            grid=self.grid,
            in_specs=[
                smem(), self.tall(w), self.tall(w), whole(mine.shape), whole(other.shape), whole(vec.shape),
            ],
            out_specs=[o[0] for o in outs],
            out_shape=[o[1] for o in outs],
            scratch_shapes=[pltpu.VMEM((w, 2 * mine.shape[1]), BF16)],
            compiler_params=params(),
            cost_estimate=cost(1.5e10, 3e7, 3e6),
        )(core, x, o, mine, other, vec)

    def mlp_backward(self, core, live, g, x1, act, slope, mine, other, vec, last):
        w, t = self.width, self.total
        return pl.pallas_call(
            functools.partial(mlp_backward, last, self.seq, self.rows),
            grid=self.grid,
            in_specs=[
                smem(), smem(),
                self.images_spec() if last else self.tall(w),
                self.tall(w), self.tall(FF), self.tall(FF),
                whole(mine.shape), whole(other.shape), whole(vec.shape),
            ],
            out_specs=[self.tall(w), whole((w, FF + TILE)), whole((w, FF + TILE))],
            out_shape=[
                struct((t, w), F32), struct((w, FF + TILE), BF16), struct((w, FF + TILE), BF16),
            ],
            scratch_shapes=[
                pltpu.VMEM((w, 2 * mine.shape[1]), BF16),
                pltpu.VMEM((w, FF), F32),
                pltpu.VMEM((w, FF), F32),
                pltpu.VMEM((8, w), F32),
                pltpu.VMEM((self.block, w), F32),
            ],
            compiler_params=params(),
            cost_estimate=cost(2e10, 3e7, 3e6),
        )(core, live, g, x1, act, slope, mine, other, vec)

    def attn_backward(self, core, g, x, qkv, lse, o, qmine, qother, wout, vec, first):
        w, t = self.width, self.total
        return pl.pallas_call(
            functools.partial(attn_backward, first, self.seq, self.rows),
            grid=self.grid,
            in_specs=[
                smem(), self.tall(w), self.tall(w), self.tall(3 * w),
                pl.BlockSpec((PAIR, 8, 256), lambda i: (i, 0, 0)),
                self.tall(w), whole(qmine.shape), whole(qother.shape), whole(wout.shape), whole(vec.shape),
            ],
            out_specs=[
                self.images_spec() if first else self.tall(w),
                whole((w, 2 * w + TILE)), whole((w, 2 * w + TILE)),
            ],
            out_shape=[
                struct((self.images, self.seq, w), F32) if first else struct((t, w), F32),
                struct((w, 2 * w + TILE), BF16), struct((w, 2 * w + TILE), BF16),
            ],
            scratch_shapes=[
                pltpu.VMEM((w, 2 * qmine.shape[1]), BF16),
                pltpu.VMEM((w, 3 * w), F32),
                pltpu.VMEM((w, w), F32),
                pltpu.VMEM((8, w), F32),
                pltpu.VMEM((self.block, 3 * w), BF16),
                pltpu.VMEM((self.block, w), BF16),
            ],
            compiler_params=params(),
            cost_estimate=cost(2e10, 2e7, 3e6),
        )(core, g, x, qkv, lse, o, qmine, qother, wout, vec)


def flip(axis, bit):
    return [(i, i ^ bit) for i in range(lax.axis_size(axis))]


def broadcast_shards(piece):
    count = lax.axis_size("shard")
    out = lax.all_to_all(
        jnp.broadcast_to(piece[None], (count,) + piece.shape), "shard", 0, 0, tiled=True
    )
    return out.reshape((-1, piece.shape[1]))


def gather(packed, core):
    half = packed.shape[1] // 2
    own = lax.dynamic_slice_in_dim(packed, core * half, half, 1)
    mine = broadcast_shards(own)
    return mine, lax.ppermute(mine, "rep", flip("rep", 1))


def reduce_group(keep, send):
    count = lax.axis_size("shard")
    rows, cols = keep.shape
    other = lax.ppermute(send, "rep", flip("rep", 1))
    joined = (keep.astype(F32) + other.astype(F32)).astype(BF16)
    parts = lax.all_to_all(joined.reshape(count, rows // count, cols), "shard", 0, 0, tiled=True)
    mine = jnp.sum(parts.astype(F32), 0).astype(BF16)
    bit = 2
    while bit < lax.axis_size("rep"):
        other = lax.ppermute(mine, "rep", flip("rep", bit))
        mine = (mine.astype(F32) + other.astype(F32)).astype(BF16)
        bit *= 2
    return mine, lax.ppermute(mine, "rep", flip("rep", 1))


def update_group(core, pair, state, outs, layer, at, cols):
    mine, other = pair
    spec = pl.BlockSpec((1, mine.shape[0], cols), lambda j: (layer, 0, at + j))
    shape = struct(state[0].shape, F32)
    given = list(outs) if outs is not None else []
    return pl.pallas_call(
        functools.partial(step_kernel, len(given)),
        grid=(2,),
        in_specs=[smem(), whole(mine.shape), whole(other.shape), spec, spec, spec]
        + [pl.BlockSpec(memory_space=pl.ANY)] * len(given),
        out_specs=[spec] * 4,
        out_shape=[shape] * 4,
        input_output_aliases={6 + i: i for i in range(len(given))},
        compiler_params=params(),
        cost_estimate=cost(1e6, 4e6, 0),
    )(core, mine, other, *state, *given)


def local(
    tokens, weights, vectors, moment_one, moment_two, vector_one, vector_two, images, cotangent
):
    count, seq, width = tokens.shape
    layers = weights.shape[0]
    plan = Layers(count, seq, width)
    core = lax.axis_index("rep") % 2
    core_arr = core.reshape(1).astype(jnp.int32)
    gathered = []
    for index in range(layers):
        low = weights[index].astype(BF16)
        turned = jnp.pad(vectors[index].T.astype(BF16), ((0, 0), (0, TILE - vectors.shape[1])))
        attn_pack = jnp.concatenate([low[:, : 3 * width], turned], 1)
        rest = low[:, 3 * width :]
        rest_pack = jnp.pad(rest, ((0, 0), (0, -rest.shape[1] % (2 * TILE))))
        gathered.append((gather(attn_pack, core), gather(rest_pack, core)))
    stored = []
    x = tokens
    for index in range(layers):
        first, last = index == 0, index == layers - 1
        (qmine, qother), (mine, other) = gathered[index]
        out = plan.attn_forward(core_arr, x, qmine, qother, first)
        qkv, o, lse, vec = out[:4]
        xp = out[4] if first else x
        x1, act, slope, x = plan.mlp_forward(core_arr, xp, o, mine, other, vec, last)
        stored.append((xp, qkv, o, lse, vec, x1, act, slope))
    output = x
    g = cotangent
    state = (moment_one, moment_two, weights)
    outs = None
    vec_grads = [None] * layers
    for index in reversed(range(layers)):
        first, last = index == 0, index == layers - 1
        (qmine, qother), (mine, other) = gathered[index]
        xp, qkv, o, lse, vec, x1, act, slope = stored[index]
        gx1, keep, send = plan.mlp_backward(
            core_arr, images, g, x1, act, slope, mine, other, vec, last
        )
        pair_m = reduce_group(keep, send)
        wout = jnp.where(core == 0, mine[:, :width], other[:, :width])
        g, keep, send = plan.attn_backward(
            core_arr, gx1, xp, qkv, lse, o, qmine, qother, wout, vec, first
        )
        pair_a = reduce_group(keep, send)
        outs = update_group(core_arr, pair_m, state, outs, index, 1, FF)
        outs = update_group(core_arr, pair_a, state, outs, index, 0, 2 * width)
        tails = [
            jnp.where(core == 0, p[0][:, -TILE:], p[1][:, -TILE:]).astype(F32).T
            for p in (pair_a, pair_m)
        ]
        vec_grads[index] = jnp.concatenate([tails[0][:5], tails[1][:7]], 0)
    vector_grad = jnp.stack(vec_grads)
    weight_grad, moment_one_new, moment_two_new, update = outs
    vector_one_new, vector_two_new, vector_update = adamw(
        vector_grad, vector_one, vector_two, vectors
    )
    return (
        output,
        g,
        weight_grad,
        vector_grad,
        moment_one_new,
        moment_two_new,
        vector_one_new,
        vector_two_new,
        update,
        vector_update,
    )


def solution(mesh):
    in_specs = (
        P(("rep", "shard"), None, None),
        P(None, "shard", None),
        P(None, None, "shard"),
        P(None, "shard", None),
        P(None, "shard", None),
        P(None, None, "shard"),
        P(None, None, "shard"),
        P(("rep", "shard")),
        P(("rep", "shard"), None, None),
    )
    out_specs = (
        P(("rep", "shard"), None, None),
        P(("rep", "shard"), None, None),
        P(None, "shard", None),
        P(None, None, "shard"),
        P(None, "shard", None),
        P(None, "shard", None),
        P(None, None, "shard"),
        P(None, None, "shard"),
        P(None, "shard", None),
        P(None, None, "shard"),
    )
    return jax.shard_map(local, mesh=mesh, in_specs=in_specs, out_specs=out_specs, check_vma=False)
```

```python
import functools
import math

import jax
import jax.numpy as jnp
from jax import lax
from jax.experimental import pallas as pl
from jax.experimental.pallas import tpu as pltpu
from jax.sharding import PartitionSpec as P

HEAD = 64
FF = 1536
STEP = 10
PAIR = 2
TILE = 128
NEG = -1e30
F32 = jnp.float32
BF16 = jnp.bfloat16
VMEM_LIMIT = 60 * 1024 * 1024


def dot(left, right):
    return jnp.dot(left, right, preferred_element_type=F32)


def dot_nt(left, right):
    return lax.dot_general(left, right, (((1,), (1,)), ((), ())), preferred_element_type=F32)


def dot_tn(left, right):
    return lax.dot_general(left, right, (((0,), (0,)), ((), ())), preferred_element_type=F32)


def norm(values):
    center = values - jnp.mean(values, -1, keepdims=True)
    scale = lax.rsqrt(jnp.mean(center * center, -1, keepdims=True) + 1e-06)
    return center * scale, scale


def norm_back(grad, normed, scale, gain):
    inner = grad * gain
    return scale * (
        inner
        - jnp.mean(inner, -1, keepdims=True)
        - normed * jnp.mean(inner * normed, -1, keepdims=True)
    )


def gelu_parts(u):
    size = jnp.abs(u)
    t = 1.0 / (1.0 + (0.3275911 / math.sqrt(2.0)) * size)
    e = jnp.exp(-0.5 * (u * u))
    poly = t * (
        0.5 * 0.254829592
        + t
        * (
            0.5 * -0.284496736
            + t * (0.5 * 1.421413741 + t * (0.5 * -1.453152027 + t * (0.5 * 1.061405429)))
        )
    )
    tail = poly * e
    phi = jnp.where(u < 0.0, tail, 1.0 - tail)
    slope = phi + u * (e * (1.0 / math.sqrt(2.0 * math.pi)))
    return u * phi, slope


def load_weights(core_ref, place_ref, sources, start, whole_ref, sems):
    half = whole_ref.shape[1] // 2
    per_core = len(sources) // 2
    copies = []
    for n, source in enumerate(sources):
        at = core_ref[0] if n < per_core else 1 - core_ref[0]
        cols = pl.ds(pl.multiple_of(at * half, TILE), half)
        copies += row_copies(
            place_ref, source, n % per_core, slice(start, start + half), whole_ref, cols, sems, len(copies)
        )
    for copy in copies:
        copy.start()
    for copy in copies:
        copy.wait()


def load_first(core_ref, place_ref, sources, start, whole_ref, sems):
    per_core = len(sources) // 2
    size = whole_ref.shape[1]

    def load(chosen):
        copies = []
        for n, source in enumerate(chosen):
            copies += row_copies(
                place_ref, source, n, slice(start, start + size), whole_ref, slice(0, size), sems, len(copies)
            )
        for copy in copies:
            copy.start()
        for copy in copies:
            copy.wait()

    @pl.when(core_ref[0] == 0)
    def _():
        load(sources[:per_core])

    @pl.when(core_ref[0] != 0)
    def _():
        load(sources[per_core:])


def row_copies(place_ref, source, nth, taken, whole_ref, cols, sems, at):
    count, rows = source.shape[:2]
    copies = []
    for k in range(count):
        row = pl.multiple_of(place_ref[nth * count + k] * rows, rows)
        copies.append(
            pltpu.make_async_copy(
                source.at[k, :, taken], whole_ref.at[pl.ds(row, rows), cols], sems.at[at + k]
            )
        )
    return copies


def attn_forward(first, seq, rows, at, start, core_ref, place_ref, x_ref, *refs):
    sources, refs = refs[:at], refs[at:]
    if first:
        qkv_ref, o_ref, lse_ref, vec_ref, xp_ref, w_ref, sems = refs
    else:
        qkv_ref, o_ref, lse_ref, vec_ref, w_ref, sems = refs
        xp_ref = x_ref
    width = o_ref.shape[1]
    heads = width // HEAD

    @pl.when(pl.program_id(0) == 0)
    def _():
        load_weights(core_ref, place_ref, sources, start, w_ref, sems)
        turned = w_ref[:, 3 * width : 3 * width + TILE].astype(F32).T
        vec_ref[...] = turned[: vec_ref.shape[0]]

    if first:
        for i in range(PAIR):
            xp_ref[i * rows : i * rows + seq, :] = x_ref[i].astype(F32)
            xp_ref[i * rows + seq : (i + 1) * rows, :] = jnp.zeros((rows - seq, width), F32)

    normed, _ = norm(xp_ref[...])
    hidden = (normed * vec_ref[0:1, :] + vec_ref[1:2, :]).astype(BF16)
    q = dot(hidden, w_ref[:, :width]) + vec_ref[2:3, :]
    qkv_ref[:, :width] = (q.astype(BF16).astype(F32) * 0.125).astype(BF16)
    qkv_ref[:, width : 2 * width] = dot(hidden, w_ref[:, width : 2 * width]).astype(BF16)
    v = dot(hidden, w_ref[:, 2 * width : 3 * width]) + vec_ref[3:4, :]
    qkv_ref[:, 2 * width :] = v.astype(BF16)

    edge = seq // 16 * 16
    alive = lax.broadcasted_iota(jnp.int32, (rows - edge, rows), 0) < seq - edge
    lane = lax.broadcasted_iota(jnp.int32, (rows, TILE), 1)
    for i in range(PAIR):
        span = slice(i * rows, (i + 1) * rows)
        turned_v = qkv_ref[span, 2 * width :].T
        outs = []
        for h in range(heads):
            tile = (h * HEAD) // TILE * TILE
            mine = (lane < HEAD) if h * HEAD % TILE == 0 else (lane >= HEAD)
            query = jnp.where(mine, qkv_ref[span, tile : tile + TILE], jnp.zeros((), BF16))
            scores = dot_nt(qkv_ref[span, width + tile : width + tile + TILE], query)
            low = scores[:edge]
            high = jnp.where(alive, scores[edge:], NEG)
            top = jnp.maximum(jnp.max(low, 0, keepdims=True), jnp.max(high, 0, keepdims=True))
            low = jnp.exp(low - top)
            high = jnp.exp(high - top)
            total = jnp.sum(low, 0, keepdims=True) + jnp.sum(high, 0, keepdims=True)
            lse_ref[i, h : h + 1, :rows] = top + jnp.log(total)
            share = 1.0 / total
            probs = jnp.concatenate([(low * share).astype(BF16), (high * share).astype(BF16)], 0)
            outs.append(dot(turned_v[h * HEAD : (h + 1) * HEAD], probs).astype(BF16))
        o_ref[span, :] = jnp.concatenate(outs, 0).T


def mlp_forward(last, seq, rows, at, start, core_ref, place_ref, x_ref, o_ref, vec_ref, *refs):
    sources, refs = refs[:at], refs[at:]
    x1_ref, act_ref, slope_ref, out_ref, w_ref, sems = refs
    width = x_ref.shape[1]

    @pl.when(pl.program_id(0) == 0)
    def _():
        load_weights(core_ref, place_ref, sources, start, w_ref, sems)

    x1 = x_ref[...] + dot(o_ref[...], w_ref[:, :width]) + vec_ref[4:5, :]
    x1_ref[...] = x1
    normed, _ = norm(x1)
    hidden = (normed * vec_ref[5:6, :] + vec_ref[6:7, :]).astype(BF16)
    total = x1 + vec_ref[7:8, :]
    for j in range(FF // width):
        cols = slice(j * width, (j + 1) * width)
        u = dot(hidden, w_ref[:, (1 + j) * width : (2 + j) * width]) + vec_ref[8 + j : 9 + j, :]
        act, slope = gelu_parts(u)
        act = act.astype(BF16)
        act_ref[:, cols] = act
        slope_ref[:, cols] = slope
        start = width + FF + j * width
        total = total + dot_nt(act, w_ref[:, start : start + width])
    if last:
        for i in range(PAIR):
            out_ref[i] = total[i * rows : i * rows + seq]
    else:
        out_ref[...] = total


def put_grads(core, first_of, second_of, keep_ref, send_ref):
    @pl.when(core == 0)
    def _():
        first_of(keep_ref)
        second_of(send_ref)

    @pl.when(core != 0)
    def _():
        first_of(send_ref)
        second_of(keep_ref)


def put_vectors(acc_ref, ref):
    size = acc_ref.shape[0]
    padded = jnp.concatenate(
        [acc_ref[...], jnp.zeros((TILE - size, acc_ref.shape[1]), F32)], 0
    )
    ref[:, ref.shape[1] - TILE :] = padded.T.astype(BF16)


def column_sum(values):
    return jnp.sum(values, 0, keepdims=True)


def mlp_backward(
    last, seq, rows, at, start, core_ref, place_ref, live_ref, g_ref, x1_ref, act_ref, slope_ref, vec_ref, *refs
):
    sources, refs = refs[:at], refs[at:]
    gx1_ref, keep_ref, send_ref, w_ref, up_ref, down_ref, acc_ref, gp_ref, sems = refs
    width = x1_ref.shape[1]
    step = pl.program_id(0)

    @pl.when(step == 0)
    def _():
        load_weights(core_ref, place_ref, sources, start, w_ref, sems)
        up_ref[...] = jnp.zeros_like(up_ref)
        down_ref[...] = jnp.zeros_like(down_ref)
        acc_ref[...] = jnp.zeros_like(acc_ref)

    if last:
        for i in range(PAIR):
            keep = (step * PAIR + i < live_ref[0]).astype(F32)
            gp_ref[i * rows : i * rows + seq, :] = g_ref[i].astype(F32) * keep
            gp_ref[i * rows + seq : (i + 1) * rows, :] = jnp.zeros((rows - seq, width), F32)
        g = gp_ref[...]
    else:
        g = g_ref[...]
    low = g.astype(BF16)
    turned = low.T
    normed, scale = norm(x1_ref[...])
    hidden = (normed * vec_ref[5:6, :] + vec_ref[6:7, :]).astype(BF16)
    turned_h = hidden.T
    acc_ref[2:3, :] += column_sum(low.astype(F32))
    total = jnp.zeros_like(g)
    for j in range(FF // width):
        cols = slice(j * width, (j + 1) * width)
        down_ref[:, cols] += dot(turned, act_ref[:, cols])
        start = width + FF + j * width
        ga = dot(low, w_ref[:, start : start + width]).astype(BF16).astype(F32)
        gu = (ga * slope_ref[:, cols]).astype(BF16)
        up_ref[:, cols] += dot(turned_h, gu)
        acc_ref[3 + j : 4 + j, :] += column_sum(gu.astype(F32))
        total = total + dot_nt(gu, w_ref[:, (1 + j) * width : (2 + j) * width])
    gh2 = total.astype(BF16).astype(F32)
    acc_ref[0:1, :] += column_sum(gh2 * normed)
    acc_ref[1:2, :] += column_sum(gh2)
    gx1_ref[...] = g + norm_back(gh2, normed, scale, vec_ref[5:6, :])

    @pl.when(step == pl.num_programs(0) - 1)
    def _():
        def up(ref):
            ref[:, :FF] = up_ref[...].astype(BF16)
            put_vectors(acc_ref, ref)

        def down(ref):
            ref[:, :FF] = down_ref[...].astype(BF16)
            ref[:, FF:] = jnp.zeros((width, TILE), BF16)

        put_grads(core_ref[0], up, down, keep_ref, send_ref)


def attn_backward(
    first, seq, rows, ats, starts, core_ref, qplace_ref, place_ref, g_ref, x_ref, qkv_ref, lse_ref, o_ref,
    vec_ref, *refs
):
    qsources, refs = refs[: ats[0]], refs[ats[0] :]
    sources, refs = refs[: ats[1]], refs[ats[1] :]
    gx_ref, keep_ref, send_ref, w_ref, wout_ref, gw_ref, gout_ref, acc_ref, gqkv_ref, go_ref, sems, osems = refs
    width = x_ref.shape[1]
    heads = width // HEAD
    step = pl.program_id(0)

    @pl.when(step == 0)
    def _():
        load_weights(core_ref, qplace_ref, qsources, starts[0], w_ref, sems)
        load_first(core_ref, place_ref, sources, starts[1], wout_ref, osems)
        gw_ref[...] = jnp.zeros_like(gw_ref)
        gout_ref[...] = jnp.zeros_like(gout_ref)
        acc_ref[...] = jnp.zeros_like(acc_ref)

    low = g_ref[...].astype(BF16)
    gout_ref[...] += dot(o_ref[...].T, low)
    acc_ref[4:5, :] += column_sum(low.astype(F32))
    go_ref[...] = dot_nt(low, wout_ref[...]).astype(BF16)

    edge = seq // 16 * 16
    alive = lax.broadcasted_iota(jnp.int32, (rows - edge, rows), 0) < seq - edge
    lane = lax.broadcasted_iota(jnp.int32, (rows, TILE), 1)
    zero = jnp.zeros((), BF16)
    for i in range(PAIR):
        span = slice(i * rows, (i + 1) * rows)
        turned_k = qkv_ref[span, width : 2 * width].T
        turned_gq = []
        for pair in range(heads // 2):
            tile = pair * TILE
            query = qkv_ref[span, tile : tile + TILE]
            key_part = qkv_ref[span, width + tile : width + tile + TILE]
            value = qkv_ref[span, 2 * width + tile : 2 * width + tile + TILE]
            go = go_ref[span, tile : tile + TILE]
            gks, gvs = [], []
            for e in range(2):
                h = 2 * pair + e
                mine = (lane < HEAD) if e == 0 else (lane >= HEAD)
                scores = dot_nt(key_part, jnp.where(mine, query, zero)) - lse_ref[i, h : h + 1, :rows]
                gp = dot_nt(value, jnp.where(mine, go, zero))
                p_low = jnp.exp(scores[:edge])
                p_high = jnp.where(alive, jnp.exp(scores[edge:]), 0.0)
                probs = jnp.concatenate([p_low.astype(BF16), p_high.astype(BF16)], 0)
                gp_low, gp_high = gp[:edge], gp[edge:]
                mean = column_sum(gp_low * p_low) + column_sum(gp_high * p_high)
                gs = jnp.concatenate(
                    [
                        (p_low * (gp_low - mean)).astype(BF16),
                        (p_high * (gp_high - mean)).astype(BF16),
                    ],
                    0,
                )
                gvs.append(dot(probs, go))
                gks.append(dot(gs, query))
                turned_gq.append((dot(turned_k[h * HEAD : (h + 1) * HEAD], gs) * 0.125).astype(BF16))
            gqkv_ref[span, width + tile : width + tile + TILE] = jnp.where(
                lane < HEAD, gks[0], gks[1]
            ).astype(BF16)
            gqkv_ref[span, 2 * width + tile : 2 * width + tile + TILE] = jnp.where(
                lane < HEAD, gvs[0], gvs[1]
            ).astype(BF16)
        gqkv_ref[span, :width] = jnp.concatenate(turned_gq, 0).T

    normed, scale = norm(x_ref[...])
    hidden = (normed * vec_ref[0:1, :] + vec_ref[1:2, :]).astype(BF16)
    turned_h = hidden.T
    total = jnp.zeros((PAIR * rows, width), F32)
    for j in range(3):
        cols = slice(j * width, (j + 1) * width)
        part = gqkv_ref[:, cols]
        gw_ref[:, cols] += dot(turned_h, part)
        total = total + dot_nt(part, w_ref[:, cols])
        if j != 1:
            at = 2 if j == 0 else 3
            acc_ref[at : at + 1, :] += column_sum(part.astype(F32))
    gh = total.astype(BF16).astype(F32)
    acc_ref[0:1, :] += column_sum(gh * normed)
    acc_ref[1:2, :] += column_sum(gh)
    gx = g_ref[...] + norm_back(gh, normed, scale, vec_ref[0:1, :])
    if first:
        for i in range(PAIR):
            gx_ref[i] = gx[i * rows : i * rows + seq]
    else:
        gx_ref[...] = gx

    @pl.when(step == pl.num_programs(0) - 1)
    def _():
        def one(ref):
            ref[:, : 2 * width] = gw_ref[:, : 2 * width].astype(BF16)
            put_vectors(acc_ref, ref)

        def two(ref):
            ref[:, :width] = gw_ref[:, 2 * width :].astype(BF16)
            ref[:, width : 2 * width] = gout_ref[...].astype(BF16)
            ref[:, 2 * width :] = jnp.zeros((width, TILE), BF16)

        put_grads(core_ref[0], one, two, keep_ref, send_ref)


def adamw(grad, first, second, old):
    first_new = 0.9 * first + 0.1 * grad
    second_new = 0.999 * second + 0.001 * grad * grad
    first_hat = first_new / (1.0 - 0.9**STEP)
    second_hat = second_new / (1.0 - 0.999**STEP)
    change = -0.01 * (first_hat / (jnp.sqrt(second_hat) + 1e-08) + 0.05 * old)
    return (first_new, second_new, change)


def step_kernel(aliased, core_ref, mine_ref, other_ref, one_ref, two_ref, old_ref, *refs):
    grad_ref, one_new_ref, two_new_ref, change_ref = refs[-4:]
    cols = grad_ref.shape[2]

    def put(from_ref):
        grad = from_ref[:, :cols].astype(F32)
        grad_ref[0] = grad
        one_new_ref[0], two_new_ref[0], change_ref[0] = adamw(grad, one_ref[0], two_ref[0], old_ref[0])

    @pl.when(core_ref[0] == pl.program_id(0))
    def _():
        put(mine_ref)

    @pl.when(core_ref[0] != pl.program_id(0))
    def _():
        put(other_ref)


def smem():
    return pl.BlockSpec(memory_space=pltpu.SMEM)


def whole(shape):
    zeros = (0,) * len(shape)
    return pl.BlockSpec(shape, lambda i: zeros)


def cost(flops, moved, exps):
    return pl.CostEstimate(flops=int(flops), bytes_accessed=int(moved), transcendentals=int(exps))


def params():
    return pltpu.CompilerParams(
        dimension_semantics=("arbitrary",), vmem_limit_bytes=VMEM_LIMIT
    )


def struct(shape, kind):
    return jax.ShapeDtypeStruct(shape, kind)


class Weights:
    def __init__(self, arrays, place, start, half):
        self.arrays, self.place, self.start, self.half = arrays, place, start, half

    def specs(self):
        return [pl.BlockSpec(memory_space=pl.ANY)] * len(self.arrays)

    def sems(self):
        return pltpu.SemaphoreType.DMA((sum(a.shape[0] for a in self.arrays),))


def call(kernel, after, in_specs, **rest):
    count = len(after)

    def run(*refs):
        kernel(*refs[count:])

    made = pl.pallas_call(
        run, in_specs=[pl.BlockSpec(memory_space=pl.ANY)] * count + in_specs, **rest
    )
    return lambda *args: made(*after, *args)


class Layers:
    def __init__(self, core, images, seq, width):
        self.core, self.images, self.seq, self.width = core, images, seq, width
        self.rows = -(-seq // 16) * 16
        self.grid = (images // PAIR,)
        self.total = images * self.rows
        self.block = PAIR * self.rows

    def tall(self, cols):
        return pl.BlockSpec((self.block, cols), lambda i: (i, 0))

    def images_spec(self):
        return pl.BlockSpec((PAIR, self.seq, self.width), lambda i: (i, 0, 0))

    def lse_spec(self):
        return pl.BlockSpec((PAIR, 8, 256), lambda i: (i, 0, 0))

    def attn_forward(self, x, wq, first, after):
        w, t = self.width, self.total
        outs = [
            (self.tall(3 * w), struct((t, 3 * w), BF16)),
            (self.tall(w), struct((t, w), BF16)),
            (self.lse_spec(), struct((self.images, 8, 256), F32)),
            (whole((16, w)), struct((16, w), F32)),
        ]
        if first:
            outs.append((self.tall(w), struct((t, w), F32)))
        return call(
            functools.partial(attn_forward, first, self.seq, self.rows, len(wq.arrays), wq.start),
            after,
            [smem(), smem(), self.images_spec() if first else self.tall(w)] + wq.specs(),
            grid=self.grid,
            out_specs=[o[0] for o in outs],
            out_shape=[o[1] for o in outs],
            scratch_shapes=[pltpu.VMEM((w, 2 * wq.half), BF16), wq.sems()],
            compiler_params=params(),
            cost_estimate=cost(1.7e10, 2e7, 3e6),
        )(self.core, wq.place, x, *wq.arrays)

    def mlp_forward(self, x, o, wr, vec, last, after):
        w, t = self.width, self.total
        outs = [
            (self.tall(w), struct((t, w), F32)),
            (self.tall(FF), struct((t, FF), BF16)),
            (self.tall(FF), struct((t, FF), F32)),
            (self.images_spec(), struct((self.images, self.seq, w), F32))
            if last
            else (self.tall(w), struct((t, w), F32)),
        ]
        return call(
            functools.partial(mlp_forward, last, self.seq, self.rows, len(wr.arrays), wr.start),
            after,
            [smem(), smem(), self.tall(w), self.tall(w), whole(vec.shape)] + wr.specs(),
            grid=self.grid,
            out_specs=[o[0] for o in outs],
            out_shape=[o[1] for o in outs],
            scratch_shapes=[pltpu.VMEM((w, 2 * wr.half), BF16), wr.sems()],
            compiler_params=params(),
            cost_estimate=cost(2.2e10, 3e7, 3e6),
        )(self.core, wr.place, x, o, vec, *wr.arrays)

    def mlp_backward(self, live, g, x1, act, slope, wr, vec, last, after):
        w, t = self.width, self.total
        return call(
            functools.partial(mlp_backward, last, self.seq, self.rows, len(wr.arrays), wr.start),
            after,
            [
                smem(), smem(), smem(),
                self.images_spec() if last else self.tall(w),
                self.tall(w), self.tall(FF), self.tall(FF), whole(vec.shape),
            ]
            + wr.specs(),
            grid=self.grid,
            out_specs=[self.tall(w), whole((w, FF + TILE)), whole((w, FF + TILE))],
            out_shape=[
                struct((t, w), F32), struct((w, FF + TILE), BF16), struct((w, FF + TILE), BF16),
            ],
            scratch_shapes=[
                pltpu.VMEM((w, 2 * wr.half), BF16),
                pltpu.VMEM((w, FF), F32),
                pltpu.VMEM((w, FF), F32),
                pltpu.VMEM((8, w), F32),
                pltpu.VMEM((self.block, w), F32),
                wr.sems(),
            ],
            compiler_params=params(),
            cost_estimate=cost(2.4e10, 3e7, 3e6),
        )(self.core, wr.place, live, g, x1, act, slope, vec, *wr.arrays)

    def attn_backward(self, g, x, qkv, lse, o, wq, wr, vec, first, after):
        w, t = self.width, self.total
        return call(
            functools.partial(
                attn_backward, first, self.seq, self.rows,
                (len(wq.arrays), len(wr.arrays)), (wq.start, wr.start),
            ),
            after,
            [
                smem(), smem(), smem(), self.tall(w), self.tall(w), self.tall(3 * w),
                self.lse_spec(), self.tall(w), whole(vec.shape),
            ]
            + wq.specs()
            + wr.specs(),
            grid=self.grid,
            out_specs=[
                self.images_spec() if first else self.tall(w),
                whole((w, 2 * w + TILE)), whole((w, 2 * w + TILE)),
            ],
            out_shape=[
                struct((self.images, self.seq, w), F32) if first else struct((t, w), F32),
                struct((w, 2 * w + TILE), BF16), struct((w, 2 * w + TILE), BF16),
            ],
            scratch_shapes=[
                pltpu.VMEM((w, 2 * wq.half), BF16),
                pltpu.VMEM((w, w), BF16),
                pltpu.VMEM((w, 3 * w), F32),
                pltpu.VMEM((w, w), F32),
                pltpu.VMEM((8, w), F32),
                pltpu.VMEM((self.block, 3 * w), BF16),
                pltpu.VMEM((self.block, w), BF16),
                wq.sems(),
                wr.sems(),
            ],
            compiler_params=params(),
            cost_estimate=cost(3e10, 2e7, 3e6),
        )(self.core, wq.place, wr.place, g, x, qkv, lse, o, vec, *wq.arrays, *wr.arrays)


def flip(axis, bit):
    return [(i, i ^ bit) for i in range(lax.axis_size(axis))]


def swap_cores(value):
    return lax.ppermute(value, "rep", flip("rep", 1))


def own_half(packed, core):
    half = packed.shape[1] // 2
    return lax.dynamic_slice_in_dim(packed, core * half, half, 1)


def spread(own):
    return jnp.broadcast_to(own[None], (lax.axis_size("shard"),) + own.shape)


def gather_direct(copies):
    mine = lax.all_to_all(copies, "shard", 0, 0, tiled=True)
    return [mine, swap_cores(mine)], jnp.arange(copies.shape[0], dtype=jnp.int32)


def near_permutes(own):
    count = lax.axis_size("shard")
    me = lax.axis_index("shard").astype(jnp.int32)
    parts = [own] + [lax.ppermute(own, "shard", flip("shard", k)) for k in range(2, count, 2)]
    even = jnp.arange(0, count, 2, dtype=jnp.int32)
    return jnp.stack(parts), jnp.concatenate([me ^ even, me ^ even ^ 1])


def near_exchange(own):
    count = lax.axis_size("shard")
    parity = lax.axis_index("shard").astype(jnp.int32) % 2
    groups = [list(range(p, count, 2)) for p in range(2)]
    near = lax.all_to_all(
        jnp.broadcast_to(own[None], (count // 2,) + own.shape),
        "shard", 0, 0, axis_index_groups=groups, tiled=True,
    )
    even = jnp.arange(0, count, 2, dtype=jnp.int32)
    return near, jnp.concatenate([even + parity, even + 1 - parity])


def after(value, *others):
    return lax.optimization_barrier((value,) + others)[0]


def join_cores(keep, send):
    other = swap_cores(send)
    return (keep.astype(F32) + other.astype(F32)).astype(BF16)


def exchange_shards(joined):
    count = lax.axis_size("shard")
    rows, cols = joined.shape
    return lax.all_to_all(joined.reshape(count, rows // count, cols), "shard", 0, 0, tiled=True)


def finish_group(parts):
    mine = jnp.sum(parts.astype(F32), 0).astype(BF16)
    bit = 2
    while bit < lax.axis_size("rep"):
        other = lax.ppermute(mine, "rep", flip("rep", bit))
        mine = (mine.astype(F32) + other.astype(F32)).astype(BF16)
        bit *= 2
    return mine, swap_cores(mine)


def update_group(core, pair, state, outs, layer, at, cols):
    mine, other = pair
    spec = pl.BlockSpec((1, mine.shape[0], cols), lambda j: (layer, 0, at + j))
    shape = struct(state[0].shape, F32)
    given = list(outs) if outs is not None else []
    return pl.pallas_call(
        functools.partial(step_kernel, len(given)),
        grid=(2,),
        in_specs=[smem(), whole(mine.shape), whole(other.shape), spec, spec, spec]
        + [pl.BlockSpec(memory_space=pl.ANY)] * len(given),
        out_specs=[spec] * 4,
        out_shape=[shape] * 4,
        input_output_aliases={6 + i: i for i in range(len(given))},
        compiler_params=params(),
        cost_estimate=cost(1e6, 4e6, 0),
    )(core, mine, other, *state, *given)


def local(
    tokens, weights, vectors, moment_one, moment_two, vector_one, vector_two, images, cotangent
):
    count, seq, width = tokens.shape
    layers = weights.shape[0]
    core = lax.axis_index("rep") % 2
    core_arr = core.reshape(1).astype(jnp.int32)
    plan = Layers(core_arr, count, seq, width)
    packs = []
    for index in range(layers):
        low = weights[index].astype(BF16)
        turned = jnp.pad(vectors[index].T.astype(BF16), ((0, 0), (0, TILE - vectors.shape[1])))
        attn_pack = jnp.concatenate([low[:, : 3 * width], turned], 1)
        rest = low[:, 3 * width :]
        rest_pack = jnp.pad(rest, ((0, 0), (0, -rest.shape[1] % (2 * TILE))))
        packs.append((own_half(attn_pack, core), own_half(rest_pack, core)))
    attn_own, rest_own = packs[0]
    copies, rest_own = lax.optimization_barrier((spread(attn_own), rest_own))
    arrays, place = gather_direct(copies)
    near, near_place = near_permutes(rest_own)
    gathered = [[Weights(arrays, place, 0, attn_own.shape[1]), None]]
    stored = []
    x = tokens
    for index in range(layers):
        first, last = index == 0, index == layers - 1
        wq = gathered[index][0]
        far = lax.ppermute(near, "shard", flip("shard", 1)) if first else None
        others = [near]
        if not last:
            next_own = after(jnp.concatenate(packs[index + 1], 1), near)
            next_near, next_place = near_exchange(next_own)
        qkv, o, lse, vec, *xp = plan.attn_forward(x, wq, first, others if first else [])
        xp = xp[0] if first else x
        if first:
            held = [near, far, swap_cores(near), swap_cores(after(far, o))]
            gathered[0][1] = Weights(held, near_place, 0, rest_own.shape[1])
        if not last:
            near = after(next_near, o)
            far = lax.ppermute(near, "shard", flip("shard", 1))
            near_other = swap_cores(near)
        x1, act, slope, x = plan.mlp_forward(
            xp, o, gathered[index][1], vec, last, [] if last else [near]
        )
        if not last:
            held = [near, far, near_other, swap_cores(after(far, x1))]
            qhalf, half = (p.shape[1] for p in packs[index + 1])
            gathered.append(
                [Weights(held, next_place, 0, qhalf), Weights(held, next_place, qhalf, half)]
            )
        stored.append((xp, qkv, o, lse, vec, x1, act, slope))
    output = x
    g = cotangent
    state = (moment_one, moment_two, weights)
    groups = []
    before = []

    def send_group(keep, send):
        if groups:
            keep, send, groups[-1] = lax.optimization_barrier((keep, send, groups[-1]))
        joined = join_cores(keep, send)
        groups.append(exchange_shards(joined))
        return [joined]

    for index in reversed(range(layers)):
        first, last = index == 0, index == layers - 1
        wq, wr = gathered[index]
        xp, qkv, o, lse, vec, x1, act, slope = stored[index]
        gx1, keep, send = plan.mlp_backward(images, g, x1, act, slope, wr, vec, last, before)
        before = send_group(keep, send)
        g, keep, send = plan.attn_backward(gx1, xp, qkv, lse, o, wq, wr, vec, first, before)
        before = send_group(keep, send)
    outs = None
    vec_grads = [None] * layers
    for n, index in enumerate(reversed(range(layers))):
        pair_m = finish_group(groups[2 * n])
        pair_a = finish_group(groups[2 * n + 1])
        outs = update_group(core_arr, pair_m, state, outs, index, 1, FF)
        outs = update_group(core_arr, pair_a, state, outs, index, 0, 2 * width)
        tails = [
            jnp.where(core == 0, p[0][:, -TILE:], p[1][:, -TILE:]).astype(F32).T
            for p in (pair_a, pair_m)
        ]
        vec_grads[index] = jnp.concatenate([tails[0][:5], tails[1][:7]], 0)
    vector_grad = jnp.stack(vec_grads)
    weight_grad, moment_one_new, moment_two_new, update = outs
    vector_one_new, vector_two_new, vector_update = adamw(
        vector_grad, vector_one, vector_two, vectors
    )
    return (
        output,
        g,
        weight_grad,
        vector_grad,
        moment_one_new,
        moment_two_new,
        vector_one_new,
        vector_two_new,
        update,
        vector_update,
    )


def solution(mesh):
    in_specs = (
        P(("rep", "shard"), None, None),
        P(None, "shard", None),
        P(None, None, "shard"),
        P(None, "shard", None),
        P(None, "shard", None),
        P(None, None, "shard"),
        P(None, None, "shard"),
        P(("rep", "shard")),
        P(("rep", "shard"), None, None),
    )
    out_specs = (
        P(("rep", "shard"), None, None),
        P(("rep", "shard"), None, None),
        P(None, "shard", None),
        P(None, None, "shard"),
        P(None, "shard", None),
        P(None, "shard", None),
        P(None, None, "shard"),
        P(None, None, "shard"),
        P(None, "shard", None),
        P(None, None, "shard"),
    )
    return jax.shard_map(local, mesh=mesh, in_specs=in_specs, out_specs=out_specs, check_vma=False)
```

```python
import functools
import math

import jax
import jax.numpy as jnp
from jax import lax
from jax.experimental import pallas as pl
from jax.experimental.pallas import tpu as pltpu
from jax.sharding import PartitionSpec as P

HEAD = 64
FF = 1536
STEP = 10
PAIR = 2
TILE = 128
CHUNK = 768
NEG = -1e30
F32 = jnp.float32
BF16 = jnp.bfloat16
VMEM_LIMIT = 60 * 1024 * 1024


def dot(left, right):
    return jnp.dot(left, right, preferred_element_type=F32)


def dot_nt(left, right):
    return lax.dot_general(left, right, (((1,), (1,)), ((), ())), preferred_element_type=F32)


def dot_tn(left, right):
    return lax.dot_general(left, right, (((0,), (0,)), ((), ())), preferred_element_type=F32)


def norm(values):
    center = values - jnp.mean(values, -1, keepdims=True)
    scale = lax.rsqrt(jnp.mean(center * center, -1, keepdims=True) + 1e-06)
    return center * scale, scale


def norm_back(grad, normed, scale, gain):
    inner = grad * gain
    return scale * (
        inner
        - jnp.mean(inner, -1, keepdims=True)
        - normed * jnp.mean(inner * normed, -1, keepdims=True)
    )


def gelu_parts(u):
    phi = 0.5 + 0.5 * lax.erf(u * math.sqrt(0.5))
    slope = phi + u * (jnp.exp2((u * u) * (-0.5 * math.log2(math.e))) * (1.0 / math.sqrt(2.0 * math.pi)))
    return u * phi, slope


def bias_up(vec_ref, width):
    return jnp.concatenate([vec_ref[8 + j : 9 + j, :] for j in range(FF // width)], 1)


def load_weights(core_ref, place_ref, sources, start, whole_ref, sems):
    half = whole_ref.shape[1] // 2
    per_core = len(sources) // 2
    copies = []
    for n, source in enumerate(sources):
        at = core_ref[0] if n < per_core else 1 - core_ref[0]
        cols = pl.ds(pl.multiple_of(at * half, TILE), half)
        copies += row_copies(
            place_ref, source, n % per_core, slice(start, start + half), whole_ref, cols, sems, len(copies)
        )
    for copy in copies:
        copy.start()
    for copy in copies:
        copy.wait()


def load_first(core_ref, place_ref, sources, start, whole_ref, sems):
    per_core = len(sources) // 2
    size = whole_ref.shape[1]

    def load(chosen):
        copies = []
        for n, source in enumerate(chosen):
            copies += row_copies(
                place_ref, source, n, slice(start, start + size), whole_ref, slice(0, size), sems, len(copies)
            )
        for copy in copies:
            copy.start()
        for copy in copies:
            copy.wait()

    @pl.when(core_ref[0] == 0)
    def _():
        load(sources[:per_core])

    @pl.when(core_ref[0] != 0)
    def _():
        load(sources[per_core:])


def row_copies(place_ref, source, nth, taken, whole_ref, cols, sems, at):
    count, rows = source.shape[:2]
    copies = []
    for k in range(count):
        row = pl.multiple_of(place_ref[nth * count + k] * rows, rows)
        copies.append(
            pltpu.make_async_copy(
                source.at[k, :, taken], whole_ref.at[pl.ds(row, rows), cols], sems.at[at + k]
            )
        )
    return copies


def attn_forward(first, seq, rows, at, start, core_ref, place_ref, x_ref, *refs):
    sources, refs = refs[:at], refs[at:]
    if first:
        qkv_ref, o_ref, lse_ref, vec_ref, xp_ref, w_ref, sems = refs
    else:
        qkv_ref, o_ref, lse_ref, vec_ref, w_ref, sems = refs
        xp_ref = x_ref
    width = o_ref.shape[1]
    heads = width // HEAD

    @pl.when(pl.program_id(0) == 0)
    def _():
        load_weights(core_ref, place_ref, sources, start, w_ref, sems)
        turned = w_ref[:, 3 * width : 3 * width + TILE].astype(F32).T
        vec_ref[...] = turned[: vec_ref.shape[0]]

    if first:
        for i in range(PAIR):
            xp_ref[i * rows : i * rows + seq, :] = x_ref[i].astype(F32)
            xp_ref[i * rows + seq : (i + 1) * rows, :] = jnp.zeros((rows - seq, width), F32)

    normed, _ = norm(xp_ref[...])
    hidden = (normed * vec_ref[0:1, :] + vec_ref[1:2, :]).astype(BF16)
    qkv = dot(hidden, w_ref[:, : 3 * width])
    qkv_ref[:, :width] = ((qkv[:, :width] + vec_ref[2:3, :]) * 0.125).astype(BF16)
    qkv_ref[:, width : 2 * width] = qkv[:, width : 2 * width].astype(BF16)
    qkv_ref[:, 2 * width :] = (qkv[:, 2 * width :] + vec_ref[3:4, :]).astype(BF16)

    edge = seq // 16 * 16
    alive = lax.broadcasted_iota(jnp.int32, (rows - edge, rows), 0) < seq - edge
    left = lax.broadcasted_iota(jnp.int32, (rows, TILE), 1) < HEAD
    work = [(i, h) for i in range(PAIR) for h in range(heads)]

    def scores_of(i, h):
        span = slice(i * rows, (i + 1) * rows)
        tile = h * HEAD // TILE * TILE
        mine = left if h * HEAD == tile else ~left
        query = jnp.where(mine, qkv_ref[span, tile : tile + TILE], jnp.zeros((), BF16))
        return dot_nt(qkv_ref[span, width + tile : width + tile + TILE], query)

    def finish(i, h, probs, total):
        out = dot(turned_v[i][h * HEAD : (h + 1) * HEAD], probs) * (1.0 / total)
        outs[i].append(out.astype(BF16))
        if h == heads - 1:
            o_ref[i * rows : (i + 1) * rows, :] = jnp.concatenate(outs[i], 0).T

    outs = [[] for _ in range(PAIR)]
    turned_v = [qkv_ref[i * rows : (i + 1) * rows, 2 * width :].T for i in range(PAIR)]
    ahead = [scores_of(*item) for item in work[:4]]
    behind = []
    for n, (i, h) in enumerate(work):
        if n + 4 < len(work):
            ahead.append(scores_of(*work[n + 4]))
        scores = ahead.pop(0)
        low = scores[:edge]
        high = jnp.where(alive, scores[edge:], NEG)
        top = jnp.maximum(jnp.max(low, 0, keepdims=True), jnp.max(high, 0, keepdims=True))
        low = jnp.exp(low - top)
        high = jnp.exp(high - top)
        total = jnp.sum(low, 0, keepdims=True) + jnp.sum(high, 0, keepdims=True)
        lse_ref[i, h : h + 1, :rows] = top + jnp.log(total)
        behind.append((i, h, jnp.concatenate([low.astype(BF16), high.astype(BF16)], 0), total))
        if len(behind) > 1:
            finish(*behind.pop(0))
    for item in behind:
        finish(*item)


def mlp_forward(last, seq, rows, at, start, core_ref, place_ref, x_ref, o_ref, vec_ref, *refs):
    sources, refs = refs[:at], refs[at:]
    x1_ref, act_ref, slope_ref, out_ref, w_ref, sems = refs
    width = x_ref.shape[1]

    @pl.when(pl.program_id(0) == 0)
    def _():
        load_weights(core_ref, place_ref, sources, start, w_ref, sems)

    x1 = x_ref[...] + dot(o_ref[...], w_ref[:, :width]) + vec_ref[4:5, :]
    x1_ref[...] = x1
    normed, _ = norm(x1)
    hidden = (normed * vec_ref[5:6, :] + vec_ref[6:7, :]).astype(BF16)
    bias = bias_up(vec_ref, width)
    units = [(r, j) for r in range(0, x1.shape[0], x1.shape[0]) for j in range(0, FF, CHUNK)]
    size = x1.shape[0]

    def up(r, j):
        return dot(hidden[r : r + size], w_ref[:, width + j : width + j + CHUNK])

    totals = {r: x1[r : r + size] + vec_ref[7:8, :] for r, _ in units}

    def down(r, j, act):
        start = width + FF + j
        totals[r] = totals[r] + dot_nt(act, w_ref[:, start : start + CHUNK])

    ahead = up(*units[0])
    behind = None
    for n, (r, j) in enumerate(units):
        u = ahead
        if n + 1 < len(units):
            ahead = up(*units[n + 1])
        if behind is not None:
            down(*behind)
        acts = []
        for k in range(0, size, 16):
            act, slope = gelu_parts(u[k : k + 16] + bias[:, j : j + CHUNK])
            slope_ref[r + k : r + k + 16, j : j + CHUNK] = slope
            acts.append(act.astype(BF16))
        act = jnp.concatenate(acts, 0)
        act_ref[r : r + size, j : j + CHUNK] = act
        behind = (r, j, act)
    down(*behind)
    total = jnp.concatenate([totals[r] for r in sorted(totals)], 0)
    if last:
        for i in range(PAIR):
            out_ref[i] = total[i * rows : i * rows + seq]
    else:
        out_ref[...] = total


def put_grads(core, first_of, second_of, keep_ref, send_ref):
    @pl.when(core == 0)
    def _():
        first_of(keep_ref)
        second_of(send_ref)

    @pl.when(core != 0)
    def _():
        first_of(send_ref)
        second_of(keep_ref)


def put_vectors(acc_ref, ref):
    size = acc_ref.shape[0]
    padded = jnp.concatenate(
        [acc_ref[...], jnp.zeros((TILE - size, acc_ref.shape[1]), F32)], 0
    )
    ref[:, ref.shape[1] - TILE :] = padded.T.astype(BF16)


def column_sum(values):
    return jnp.sum(values, 0, keepdims=True)


def mlp_backward(
    last, seq, rows, at, start, core_ref, place_ref, live_ref, g_ref, x1_ref, act_ref, slope_ref, vec_ref, *refs
):
    sources, refs = refs[:at], refs[at:]
    gx1_ref, keep_ref, send_ref, w_ref, up_ref, down_ref, acc_ref, bias_ref, gp_ref, sems = refs
    width = x1_ref.shape[1]
    step = pl.program_id(0)

    @pl.when(step == 0)
    def _():
        load_weights(core_ref, place_ref, sources, start, w_ref, sems)
        up_ref[...] = jnp.zeros_like(up_ref)
        bias_ref[...] = jnp.zeros_like(bias_ref)
        down_ref[...] = jnp.zeros_like(down_ref)
        acc_ref[...] = jnp.zeros_like(acc_ref)

    if last:
        for i in range(PAIR):
            keep = (step * PAIR + i < live_ref[0]).astype(F32)
            gp_ref[i * rows : i * rows + seq, :] = g_ref[i].astype(F32) * keep
            gp_ref[i * rows + seq : (i + 1) * rows, :] = jnp.zeros((rows - seq, width), F32)
        g = gp_ref[...]
    else:
        g = g_ref[...]
    low = g.astype(BF16)
    size = CHUNK

    def back(j):
        start = width + FF + j
        return dot(low, w_ref[:, start : start + size])

    ahead = back(0)
    turned = low.T
    normed, scale = norm(x1_ref[...])
    hidden = (normed * vec_ref[5:6, :] + vec_ref[6:7, :]).astype(BF16)
    turned_h = hidden.T
    acc_ref[2:3, :] += column_sum(g)
    total = None

    def finish(total, j, gu):
        up_ref[:, j : j + size] += dot(turned_h, gu)
        part = dot_nt(gu, w_ref[:, width + j : width + j + size])
        return part if total is None else total + part

    behind = None
    for j in range(0, FF, size):
        ga = ahead
        if j + size < FF:
            ahead = back(j + size)
        down_ref[:, j : j + size] += dot(turned, act_ref[:, j : j + size])
        if behind is not None:
            total = finish(total, *behind)
        gus = []
        sums = jnp.zeros((8, size), F32)
        for r in range(0, ga.shape[0], 16):
            gu = ga[r : r + 16].astype(BF16).astype(F32) * slope_ref[r : r + 16, j : j + size]
            sums = sums + gu[:8] + gu[8:]
            gus.append(gu.astype(BF16))
        bias_ref[:, j : j + size] += sums
        behind = (j, jnp.concatenate(gus, 0))
    total = finish(total, *behind)
    gh2 = total.astype(BF16).astype(F32)
    acc_ref[0:1, :] += column_sum(gh2 * normed)
    acc_ref[1:2, :] += column_sum(gh2)
    gx1_ref[...] = g + norm_back(gh2, normed, scale, vec_ref[5:6, :])

    @pl.when(step == pl.num_programs(0) - 1)
    def _():
        sums = column_sum(bias_ref[...])
        for j in range(FF // width):
            acc_ref[3 + j : 4 + j, :] = sums[:, j * width : (j + 1) * width]

        def up(ref):
            ref[:, :FF] = up_ref[...].astype(BF16)
            put_vectors(acc_ref, ref)

        def down(ref):
            ref[:, :FF] = down_ref[...].astype(BF16)
            ref[:, FF:] = jnp.zeros((width, TILE), BF16)

        put_grads(core_ref[0], up, down, keep_ref, send_ref)


def attn_backward(
    first, seq, rows, ats, starts, core_ref, qplace_ref, place_ref, g_ref, x_ref, qkv_ref, lse_ref, o_ref,
    vec_ref, *refs
):
    qsources, refs = refs[: ats[0]], refs[ats[0] :]
    sources, refs = refs[: ats[1]], refs[ats[1] :]
    gx_ref, keep_ref, send_ref, w_ref, wout_ref, gw_ref, gout_ref, acc_ref, gqkv_ref, go_ref, sems, osems = refs
    width = x_ref.shape[1]
    heads = width // HEAD
    step = pl.program_id(0)

    @pl.when(step == 0)
    def _():
        load_weights(core_ref, qplace_ref, qsources, starts[0], w_ref, sems)
        load_first(core_ref, place_ref, sources, starts[1], wout_ref, osems)
        gw_ref[...] = jnp.zeros_like(gw_ref)
        gout_ref[...] = jnp.zeros_like(gout_ref)
        acc_ref[...] = jnp.zeros_like(acc_ref)

    low = g_ref[...].astype(BF16)
    gout_ref[...] += dot(o_ref[...].T, low)
    acc_ref[4:5, :] += column_sum(g_ref[...])
    go_ref[...] = dot_nt(low, wout_ref[...]).astype(BF16)

    edge = seq // 16 * 16
    alive = lax.broadcasted_iota(jnp.int32, (rows - edge, rows), 0) < seq - edge
    left = lax.broadcasted_iota(jnp.int32, (rows, TILE), 1) < HEAD
    zero = jnp.zeros((), BF16)
    work = [(i, h) for i in range(PAIR) for h in range(heads)]

    def tile_of(ref, part, i, h):
        at = part * width + h * HEAD // TILE * TILE
        return ref[i * rows : (i + 1) * rows, at : at + TILE]

    def start(i, h):
        mine = left if h * HEAD % TILE == 0 else ~left
        query = jnp.where(mine, tile_of(qkv_ref, 0, i, h), zero)
        go = jnp.where(mine, tile_of(go_ref, 0, i, h), zero)
        return dot_nt(tile_of(qkv_ref, 1, i, h), query), dot_nt(tile_of(qkv_ref, 2, i, h), go)

    def finish(i, h, probs, gs):
        gvs[i].append(dot(probs, tile_of(go_ref, 0, i, h)))
        gks[i].append(dot(gs, tile_of(qkv_ref, 0, i, h)))
        gqs[i].append((dot(turned_k[i][h * HEAD : (h + 1) * HEAD], gs) * 0.125).astype(BF16))
        span = slice(i * rows, (i + 1) * rows)
        if h % 2:
            for part, held in ((1, gks[i]), (2, gvs[i])):
                at = part * width + h * HEAD // TILE * TILE
                gqkv_ref[span, at : at + TILE] = jnp.where(left, held[h - 1], held[h]).astype(BF16)
        if h == heads - 1:
            gqkv_ref[span, :width] = jnp.concatenate(gqs[i], 0).T

    gks, gvs, gqs = ([[] for _ in range(PAIR)] for _ in range(3))
    turned_k = [qkv_ref[i * rows : (i + 1) * rows, width : 2 * width].T for i in range(PAIR)]
    ahead = [start(*item) for item in work[:2]]
    behind = []
    for n, (i, h) in enumerate(work):
        if n + 2 < len(work):
            ahead.append(start(*work[n + 2]))
        scores, gp = ahead.pop(0)
        scores = scores - lse_ref[i, h : h + 1, :rows]
        p_low = jnp.exp(scores[:edge])
        p_high = jnp.where(alive, jnp.exp(scores[edge:]), 0.0)
        probs = jnp.concatenate([p_low.astype(BF16), p_high.astype(BF16)], 0)
        gp_low, gp_high = gp[:edge], gp[edge:]
        mean = column_sum(gp_low * p_low) + column_sum(gp_high * p_high)
        gs_low = (p_low * (gp_low - mean)).astype(BF16)
        gs_high = (p_high * (gp_high - mean)).astype(BF16)
        behind.append((i, h, probs, jnp.concatenate([gs_low, gs_high], 0)))
        if len(behind) > 1:
            finish(*behind.pop(0))
    for item in behind:
        finish(*item)

    normed, scale = norm(x_ref[...])
    hidden = (normed * vec_ref[0:1, :] + vec_ref[1:2, :]).astype(BF16)
    turned_h = hidden.T
    gqkv = gqkv_ref[...]
    gw_ref[...] += dot(turned_h, gqkv)
    total = dot_nt(gqkv, w_ref[:, : 3 * width])
    acc_ref[2:3, :] += column_sum(gqkv[:, :width].astype(F32))
    acc_ref[3:4, :] += column_sum(gqkv[:, 2 * width :].astype(F32))
    gh = total.astype(BF16).astype(F32)
    acc_ref[0:1, :] += column_sum(gh * normed)
    acc_ref[1:2, :] += column_sum(gh)
    gx = g_ref[...] + norm_back(gh, normed, scale, vec_ref[0:1, :])
    if first:
        for i in range(PAIR):
            gx_ref[i] = gx[i * rows : i * rows + seq]
    else:
        gx_ref[...] = gx

    @pl.when(step == pl.num_programs(0) - 1)
    def _():
        def one(ref):
            ref[:, : 2 * width] = gw_ref[:, : 2 * width].astype(BF16)
            put_vectors(acc_ref, ref)

        def two(ref):
            ref[:, :width] = gw_ref[:, 2 * width :].astype(BF16)
            ref[:, width : 2 * width] = gout_ref[...].astype(BF16)
            ref[:, 2 * width :] = jnp.zeros((width, TILE), BF16)

        put_grads(core_ref[0], one, two, keep_ref, send_ref)


def adamw(grad, first, second, old):
    first_new = 0.9 * first + 0.1 * grad
    second_new = 0.999 * second + 0.001 * grad * grad
    first_hat = first_new / (1.0 - 0.9**STEP)
    second_hat = second_new / (1.0 - 0.999**STEP)
    change = -0.01 * (first_hat / (jnp.sqrt(second_hat) + 1e-08) + 0.05 * old)
    return (first_new, second_new, change)


def step_kernel(aliased, core_ref, mine_ref, other_ref, one_ref, two_ref, old_ref, *refs):
    grad_ref, one_new_ref, two_new_ref, change_ref = refs[-4:]
    cols = grad_ref.shape[2]

    def put(from_ref):
        grad = from_ref[:, :cols].astype(F32)
        grad_ref[0] = grad
        one_new_ref[0], two_new_ref[0], change_ref[0] = adamw(grad, one_ref[0], two_ref[0], old_ref[0])

    @pl.when(core_ref[0] == pl.program_id(0))
    def _():
        put(mine_ref)

    @pl.when(core_ref[0] != pl.program_id(0))
    def _():
        put(other_ref)


def smem():
    return pl.BlockSpec(memory_space=pltpu.SMEM)


def whole(shape):
    zeros = (0,) * len(shape)
    return pl.BlockSpec(shape, lambda i: zeros)


def cost(flops, moved, exps):
    return pl.CostEstimate(flops=int(flops), bytes_accessed=int(moved), transcendentals=int(exps))


def params():
    return pltpu.CompilerParams(
        dimension_semantics=("arbitrary",), vmem_limit_bytes=VMEM_LIMIT
    )


def struct(shape, kind):
    return jax.ShapeDtypeStruct(shape, kind)


class Weights:
    def __init__(self, arrays, place, start, half):
        self.arrays, self.place, self.start, self.half = arrays, place, start, half

    def specs(self):
        return [pl.BlockSpec(memory_space=pl.ANY)] * len(self.arrays)

    def sems(self):
        return pltpu.SemaphoreType.DMA((sum(a.shape[0] for a in self.arrays),))


def call(kernel, after, in_specs, **rest):
    count = len(after)

    def run(*refs):
        kernel(*refs[count:])

    made = pl.pallas_call(
        run, in_specs=[pl.BlockSpec(memory_space=pl.ANY)] * count + in_specs, **rest
    )
    return lambda *args: made(*after, *args)


class Layers:
    def __init__(self, core, images, seq, width):
        self.core, self.images, self.seq, self.width = core, images, seq, width
        self.rows = -(-seq // 16) * 16
        self.grid = (images // PAIR,)
        self.total = images * self.rows
        self.block = PAIR * self.rows

    def tall(self, cols):
        return pl.BlockSpec((self.block, cols), lambda i: (i, 0))

    def images_spec(self):
        return pl.BlockSpec((PAIR, self.seq, self.width), lambda i: (i, 0, 0))

    def lse_spec(self):
        return pl.BlockSpec((PAIR, 8, 256), lambda i: (i, 0, 0))

    def attn_forward(self, x, wq, first, after):
        w, t = self.width, self.total
        outs = [
            (self.tall(3 * w), struct((t, 3 * w), BF16)),
            (self.tall(w), struct((t, w), BF16)),
            (self.lse_spec(), struct((self.images, 8, 256), F32)),
            (whole((16, w)), struct((16, w), F32)),
        ]
        if first:
            outs.append((self.tall(w), struct((t, w), F32)))
        return call(
            functools.partial(attn_forward, first, self.seq, self.rows, len(wq.arrays), wq.start),
            after,
            [smem(), smem(), self.images_spec() if first else self.tall(w)] + wq.specs(),
            grid=self.grid,
            out_specs=[o[0] for o in outs],
            out_shape=[o[1] for o in outs],
            scratch_shapes=[pltpu.VMEM((w, 2 * wq.half), BF16), wq.sems()],
            compiler_params=params(),
            cost_estimate=cost(1.7e10, 2e7, 3e6),
        )(self.core, wq.place, x, *wq.arrays)

    def mlp_forward(self, x, o, wr, vec, last, after):
        w, t = self.width, self.total
        outs = [
            (self.tall(w), struct((t, w), F32)),
            (self.tall(FF), struct((t, FF), BF16)),
            (self.tall(FF), struct((t, FF), F32)),
            (self.images_spec(), struct((self.images, self.seq, w), F32))
            if last
            else (self.tall(w), struct((t, w), F32)),
        ]
        return call(
            functools.partial(mlp_forward, last, self.seq, self.rows, len(wr.arrays), wr.start),
            after,
            [smem(), smem(), self.tall(w), self.tall(w), whole(vec.shape)] + wr.specs(),
            grid=self.grid,
            out_specs=[o[0] for o in outs],
            out_shape=[o[1] for o in outs],
            scratch_shapes=[pltpu.VMEM((w, 2 * wr.half), BF16), wr.sems()],
            compiler_params=params(),
            cost_estimate=cost(2.2e10, 3e7, 3e6),
        )(self.core, wr.place, x, o, vec, *wr.arrays)

    def mlp_backward(self, live, g, x1, act, slope, wr, vec, last, after):
        w, t = self.width, self.total
        return call(
            functools.partial(mlp_backward, last, self.seq, self.rows, len(wr.arrays), wr.start),
            after,
            [
                smem(), smem(), smem(),
                self.images_spec() if last else self.tall(w),
                self.tall(w), self.tall(FF), self.tall(FF), whole(vec.shape),
            ]
            + wr.specs(),
            grid=self.grid,
            out_specs=[self.tall(w), whole((w, FF + TILE)), whole((w, FF + TILE))],
            out_shape=[
                struct((t, w), F32), struct((w, FF + TILE), BF16), struct((w, FF + TILE), BF16),
            ],
            scratch_shapes=[
                pltpu.VMEM((w, 2 * wr.half), BF16),
                pltpu.VMEM((w, FF), F32),
                pltpu.VMEM((w, FF), F32),
                pltpu.VMEM((8, w), F32),
                pltpu.VMEM((8, FF), F32),
                pltpu.VMEM((self.block, w), F32),
                wr.sems(),
            ],
            compiler_params=params(),
            cost_estimate=cost(2.4e10, 3e7, 3e6),
        )(self.core, wr.place, live, g, x1, act, slope, vec, *wr.arrays)

    def attn_backward(self, g, x, qkv, lse, o, wq, wr, vec, first, after):
        w, t = self.width, self.total
        return call(
            functools.partial(
                attn_backward, first, self.seq, self.rows,
                (len(wq.arrays), len(wr.arrays)), (wq.start, wr.start),
            ),
            after,
            [
                smem(), smem(), smem(), self.tall(w), self.tall(w), self.tall(3 * w),
                self.lse_spec(), self.tall(w), whole(vec.shape),
            ]
            + wq.specs()
            + wr.specs(),
            grid=self.grid,
            out_specs=[
                self.images_spec() if first else self.tall(w),
                whole((w, 2 * w + TILE)), whole((w, 2 * w + TILE)),
            ],
            out_shape=[
                struct((self.images, self.seq, w), F32) if first else struct((t, w), F32),
                struct((w, 2 * w + TILE), BF16), struct((w, 2 * w + TILE), BF16),
            ],
            scratch_shapes=[
                pltpu.VMEM((w, 2 * wq.half), BF16),
                pltpu.VMEM((w, w), BF16),
                pltpu.VMEM((w, 3 * w), F32),
                pltpu.VMEM((w, w), F32),
                pltpu.VMEM((8, w), F32),
                pltpu.VMEM((self.block, 3 * w), BF16),
                pltpu.VMEM((self.block, w), BF16),
                wq.sems(),
                wr.sems(),
            ],
            compiler_params=params(),
            cost_estimate=cost(3e10, 2e7, 3e6),
        )(self.core, wq.place, wr.place, g, x, qkv, lse, o, vec, *wq.arrays, *wr.arrays)


def flip(axis, bit):
    return [(i, i ^ bit) for i in range(lax.axis_size(axis))]


def swap_cores(value):
    return lax.ppermute(value, "rep", flip("rep", 1))


def own_half(packed, core):
    half = packed.shape[1] // 2
    return lax.dynamic_slice_in_dim(packed, core * half, half, 1)


def spread(own):
    return jnp.broadcast_to(own[None], (lax.axis_size("shard"),) + own.shape)


def gather_direct(copies):
    mine = lax.all_to_all(copies, "shard", 0, 0, tiled=True)
    return [mine, swap_cores(mine)], jnp.arange(copies.shape[0], dtype=jnp.int32)


def near_permutes(own):
    count = lax.axis_size("shard")
    me = lax.axis_index("shard").astype(jnp.int32)
    parts = [own] + [lax.ppermute(own, "shard", flip("shard", k)) for k in range(2, count, 2)]
    even = jnp.arange(0, count, 2, dtype=jnp.int32)
    return jnp.stack(parts), jnp.concatenate([me ^ even, me ^ even ^ 1])


def near_exchange(own):
    count = lax.axis_size("shard")
    parity = lax.axis_index("shard").astype(jnp.int32) % 2
    groups = [list(range(p, count, 2)) for p in range(2)]
    near = lax.all_to_all(
        jnp.broadcast_to(own[None], (count // 2,) + own.shape),
        "shard", 0, 0, axis_index_groups=groups, tiled=True,
    )
    even = jnp.arange(0, count, 2, dtype=jnp.int32)
    return near, jnp.concatenate([even + parity, even + 1 - parity])


def after(value, *others):
    return lax.optimization_barrier((value,) + others)[0]


def join_cores(keep, send):
    other = swap_cores(send)
    return (keep.astype(F32) + other.astype(F32)).astype(BF16)


def exchange_shards(joined):
    count = lax.axis_size("shard")
    rows, cols = joined.shape
    return lax.all_to_all(joined.reshape(count, rows // count, cols), "shard", 0, 0, tiled=True)


def finish_group(parts):
    mine = jnp.sum(parts.astype(F32), 0).astype(BF16)
    bit = 2
    while bit < lax.axis_size("rep"):
        other = lax.ppermute(mine, "rep", flip("rep", bit))
        mine = (mine.astype(F32) + other.astype(F32)).astype(BF16)
        bit *= 2
    return mine, swap_cores(mine)


def update_group(core, pair, state, outs, layer, at, cols):
    mine, other = pair
    spec = pl.BlockSpec((1, mine.shape[0], cols), lambda j: (layer, 0, at + j))
    shape = struct(state[0].shape, F32)
    given = list(outs) if outs is not None else []
    return pl.pallas_call(
        functools.partial(step_kernel, len(given)),
        grid=(2,),
        in_specs=[smem(), whole(mine.shape), whole(other.shape), spec, spec, spec]
        + [pl.BlockSpec(memory_space=pl.ANY)] * len(given),
        out_specs=[spec] * 4,
        out_shape=[shape] * 4,
        input_output_aliases={6 + i: i for i in range(len(given))},
        compiler_params=params(),
        cost_estimate=cost(1e6, 4e6, 0),
    )(core, mine, other, *state, *given)


def local(
    tokens, weights, vectors, moment_one, moment_two, vector_one, vector_two, images, cotangent
):
    count, seq, width = tokens.shape
    layers = weights.shape[0]
    core = lax.axis_index("rep") % 2
    core_arr = core.reshape(1).astype(jnp.int32)
    plan = Layers(core_arr, count, seq, width)
    packs = []
    for index in range(layers):
        low = weights[index].astype(BF16)
        turned = jnp.pad(vectors[index].T.astype(BF16), ((0, 0), (0, TILE - vectors.shape[1])))
        attn_pack = jnp.concatenate([low[:, : 3 * width], turned], 1)
        rest = low[:, 3 * width :]
        rest_pack = jnp.pad(rest, ((0, 0), (0, -rest.shape[1] % (2 * TILE))))
        packs.append((own_half(attn_pack, core), own_half(rest_pack, core)))
    attn_own, rest_own = packs[0]
    copies, rest_own = lax.optimization_barrier((spread(attn_own), rest_own))
    arrays, place = gather_direct(copies)
    near, near_place = near_permutes(rest_own)
    gathered = [[Weights(arrays, place, 0, attn_own.shape[1]), None]]
    stored = []
    x = tokens
    for index in range(layers):
        first, last = index == 0, index == layers - 1
        wq = gathered[index][0]
        far = lax.ppermute(near, "shard", flip("shard", 1)) if first else None
        others = [near]
        if not last:
            next_own = after(jnp.concatenate(packs[index + 1], 1), near)
            next_near, next_place = near_exchange(next_own)
        qkv, o, lse, vec, *xp = plan.attn_forward(x, wq, first, others if first else [])
        xp = xp[0] if first else x
        if first:
            held = [near, far, swap_cores(near), swap_cores(after(far, o))]
            gathered[0][1] = Weights(held, near_place, 0, rest_own.shape[1])
        if not last:
            near = after(next_near, o)
            far = lax.ppermute(near, "shard", flip("shard", 1))
            near_other = swap_cores(near)
        x1, act, slope, x = plan.mlp_forward(
            xp, o, gathered[index][1], vec, last, [] if last else [near]
        )
        if not last:
            held = [near, far, near_other, swap_cores(after(far, x1))]
            qhalf, half = (p.shape[1] for p in packs[index + 1])
            gathered.append(
                [Weights(held, next_place, 0, qhalf), Weights(held, next_place, qhalf, half)]
            )
        stored.append((xp, qkv, o, lse, vec, x1, act, slope))
    output = x
    g = cotangent
    state = (moment_one, moment_two, weights)
    groups = []
    before = []

    def send_group(keep, send):
        if groups:
            keep, send, groups[-1] = lax.optimization_barrier((keep, send, groups[-1]))
        joined = join_cores(keep, send)
        groups.append(exchange_shards(joined))
        return [joined]

    for index in reversed(range(layers)):
        first, last = index == 0, index == layers - 1
        wq, wr = gathered[index]
        xp, qkv, o, lse, vec, x1, act, slope = stored[index]
        gx1, keep, send = plan.mlp_backward(images, g, x1, act, slope, wr, vec, last, before)
        before = send_group(keep, send)
        g, keep, send = plan.attn_backward(gx1, xp, qkv, lse, o, wq, wr, vec, first, before)
        before = send_group(keep, send)
    outs = None
    vec_grads = [None] * layers
    for n, index in enumerate(reversed(range(layers))):
        pair_m = finish_group(groups[2 * n])
        pair_a = finish_group(groups[2 * n + 1])
        outs = update_group(core_arr, pair_m, state, outs, index, 1, FF)
        outs = update_group(core_arr, pair_a, state, outs, index, 0, 2 * width)
        tails = [
            jnp.where(core == 0, p[0][:, -TILE:], p[1][:, -TILE:]).astype(F32).T
            for p in (pair_a, pair_m)
        ]
        vec_grads[index] = jnp.concatenate([tails[0][:5], tails[1][:7]], 0)
    vector_grad = jnp.stack(vec_grads)
    weight_grad, moment_one_new, moment_two_new, update = outs
    vector_one_new, vector_two_new, vector_update = adamw(
        vector_grad, vector_one, vector_two, vectors
    )
    return (
        output,
        g,
        weight_grad,
        vector_grad,
        moment_one_new,
        moment_two_new,
        vector_one_new,
        vector_two_new,
        update,
        vector_update,
    )


def solution(mesh):
    in_specs = (
        P(("rep", "shard"), None, None),
        P(None, "shard", None),
        P(None, None, "shard"),
        P(None, "shard", None),
        P(None, "shard", None),
        P(None, None, "shard"),
        P(None, None, "shard"),
        P(("rep", "shard")),
        P(("rep", "shard"), None, None),
    )
    out_specs = (
        P(("rep", "shard"), None, None),
        P(("rep", "shard"), None, None),
        P(None, "shard", None),
        P(None, None, "shard"),
        P(None, "shard", None),
        P(None, "shard", None),
        P(None, None, "shard"),
        P(None, None, "shard"),
        P(None, "shard", None),
        P(None, None, "shard"),
    )
    return jax.shard_map(local, mesh=mesh, in_specs=in_specs, out_specs=out_specs, check_vma=False)
```

```python
import functools
import math

import jax
import jax.numpy as jnp
from jax import lax
from jax.experimental import pallas as pl
from jax.experimental.pallas import tpu as pltpu
from jax.sharding import PartitionSpec as P

HEAD = 64
FF = 1536
STEP = 10
PAIR = 2
TILE = 128
CHUNK = 768
NEG = -1e30
F32 = jnp.float32
BF16 = jnp.bfloat16
VMEM_LIMIT = 60 * 1024 * 1024


def dot(left, right):
    return jnp.dot(left, right, preferred_element_type=F32)


def dot_nt(left, right):
    return lax.dot_general(left, right, (((1,), (1,)), ((), ())), preferred_element_type=F32)


def dot_tn(left, right):
    return lax.dot_general(left, right, (((0,), (0,)), ((), ())), preferred_element_type=F32)


def norm(values):
    center = values - jnp.mean(values, -1, keepdims=True)
    scale = lax.rsqrt(jnp.mean(center * center, -1, keepdims=True) + 1e-06)
    return center * scale, scale


def norm_back(grad, normed, scale, gain):
    inner = grad * gain
    return scale * (
        inner
        - jnp.mean(inner, -1, keepdims=True)
        - normed * jnp.mean(inner * normed, -1, keepdims=True)
    )


def gelu_parts(u):
    phi = 0.5 + 0.5 * lax.erf(u * math.sqrt(0.5))
    slope = phi + u * (jnp.exp2((u * u) * (-0.5 * math.log2(math.e))) * (1.0 / math.sqrt(2.0 * math.pi)))
    return u * phi, slope


def bias_up(vec_ref, width):
    return jnp.concatenate([vec_ref[8 + j : 9 + j, :] for j in range(FF // width)], 1)


def weight_copies(core_ref, place_ref, sources, start, whole_ref, sems):
    half = whole_ref.shape[1] // 2
    per_core = len(sources) // 2
    copies = []
    for n, source in enumerate(sources):
        at = core_ref[0] if n < per_core else 1 - core_ref[0]
        cols = pl.ds(pl.multiple_of(at * half, TILE), half)
        base = sum(piece.shape[0] for piece in sources[: n % per_core])
        copies += row_copies(
            place_ref, source, base, slice(start, start + half), whole_ref, cols, sems, len(copies)
        )
    return copies


def load_weights(*args):
    copies = weight_copies(*args)
    for copy in copies:
        copy.start()
    for copy in copies:
        copy.wait()


def load_first(core_ref, place_ref, sources, start, whole_ref, sems):
    per_core = len(sources) // 2
    size = whole_ref.shape[1]

    def load(chosen):
        copies = []
        for n, source in enumerate(chosen):
            copies += row_copies(
                place_ref, source, len(copies), slice(start, start + size), whole_ref, slice(0, size), sems,
                len(copies),
            )
        for copy in copies:
            copy.start()
        for copy in copies:
            copy.wait()

    @pl.when(core_ref[0] == 0)
    def _():
        load(sources[:per_core])

    @pl.when(core_ref[0] != 0)
    def _():
        load(sources[per_core:])


def row_copies(place_ref, source, base, taken, whole_ref, cols, sems, at):
    count, rows = source.shape[:2]
    copies = []
    for k in range(count):
        row = pl.multiple_of(place_ref[base + k] * rows, rows)
        copies.append(
            pltpu.make_async_copy(
                source.at[k, :, taken], whole_ref.at[pl.ds(row, rows), cols], sems.at[at + k]
            )
        )
    return copies


def attn_forward(first, seq, rows, at, start, core_ref, place_ref, x_ref, *refs):
    sources, refs = refs[:at], refs[at:]
    if first:
        qkv_ref, o_ref, lse_ref, vec_ref, xp_ref, w_ref, sems = refs
    else:
        qkv_ref, o_ref, lse_ref, vec_ref, w_ref, sems = refs
        xp_ref = x_ref
    width = o_ref.shape[1]
    heads = width // HEAD

    @pl.when(pl.program_id(0) == 0)
    def _():
        load_weights(core_ref, place_ref, sources, start, w_ref, sems)
        turned = w_ref[:, 3 * width : 3 * width + TILE].astype(F32).T
        vec_ref[...] = turned[: vec_ref.shape[0]]

    if first:
        for i in range(PAIR):
            xp_ref[i * rows : i * rows + seq, :] = x_ref[i].astype(F32)
            xp_ref[i * rows + seq : (i + 1) * rows, :] = jnp.zeros((rows - seq, width), F32)

    normed, _ = norm(xp_ref[...])
    hidden = (normed * vec_ref[0:1, :] + vec_ref[1:2, :]).astype(BF16)
    qkv = dot(hidden, w_ref[:, : 3 * width])
    qkv_ref[:, :width] = ((qkv[:, :width] + vec_ref[2:3, :]) * 0.125).astype(BF16)
    qkv_ref[:, width : 2 * width] = qkv[:, width : 2 * width].astype(BF16)
    qkv_ref[:, 2 * width :] = (qkv[:, 2 * width :] + vec_ref[3:4, :]).astype(BF16)

    edge = seq // 16 * 16
    alive = lax.broadcasted_iota(jnp.int32, (rows - edge, rows), 0) < seq - edge
    left = lax.broadcasted_iota(jnp.int32, (rows, TILE), 1) < HEAD
    work = [(i, h) for i in range(PAIR) for h in range(heads)]

    def scores_of(i, h):
        span = slice(i * rows, (i + 1) * rows)
        tile = h * HEAD // TILE * TILE
        mine = left if h * HEAD == tile else ~left
        query = jnp.where(mine, qkv_ref[span, tile : tile + TILE], jnp.zeros((), BF16))
        return dot_nt(qkv_ref[span, width + tile : width + tile + TILE], query)

    def finish(i, h, probs, total):
        out = dot(turned_v[i][h * HEAD : (h + 1) * HEAD], probs) * (1.0 / total)
        outs[i].append(out.astype(BF16))
        if h == heads - 1:
            o_ref[i * rows : (i + 1) * rows, :] = jnp.concatenate(outs[i], 0).T

    outs = [[] for _ in range(PAIR)]
    turned_v = [qkv_ref[i * rows : (i + 1) * rows, 2 * width :].T for i in range(PAIR)]
    ahead = [scores_of(*item) for item in work[:4]]
    behind = []
    for n, (i, h) in enumerate(work):
        if n + 4 < len(work):
            ahead.append(scores_of(*work[n + 4]))
        scores = ahead.pop(0)
        low = scores[:edge]
        high = jnp.where(alive, scores[edge:], NEG)
        top = jnp.maximum(jnp.max(low, 0, keepdims=True), jnp.max(high, 0, keepdims=True))
        low = jnp.exp(low - top)
        high = jnp.exp(high - top)
        total = jnp.sum(low, 0, keepdims=True) + jnp.sum(high, 0, keepdims=True)
        lse_ref[i, h : h + 1, :rows] = top + jnp.log(total)
        behind.append((i, h, jnp.concatenate([low.astype(BF16), high.astype(BF16)], 0), total))
        if len(behind) > 1:
            finish(*behind.pop(0))
    for item in behind:
        finish(*item)


def mlp_forward(last, seq, rows, at, start, core_ref, place_ref, x_ref, o_ref, vec_ref, *refs):
    sources, refs = refs[:at], refs[at:]
    x1_ref, act_ref, slope_ref, out_ref, w_ref, sems = refs
    width = x_ref.shape[1]

    if at:

        @pl.when(pl.program_id(0) == 0)
        def _():
            load_weights(core_ref, place_ref, sources, start, w_ref, sems)

    x1 = x_ref[...] + dot(o_ref[...], w_ref[:, :width]) + vec_ref[4:5, :]
    x1_ref[...] = x1
    normed, _ = norm(x1)
    hidden = (normed * vec_ref[5:6, :] + vec_ref[6:7, :]).astype(BF16)
    bias = bias_up(vec_ref, width)
    units = [(r, j) for r in range(0, x1.shape[0], x1.shape[0]) for j in range(0, FF, CHUNK)]
    size = x1.shape[0]

    def up(r, j):
        return dot(hidden[r : r + size], w_ref[:, width + j : width + j + CHUNK])

    totals = {r: x1[r : r + size] + vec_ref[7:8, :] for r, _ in units}

    def down(r, j, act):
        start = width + FF + j
        totals[r] = totals[r] + dot_nt(act, w_ref[:, start : start + CHUNK])

    ahead = up(*units[0])
    behind = None
    for n, (r, j) in enumerate(units):
        u = ahead
        if n + 1 < len(units):
            ahead = up(*units[n + 1])
        if behind is not None:
            down(*behind)
        acts = []
        for k in range(0, size, 16):
            act, slope = gelu_parts(u[k : k + 16] + bias[:, j : j + CHUNK])
            slope_ref[r + k : r + k + 16, j : j + CHUNK] = slope
            acts.append(act.astype(BF16))
        act = jnp.concatenate(acts, 0)
        act_ref[r : r + size, j : j + CHUNK] = act
        behind = (r, j, act)
    down(*behind)
    total = jnp.concatenate([totals[r] for r in sorted(totals)], 0)
    if last:
        for i in range(PAIR):
            out_ref[i] = total[i * rows : i * rows + seq]
    else:
        out_ref[...] = total


def put_grads(core, first_of, second_of, keep_ref, send_ref):
    @pl.when(core == 0)
    def _():
        first_of(keep_ref)
        second_of(send_ref)

    @pl.when(core != 0)
    def _():
        first_of(send_ref)
        second_of(keep_ref)


def put_vectors(acc_ref, ref):
    size = acc_ref.shape[0]
    padded = jnp.concatenate(
        [acc_ref[...], jnp.zeros((TILE - size, acc_ref.shape[1]), F32)], 0
    )
    ref[:, ref.shape[1] - TILE :] = padded.T.astype(BF16)


def column_sum(values):
    return jnp.sum(values, 0, keepdims=True)


def mlp_backward(
    last, seq, rows, at, start, core_ref, place_ref, live_ref, g_ref, x1_ref, act_ref, slope_ref, vec_ref, *refs
):
    sources, refs = refs[:at], refs[at:]
    gx1_ref, keep_ref, send_ref, w_ref, up_ref, down_ref, acc_ref, bias_ref, gp_ref, sems = refs
    width = x1_ref.shape[1]
    step = pl.program_id(0)

    if at:

        @pl.when(step == 0)
        def _():
            load_weights(core_ref, place_ref, sources, start, w_ref, sems)
            for ref in (up_ref, down_ref, acc_ref, bias_ref):
                ref[...] = jnp.zeros_like(ref)

    if last:
        for i in range(PAIR):
            keep = (step * PAIR + i < live_ref[0]).astype(F32)
            gp_ref[i * rows : i * rows + seq, :] = g_ref[i].astype(F32) * keep
            gp_ref[i * rows + seq : (i + 1) * rows, :] = jnp.zeros((rows - seq, width), F32)
        g = gp_ref[...]
    else:
        g = g_ref[...]
    low = g.astype(BF16)
    size = CHUNK

    def back(j):
        start = width + FF + j
        return dot(low, w_ref[:, start : start + size])

    ahead = back(0)
    turned = low.T
    normed, scale = norm(x1_ref[...])
    hidden = (normed * vec_ref[5:6, :] + vec_ref[6:7, :]).astype(BF16)
    turned_h = hidden.T
    acc_ref[2:3, :] += column_sum(g)
    total = None

    def finish(total, j, gu):
        up_ref[:, j : j + size] += dot(turned_h, gu)
        part = dot_nt(gu, w_ref[:, width + j : width + j + size])
        return part if total is None else total + part

    behind = None
    for j in range(0, FF, size):
        ga = ahead
        if j + size < FF:
            ahead = back(j + size)
        down_ref[:, j : j + size] += dot(turned, act_ref[:, j : j + size])
        if behind is not None:
            total = finish(total, *behind)
        gus = []
        sums = jnp.zeros((8, size), F32)
        for r in range(0, ga.shape[0], 16):
            gu = ga[r : r + 16].astype(BF16).astype(F32) * slope_ref[r : r + 16, j : j + size]
            sums = sums + gu[:8] + gu[8:]
            gus.append(gu.astype(BF16))
        bias_ref[:, j : j + size] += sums
        behind = (j, jnp.concatenate(gus, 0))
    total = finish(total, *behind)
    gh2 = total.astype(BF16).astype(F32)
    acc_ref[0:1, :] += column_sum(gh2 * normed)
    acc_ref[1:2, :] += column_sum(gh2)
    gx1_ref[...] = g + norm_back(gh2, normed, scale, vec_ref[5:6, :])

    @pl.when(step == pl.num_programs(0) - 1)
    def _():
        sums = column_sum(bias_ref[...])
        for j in range(FF // width):
            acc_ref[3 + j : 4 + j, :] = sums[:, j * width : (j + 1) * width]

        def up(ref):
            ref[:, :FF] = up_ref[...].astype(BF16)
            put_vectors(acc_ref, ref)

        def down(ref):
            ref[:, :FF] = down_ref[...].astype(BF16)
            ref[:, FF:] = jnp.zeros((width, TILE), BF16)

        put_grads(core_ref[0], up, down, keep_ref, send_ref)


def last_layer(seq, rows, at, starts, core_ref, place_ref, live_ref, x_ref, g_ref, *refs):
    sources, refs = refs[:at], refs[at:]
    (qkv_ref, o_ref, lse_ref, vec_ref, out_ref, gx1_ref, keep_ref, send_ref,
     wq_ref, wr_ref, x1_ref, act_ref, slope_ref, up_ref, down_ref, acc_ref, bias_ref, gp_ref, sems, rsems) = refs
    step = pl.program_id(0)
    copies = weight_copies(core_ref, place_ref, sources, starts[1], wr_ref, rsems)

    @pl.when(step == 0)
    def _():
        for copy in copies:
            copy.start()
        for ref in (up_ref, down_ref, acc_ref, bias_ref):
            ref[...] = jnp.zeros_like(ref)

    attn_forward(
        False, seq, rows, at, starts[0], core_ref, place_ref, x_ref, *sources,
        qkv_ref, o_ref, lse_ref, vec_ref, wq_ref, sems,
    )

    @pl.when(step == 0)
    def _():
        for copy in copies:
            copy.wait()

    mlp_forward(
        True, seq, rows, 0, 0, core_ref, place_ref, x_ref, o_ref, vec_ref,
        x1_ref, act_ref, slope_ref, out_ref, wr_ref, rsems,
    )
    mlp_backward(
        True, seq, rows, 0, 0, core_ref, place_ref, live_ref, g_ref, x1_ref, act_ref, slope_ref, vec_ref,
        gx1_ref, keep_ref, send_ref, wr_ref, up_ref, down_ref, acc_ref, bias_ref, gp_ref, rsems,
    )


def attn_backward(
    first, seq, rows, ats, starts, core_ref, qplace_ref, place_ref, g_ref, x_ref, qkv_ref, lse_ref, o_ref,
    vec_ref, *refs
):
    qsources, refs = refs[: ats[0]], refs[ats[0] :]
    sources, refs = refs[: ats[1]], refs[ats[1] :]
    gx_ref, keep_ref, send_ref, w_ref, wout_ref, gw_ref, gout_ref, acc_ref, gqkv_ref, go_ref, sems, osems = refs
    width = x_ref.shape[1]
    heads = width // HEAD
    step = pl.program_id(0)

    @pl.when(step == 0)
    def _():
        load_weights(core_ref, qplace_ref, qsources, starts[0], w_ref, sems)
        load_first(core_ref, place_ref, sources, starts[1], wout_ref, osems)
        gw_ref[...] = jnp.zeros_like(gw_ref)
        gout_ref[...] = jnp.zeros_like(gout_ref)
        acc_ref[...] = jnp.zeros_like(acc_ref)

    low = g_ref[...].astype(BF16)
    gout_ref[...] += dot(o_ref[...].T, low)
    acc_ref[4:5, :] += column_sum(g_ref[...])
    go_ref[...] = dot_nt(low, wout_ref[...]).astype(BF16)

    edge = seq // 16 * 16
    alive = lax.broadcasted_iota(jnp.int32, (rows - edge, rows), 0) < seq - edge
    left = lax.broadcasted_iota(jnp.int32, (rows, TILE), 1) < HEAD
    zero = jnp.zeros((), BF16)
    work = [(i, h) for i in range(PAIR) for h in range(heads)]

    def tile_of(ref, part, i, h):
        at = part * width + h * HEAD // TILE * TILE
        return ref[i * rows : (i + 1) * rows, at : at + TILE]

    def start(i, h):
        mine = left if h * HEAD % TILE == 0 else ~left
        query = jnp.where(mine, tile_of(qkv_ref, 0, i, h), zero)
        go = jnp.where(mine, tile_of(go_ref, 0, i, h), zero)
        return dot_nt(tile_of(qkv_ref, 1, i, h), query), dot_nt(tile_of(qkv_ref, 2, i, h), go)

    def finish(i, h, probs, gs):
        gvs[i].append(dot(probs, tile_of(go_ref, 0, i, h)))
        gks[i].append(dot(gs, tile_of(qkv_ref, 0, i, h)))
        gqs[i].append((dot(turned_k[i][h * HEAD : (h + 1) * HEAD], gs) * 0.125).astype(BF16))
        span = slice(i * rows, (i + 1) * rows)
        if h % 2:
            for part, held in ((1, gks[i]), (2, gvs[i])):
                at = part * width + h * HEAD // TILE * TILE
                gqkv_ref[span, at : at + TILE] = jnp.where(left, held[h - 1], held[h]).astype(BF16)
        if h == heads - 1:
            gqkv_ref[span, :width] = jnp.concatenate(gqs[i], 0).T

    gks, gvs, gqs = ([[] for _ in range(PAIR)] for _ in range(3))
    turned_k = [qkv_ref[i * rows : (i + 1) * rows, width : 2 * width].T for i in range(PAIR)]
    ahead = [start(*item) for item in work[:2]]
    behind = []
    for n, (i, h) in enumerate(work):
        if n + 2 < len(work):
            ahead.append(start(*work[n + 2]))
        scores, gp = ahead.pop(0)
        scores = scores - lse_ref[i, h : h + 1, :rows]
        p_low = jnp.exp(scores[:edge])
        p_high = jnp.where(alive, jnp.exp(scores[edge:]), 0.0)
        probs = jnp.concatenate([p_low.astype(BF16), p_high.astype(BF16)], 0)
        gp_low, gp_high = gp[:edge], gp[edge:]
        mean = column_sum(gp_low * p_low) + column_sum(gp_high * p_high)
        gs_low = (p_low * (gp_low - mean)).astype(BF16)
        gs_high = (p_high * (gp_high - mean)).astype(BF16)
        behind.append((i, h, probs, jnp.concatenate([gs_low, gs_high], 0)))
        if len(behind) > 1:
            finish(*behind.pop(0))
    for item in behind:
        finish(*item)

    normed, scale = norm(x_ref[...])
    hidden = (normed * vec_ref[0:1, :] + vec_ref[1:2, :]).astype(BF16)
    turned_h = hidden.T
    gqkv = gqkv_ref[...]
    gw_ref[...] += dot(turned_h, gqkv)
    total = dot_nt(gqkv, w_ref[:, : 3 * width])
    acc_ref[2:3, :] += column_sum(gqkv[:, :width].astype(F32))
    acc_ref[3:4, :] += column_sum(gqkv[:, 2 * width :].astype(F32))
    gh = total.astype(BF16).astype(F32)
    acc_ref[0:1, :] += column_sum(gh * normed)
    acc_ref[1:2, :] += column_sum(gh)
    gx = g_ref[...] + norm_back(gh, normed, scale, vec_ref[0:1, :])
    if first:
        for i in range(PAIR):
            gx_ref[i] = gx[i * rows : i * rows + seq]
    else:
        gx_ref[...] = gx

    @pl.when(step == pl.num_programs(0) - 1)
    def _():
        def one(ref):
            ref[:, : 2 * width] = gw_ref[:, : 2 * width].astype(BF16)
            put_vectors(acc_ref, ref)

        def two(ref):
            ref[:, :width] = gw_ref[:, 2 * width :].astype(BF16)
            ref[:, width : 2 * width] = gout_ref[...].astype(BF16)
            ref[:, 2 * width :] = jnp.zeros((width, TILE), BF16)

        put_grads(core_ref[0], one, two, keep_ref, send_ref)


def adamw(grad, first, second, old):
    first_new = 0.9 * first + 0.1 * grad
    second_new = 0.999 * second + 0.001 * grad * grad
    first_hat = first_new / (1.0 - 0.9**STEP)
    second_hat = second_new / (1.0 - 0.999**STEP)
    change = -0.01 * (first_hat / (jnp.sqrt(second_hat) + 1e-08) + 0.05 * old)
    return (first_new, second_new, change)


def step_kernel(start, core_ref, mine_ref, other_ref, one_ref, two_ref, old_ref, *refs):
    grad_ref, one_new_ref, two_new_ref, change_ref = refs[-4:]
    cols = slice(start, start + grad_ref.shape[2])

    def put(from_ref):
        grad = from_ref[:, cols].astype(F32)
        grad_ref[0] = grad
        one_new_ref[0], two_new_ref[0], change_ref[0] = adamw(grad, one_ref[0], two_ref[0], old_ref[0])

    @pl.when(core_ref[0] == pl.program_id(0))
    def _():
        put(mine_ref)

    @pl.when(core_ref[0] != pl.program_id(0))
    def _():
        put(other_ref)


def smem():
    return pl.BlockSpec(memory_space=pltpu.SMEM)


def whole(shape):
    zeros = (0,) * len(shape)
    return pl.BlockSpec(shape, lambda i: zeros)


def cost(flops, moved, exps):
    return pl.CostEstimate(flops=int(flops), bytes_accessed=int(moved), transcendentals=int(exps))


def params():
    return pltpu.CompilerParams(
        dimension_semantics=("arbitrary",), vmem_limit_bytes=VMEM_LIMIT
    )


def struct(shape, kind):
    return jax.ShapeDtypeStruct(shape, kind)


class Weights:
    def __init__(self, arrays, place, start, half):
        self.arrays, self.place, self.start, self.half = arrays, place, start, half

    def specs(self):
        return [pl.BlockSpec(memory_space=pl.ANY)] * len(self.arrays)

    def sems(self):
        return pltpu.SemaphoreType.DMA((sum(a.shape[0] for a in self.arrays),))


def call(kernel, after, in_specs, **rest):
    count = len(after)

    def run(*refs):
        kernel(*refs[count:])

    made = pl.pallas_call(
        run, in_specs=[pl.BlockSpec(memory_space=pl.ANY)] * count + in_specs, **rest
    )
    return lambda *args: made(*after, *args)


class Layers:
    def __init__(self, core, images, seq, width):
        self.core, self.images, self.seq, self.width = core, images, seq, width
        self.rows = -(-seq // 16) * 16
        self.grid = (images // PAIR,)
        self.total = images * self.rows
        self.block = PAIR * self.rows

    def tall(self, cols):
        return pl.BlockSpec((self.block, cols), lambda i: (i, 0))

    def images_spec(self):
        return pl.BlockSpec((PAIR, self.seq, self.width), lambda i: (i, 0, 0))

    def lse_spec(self):
        return pl.BlockSpec((PAIR, 8, 256), lambda i: (i, 0, 0))

    def attn_forward(self, x, wq, first, after):
        w, t = self.width, self.total
        outs = [
            (self.tall(3 * w), struct((t, 3 * w), BF16)),
            (self.tall(w), struct((t, w), BF16)),
            (self.lse_spec(), struct((self.images, 8, 256), F32)),
            (whole((16, w)), struct((16, w), F32)),
        ]
        if first:
            outs.append((self.tall(w), struct((t, w), F32)))
        return call(
            functools.partial(attn_forward, first, self.seq, self.rows, len(wq.arrays), wq.start),
            after,
            [smem(), smem(), self.images_spec() if first else self.tall(w)] + wq.specs(),
            grid=self.grid,
            out_specs=[o[0] for o in outs],
            out_shape=[o[1] for o in outs],
            scratch_shapes=[pltpu.VMEM((w, 2 * wq.half), BF16), wq.sems()],
            compiler_params=params(),
            cost_estimate=cost(1.7e10, 2e7, 3e6),
        )(self.core, wq.place, x, *wq.arrays)

    def mlp_forward(self, x, o, wr, vec, last, after):
        w, t = self.width, self.total
        outs = [
            (self.tall(w), struct((t, w), F32)),
            (self.tall(FF), struct((t, FF), BF16)),
            (self.tall(FF), struct((t, FF), F32)),
            (self.images_spec(), struct((self.images, self.seq, w), F32))
            if last
            else (self.tall(w), struct((t, w), F32)),
        ]
        return call(
            functools.partial(mlp_forward, last, self.seq, self.rows, len(wr.arrays), wr.start),
            after,
            [smem(), smem(), self.tall(w), self.tall(w), whole(vec.shape)] + wr.specs(),
            grid=self.grid,
            out_specs=[o[0] for o in outs],
            out_shape=[o[1] for o in outs],
            scratch_shapes=[pltpu.VMEM((w, 2 * wr.half), BF16), wr.sems()],
            compiler_params=params(),
            cost_estimate=cost(2.2e10, 3e7, 3e6),
        )(self.core, wr.place, x, o, vec, *wr.arrays)

    def mlp_backward(self, live, g, x1, act, slope, wr, vec, last, after):
        w, t = self.width, self.total
        return call(
            functools.partial(mlp_backward, last, self.seq, self.rows, len(wr.arrays), wr.start),
            after,
            [
                smem(), smem(), smem(),
                self.images_spec() if last else self.tall(w),
                self.tall(w), self.tall(FF), self.tall(FF), whole(vec.shape),
            ]
            + wr.specs(),
            grid=self.grid,
            out_specs=[self.tall(w), whole((w, FF + TILE)), whole((w, FF + TILE))],
            out_shape=[
                struct((t, w), F32), struct((w, FF + TILE), BF16), struct((w, FF + TILE), BF16),
            ],
            scratch_shapes=[
                pltpu.VMEM((w, 2 * wr.half), BF16),
                pltpu.VMEM((w, FF), F32),
                pltpu.VMEM((w, FF), F32),
                pltpu.VMEM((8, w), F32),
                pltpu.VMEM((8, FF), F32),
                pltpu.VMEM((self.block, w), F32),
                wr.sems(),
            ],
            compiler_params=params(),
            cost_estimate=cost(2.4e10, 3e7, 3e6),
        )(self.core, wr.place, live, g, x1, act, slope, vec, *wr.arrays)

    def last_layer(self, live, x, g, wq, wr):
        w, t = self.width, self.total
        outs = [
            (self.tall(3 * w), struct((t, 3 * w), BF16)),
            (self.tall(w), struct((t, w), BF16)),
            (self.lse_spec(), struct((self.images, 8, 256), F32)),
            (whole((16, w)), struct((16, w), F32)),
            (self.images_spec(), struct((self.images, self.seq, w), F32)),
            (self.tall(w), struct((t, w), F32)),
            (whole((w, FF + TILE)), struct((w, FF + TILE), BF16)),
            (whole((w, FF + TILE)), struct((w, FF + TILE), BF16)),
        ]
        return call(
            functools.partial(last_layer, self.seq, self.rows, len(wq.arrays), (wq.start, wr.start)),
            [],
            [smem(), smem(), smem(), self.tall(w), self.images_spec()] + wq.specs(),
            grid=self.grid,
            out_specs=[o[0] for o in outs],
            out_shape=[o[1] for o in outs],
            scratch_shapes=[
                pltpu.VMEM((w, 2 * wq.half), BF16),
                pltpu.VMEM((w, 2 * wr.half), BF16),
                pltpu.VMEM((self.block, w), F32),
                pltpu.VMEM((self.block, FF), BF16),
                pltpu.VMEM((self.block, FF), F32),
                pltpu.VMEM((w, FF), F32),
                pltpu.VMEM((w, FF), F32),
                pltpu.VMEM((8, w), F32),
                pltpu.VMEM((8, FF), F32),
                pltpu.VMEM((self.block, w), F32),
                wq.sems(),
                wr.sems(),
            ],
            compiler_params=params(),
            cost_estimate=cost(4.5e10, 3e7, 3e6),
        )(self.core, wq.place, live, x, g, *wq.arrays)

    def attn_backward(self, g, x, qkv, lse, o, wq, wr, vec, first, after):
        w, t = self.width, self.total
        return call(
            functools.partial(
                attn_backward, first, self.seq, self.rows,
                (len(wq.arrays), len(wr.arrays)), (wq.start, wr.start),
            ),
            after,
            [
                smem(), smem(), smem(), self.tall(w), self.tall(w), self.tall(3 * w),
                self.lse_spec(), self.tall(w), whole(vec.shape),
            ]
            + wq.specs()
            + wr.specs(),
            grid=self.grid,
            out_specs=[
                self.images_spec() if first else self.tall(w),
                whole((w, 2 * w + TILE)), whole((w, 2 * w + TILE)),
            ],
            out_shape=[
                struct((self.images, self.seq, w), F32) if first else struct((t, w), F32),
                struct((w, 2 * w + TILE), BF16), struct((w, 2 * w + TILE), BF16),
            ],
            scratch_shapes=[
                pltpu.VMEM((w, 2 * wq.half), BF16),
                pltpu.VMEM((w, w), BF16),
                pltpu.VMEM((w, 3 * w), F32),
                pltpu.VMEM((w, w), F32),
                pltpu.VMEM((8, w), F32),
                pltpu.VMEM((self.block, 3 * w), BF16),
                pltpu.VMEM((self.block, w), BF16),
                wq.sems(),
                wr.sems(),
            ],
            compiler_params=params(),
            cost_estimate=cost(3e10, 2e7, 3e6),
        )(self.core, wq.place, wr.place, g, x, qkv, lse, o, vec, *wq.arrays, *wr.arrays)


def flip(axis, bit):
    return [(i, i ^ bit) for i in range(lax.axis_size(axis))]


def swap_cores(value):
    return lax.ppermute(value, "rep", flip("rep", 1))


def own_half(packed, core):
    half = packed.shape[1] // 2
    return lax.dynamic_slice_in_dim(packed, core * half, half, 1)


def spread(own):
    return jnp.broadcast_to(own[None], (lax.axis_size("shard"),) + own.shape)


def gather_direct(copies):
    mine = lax.all_to_all(copies, "shard", 0, 0, tiled=True)
    return [mine, swap_cores(mine)], jnp.arange(copies.shape[0], dtype=jnp.int32)


class Gathering:
    def __init__(self, own):
        self.near = [own[None]]
        self.far = [self.neighbour(self.near[0])]
        self.ids = [0]

    @staticmethod
    def neighbour(piece):
        return lax.ppermute(piece, "shard", flip("shard", 1))

    def step(self, bit, anchor=None):
        have = self.near[0] if len(self.near) == 1 else jnp.concatenate(self.near, 0)
        have = have if anchor is None else after(have, anchor)
        self.near.append(lax.ppermute(have, "shard", flip("shard", bit)))
        self.ids += [i ^ bit for i in self.ids]

    def pass_on(self, *anchors):
        piece = after(self.near[-1], *anchors) if anchors else self.near[-1]
        self.far.append(self.neighbour(piece))

    def held(self, anchor=None):
        pieces = self.near + self.far
        if anchor is not None:
            pieces[-1] = after(pieces[-1], anchor)
        return pieces + [swap_cores(p) for p in pieces]

    def place(self):
        me = lax.axis_index("shard").astype(jnp.int32)
        return me ^ jnp.array(self.ids + [i ^ 1 for i in self.ids], jnp.int32)


def after(value, *others):
    return lax.optimization_barrier((value,) + others)[0]


def turn_kernel(in_ref, out_ref):
    for i in range(in_ref.shape[0]):
        out_ref[:, i, :] = in_ref[i]


def turn_images(value):
    images, seq, width = value.shape
    return pl.pallas_call(
        turn_kernel,
        grid=(width // TILE,),
        in_specs=[pl.BlockSpec((images, seq, TILE), lambda i: (0, 0, i))],
        out_specs=pl.BlockSpec((seq, images, TILE), lambda i: (0, 0, i)),
        out_shape=struct((seq, images, width), value.dtype),
        compiler_params=params(),
        cost_estimate=cost(1e6, 5e6, 0),
    )(value)


def join_cores(keep, send):
    other = swap_cores(send)
    return (keep.astype(F32) + other.astype(F32)).astype(BF16)


def exchange_shards(joined):
    count = lax.axis_size("shard")
    rows, cols = joined.shape
    return lax.all_to_all(joined.reshape(count, rows // count, cols), "shard", 0, 0, tiled=True)


def finish_groups(groups):
    mine = jnp.concatenate([jnp.sum(parts.astype(F32), 0).astype(BF16) for parts in groups], 1)
    bit = 2
    while bit < lax.axis_size("rep"):
        other = lax.ppermute(mine, "rep", flip("rep", bit))
        mine = (mine.astype(F32) + other.astype(F32)).astype(BF16)
        bit *= 2
    return mine, swap_cores(mine)


def update_group(core, pair, start, state, outs, layer, at, cols):
    mine, other = pair
    spec = pl.BlockSpec((1, mine.shape[0], cols), lambda j: (layer, 0, at + j))
    shape = struct(state[0].shape, F32)
    given = list(outs) if outs is not None else []
    return pl.pallas_call(
        functools.partial(step_kernel, start),
        grid=(2,),
        in_specs=[smem(), whole(mine.shape), whole(other.shape), spec, spec, spec]
        + [pl.BlockSpec(memory_space=pl.ANY)] * len(given),
        out_specs=[spec] * 4,
        out_shape=[shape] * 4,
        input_output_aliases={6 + i: i for i in range(len(given))},
        compiler_params=params(),
        cost_estimate=cost(1e6, 4e6, 0),
    )(core, mine, other, *state, *given)


def local(
    tokens, weights, vectors, moment_one, moment_two, vector_one, vector_two, images, cotangent
):
    count, seq, width = tokens.shape
    layers = weights.shape[0]
    core = lax.axis_index("rep") % 2
    core_arr = core.reshape(1).astype(jnp.int32)
    plan = Layers(core_arr, count, seq, width)
    packs = []
    for index in range(layers):
        low = weights[index].astype(BF16)
        turned = jnp.pad(vectors[index].T.astype(BF16), ((0, 0), (0, TILE - vectors.shape[1])))
        attn_pack = jnp.concatenate([low[:, : 3 * width], turned], 1)
        rest = low[:, 3 * width :]
        rest_pack = jnp.pad(rest, ((0, 0), (0, -rest.shape[1] % (2 * TILE))))
        packs.append((own_half(attn_pack, core), own_half(rest_pack, core)))
    bits = []
    bit = lax.axis_size("shard") // 2
    while bit > 1:
        bits.append(bit)
        bit //= 2
    attn_own, rest_own = packs[0]
    copies, rest_own = lax.optimization_barrier((spread(attn_own), rest_own))
    arrays, place = gather_direct(copies)
    rest = Gathering(rest_own)
    for bit in bits:
        rest.step(bit)
        if bit != bits[-1]:
            rest.pass_on()
    gathered = [[Weights(arrays, place, 0, attn_own.shape[1]), None]]
    stored = []
    x = tokens
    for index in range(layers):
        first, last = index == 0, index == layers - 1
        if not last:
            ahead = Gathering(after(jnp.concatenate(packs[index + 1], 1), rest.near[1]))
            for bit in bits[:-1]:
                ahead.step(bit)
        if last and not first:
            qkv, o, lse, vec, output, *tail = plan.last_layer(images, x, cotangent, *gathered[index])
            stored.append((x, qkv, o, lse, vec, None, None, None))
            break
        qkv, o, lse, vec, *xp = plan.attn_forward(
            x, gathered[index][0], first, [rest.near[1]] if first else []
        )
        xp = xp[0] if first else x
        if first:
            rest.pass_on(o, rest.far[-1])
            gathered[0][1] = Weights(rest.held(o), rest.place(), 0, rest_own.shape[1])
        if not last:
            ahead.pass_on(o)
            ahead.step(bits[-1], o)
        x1, act, slope, x = plan.mlp_forward(
            xp, o, gathered[index][1], vec, last, [] if last else [ahead.near[-1]]
        )
        if not last:
            ahead.pass_on()
            held = ahead.held(x1)
            qhalf, half = (p.shape[1] for p in packs[index + 1])
            gathered.append(
                [Weights(held, ahead.place(), 0, qhalf), Weights(held, ahead.place(), qhalf, half)]
            )
        stored.append((xp, qkv, o, lse, vec, x1, act, slope))
    g = None
    state = (moment_one, moment_two, weights)
    outs, turned = None, None
    tails = {}

    def finish(done, outs):
        pair = finish_groups([parts for parts, _ in done])
        start = 0
        for _, spot in done:
            outs = update_group(core_arr, pair, start, state, outs, *spot)
            start += spot[2]
            mine, other = (p[:, start : start + TILE] for p in pair)
            tails[spot[:2]] = jnp.where(core == 0, mine, other).astype(F32).T
            start += TILE
        return outs

    groups, before = [], []
    for index in reversed(range(layers)):
        first, last = index == 0, index == layers - 1
        wq, wr = gathered[index]
        xp, qkv, o, lse, vec, x1, act, slope = stored[index]
        for half in range(2):
            if half == 0:
                gx1, keep, send = (
                    tail if last else plan.mlp_backward(images, g, x1, act, slope, wr, vec, last, before)
                )
                spot = (index, 1, FF)
            else:
                g, keep, send = plan.attn_backward(gx1, xp, qkv, lse, o, wq, wr, vec, first, before)
                spot = (index, 0, 2 * width)
                if last:
                    turned = turn_images(after(output, g))
                if first:
                    parts, at = groups.pop(0)
                    outs = finish([(after(parts, g), at)], outs)
            if groups:
                parts, at = groups[-1]
                keep, send, turned, outs, parts = lax.optimization_barrier((keep, send, turned, outs, parts))
                groups[-1] = parts, at
            joined = join_cores(keep, send)
            before = [joined]
            groups.append((exchange_shards(joined), spot))
    output = turned.swapaxes(0, 1)
    outs = finish(groups[:-1], outs)
    parts, spot = groups[-1]
    parts, outs = lax.optimization_barrier((parts, outs))
    outs = finish([(parts, spot)], outs)
    vec_grads = [
        jnp.concatenate([tails[index, 0][:5], tails[index, 1][:7]], 0) for index in range(layers)
    ]
    vector_grad = jnp.stack(vec_grads)
    weight_grad, moment_one_new, moment_two_new, update = outs
    vector_one_new, vector_two_new, vector_update = adamw(
        vector_grad, vector_one, vector_two, vectors
    )
    return (
        output,
        g,
        weight_grad,
        vector_grad,
        moment_one_new,
        moment_two_new,
        vector_one_new,
        vector_two_new,
        update,
        vector_update,
    )


def solution(mesh):
    in_specs = (
        P(("rep", "shard"), None, None),
        P(None, "shard", None),
        P(None, None, "shard"),
        P(None, "shard", None),
        P(None, "shard", None),
        P(None, None, "shard"),
        P(None, None, "shard"),
        P(("rep", "shard")),
        P(("rep", "shard"), None, None),
    )
    out_specs = (
        P(("rep", "shard"), None, None),
        P(("rep", "shard"), None, None),
        P(None, "shard", None),
        P(None, None, "shard"),
        P(None, "shard", None),
        P(None, "shard", None),
        P(None, None, "shard"),
        P(None, None, "shard"),
        P(None, "shard", None),
        P(None, None, "shard"),
    )
    return jax.shard_map(local, mesh=mesh, in_specs=in_specs, out_specs=out_specs, check_vma=False)
```

```python
import functools
import math

import jax
import jax.numpy as jnp
from jax import lax
from jax.experimental import pallas as pl
from jax.experimental.pallas import tpu as pltpu
from jax.sharding import PartitionSpec as P

HEAD = 64
FF = 1536
STEP = 10
PAIR = 2
TILE = 128
CHUNK = 768
NEG = -1e30
F32 = jnp.float32
BF16 = jnp.bfloat16
VMEM_LIMIT = 60 * 1024 * 1024


def dot(left, right):
    return jnp.dot(left, right, preferred_element_type=F32)


def dot_nt(left, right):
    return lax.dot_general(left, right, (((1,), (1,)), ((), ())), preferred_element_type=F32)


def dot_tn(left, right):
    return lax.dot_general(left, right, (((0,), (0,)), ((), ())), preferred_element_type=F32)


def norm(values):
    center = values - jnp.mean(values, -1, keepdims=True)
    scale = lax.rsqrt(jnp.mean(center * center, -1, keepdims=True) + 1e-06)
    return center * scale, scale


def norm_back(grad, normed, scale, gain):
    inner = grad * gain
    return scale * (
        inner
        - jnp.mean(inner, -1, keepdims=True)
        - normed * jnp.mean(inner * normed, -1, keepdims=True)
    )


def gelu_parts(u):
    phi = 0.5 + 0.5 * lax.erf(u * math.sqrt(0.5))
    slope = phi + u * (jnp.exp2((u * u) * (-0.5 * math.log2(math.e))) * (1.0 / math.sqrt(2.0 * math.pi)))
    return u * phi, slope


def bias_up(vec_ref, width):
    return jnp.concatenate([vec_ref[8 + j : 9 + j, :] for j in range(FF // width)], 1)


def weight_copies(core_ref, place_ref, sources, start, whole_ref, sems):
    half = whole_ref.shape[1] // 2
    per_core = len(sources) // 2
    copies = []
    for n, source in enumerate(sources):
        at = core_ref[0] if n < per_core else 1 - core_ref[0]
        cols = pl.ds(pl.multiple_of(at * half, TILE), half)
        base = sum(piece.shape[0] for piece in sources[: n % per_core])
        copies += row_copies(
            place_ref, source, base, slice(start, start + half), whole_ref, cols, sems, len(copies)
        )
    return copies


def load_weights(*args):
    copies = weight_copies(*args)
    for copy in copies:
        copy.start()
    for copy in copies:
        copy.wait()


def load_first(core_ref, place_ref, sources, start, whole_ref, sems):
    per_core = len(sources) // 2
    size = whole_ref.shape[1]

    def load(chosen):
        copies = []
        for n, source in enumerate(chosen):
            copies += row_copies(
                place_ref, source, len(copies), slice(start, start + size), whole_ref, slice(0, size), sems,
                len(copies),
            )
        for copy in copies:
            copy.start()
        for copy in copies:
            copy.wait()

    @pl.when(core_ref[0] == 0)
    def _():
        load(sources[:per_core])

    @pl.when(core_ref[0] != 0)
    def _():
        load(sources[per_core:])


def row_copies(place_ref, source, base, taken, whole_ref, cols, sems, at):
    count, rows = source.shape[:2]
    copies = []
    for k in range(count):
        row = pl.multiple_of(place_ref[base + k] * rows, rows)
        copies.append(
            pltpu.make_async_copy(
                source.at[k, :, taken], whole_ref.at[pl.ds(row, rows), cols], sems.at[at + k]
            )
        )
    return copies


def attn_forward(first, seq, rows, at, start, core_ref, place_ref, x_ref, *refs):
    sources, refs = refs[:at], refs[at:]
    if first:
        qkv_ref, o_ref, lse_ref, vec_ref, xp_ref, w_ref, sems = refs
    else:
        qkv_ref, o_ref, lse_ref, vec_ref, w_ref, sems = refs
        xp_ref = x_ref
    width = o_ref.shape[1]
    heads = width // HEAD

    copies = weight_copies(core_ref, place_ref, sources, start, w_ref, sems)

    @pl.when(pl.program_id(0) == 0)
    def _():
        for copy in copies:
            copy.start()

    if first:
        for i in range(PAIR):
            xp_ref[i * rows : i * rows + seq, :] = x_ref[i].astype(F32)
            xp_ref[i * rows + seq : (i + 1) * rows, :] = jnp.zeros((rows - seq, width), F32)

    normed, _ = norm(xp_ref[...])

    @pl.when(pl.program_id(0) == 0)
    def _():
        for copy in copies:
            copy.wait()
        turned = w_ref[:, 3 * width : 3 * width + TILE].astype(F32).T
        vec_ref[...] = turned[: vec_ref.shape[0]]

    hidden = (normed * vec_ref[0:1, :] + vec_ref[1:2, :]).astype(BF16)
    qkv = dot(hidden, w_ref[:, : 3 * width])
    qkv_ref[:, :width] = ((qkv[:, :width] + vec_ref[2:3, :]) * 0.125).astype(BF16)
    qkv_ref[:, width : 2 * width] = qkv[:, width : 2 * width].astype(BF16)
    qkv_ref[:, 2 * width :] = (qkv[:, 2 * width :] + vec_ref[3:4, :]).astype(BF16)

    edge = seq // 16 * 16
    alive = lax.broadcasted_iota(jnp.int32, (rows - edge, rows), 0) < seq - edge
    left = lax.broadcasted_iota(jnp.int32, (rows, TILE), 1) < HEAD
    work = [(i, h) for i in range(PAIR) for h in range(heads)]

    def scores_of(i, h):
        span = slice(i * rows, (i + 1) * rows)
        tile = h * HEAD // TILE * TILE
        mine = left if h * HEAD == tile else ~left
        query = jnp.where(mine, qkv_ref[span, tile : tile + TILE], jnp.zeros((), BF16))
        return dot_nt(qkv_ref[span, width + tile : width + tile + TILE], query)

    def finish(i, h, probs, total):
        out = dot(turned_v[i][h * HEAD : (h + 1) * HEAD], probs) * (1.0 / total)
        outs[i].append(out.astype(BF16))
        if h == heads - 1:
            o_ref[i * rows : (i + 1) * rows, :] = jnp.concatenate(outs[i], 0).T

    outs = [[] for _ in range(PAIR)]
    turned_v = [qkv_ref[i * rows : (i + 1) * rows, 2 * width :].T for i in range(PAIR)]
    ahead = [scores_of(*item) for item in work[:4]]
    behind = []
    for n, (i, h) in enumerate(work):
        if n + 4 < len(work):
            ahead.append(scores_of(*work[n + 4]))
        scores = ahead.pop(0)
        low = scores[:edge]
        high = jnp.where(alive, scores[edge:], NEG)
        top = jnp.maximum(jnp.max(low, 0, keepdims=True), jnp.max(high, 0, keepdims=True))
        low = jnp.exp(low - top)
        high = jnp.exp(high - top)
        total = jnp.sum(low, 0, keepdims=True) + jnp.sum(high, 0, keepdims=True)
        lse_ref[i, h : h + 1, :rows] = top + jnp.log(total)
        behind.append((i, h, jnp.concatenate([low.astype(BF16), high.astype(BF16)], 0), total))
        if len(behind) > 1:
            finish(*behind.pop(0))
    for item in behind:
        finish(*item)


def mlp_forward(last, seq, rows, at, start, core_ref, place_ref, x_ref, o_ref, vec_ref, *refs):
    sources, refs = refs[:at], refs[at:]
    x1_ref, act_ref, slope_ref, out_ref, w_ref, sems = refs
    width = x_ref.shape[1]

    if at:

        @pl.when(pl.program_id(0) == 0)
        def _():
            load_weights(core_ref, place_ref, sources, start, w_ref, sems)

    x1 = x_ref[...] + dot(o_ref[...], w_ref[:, :width]) + vec_ref[4:5, :]
    x1_ref[...] = x1
    normed, _ = norm(x1)
    hidden = (normed * vec_ref[5:6, :] + vec_ref[6:7, :]).astype(BF16)
    bias = bias_up(vec_ref, width)
    units = [(r, j) for r in range(0, x1.shape[0], x1.shape[0]) for j in range(0, FF, CHUNK)]
    size = x1.shape[0]

    def up(r, j):
        return dot(hidden[r : r + size], w_ref[:, width + j : width + j + CHUNK])

    totals = {r: x1[r : r + size] + vec_ref[7:8, :] for r, _ in units}

    def down(r, j, act):
        start = width + FF + j
        totals[r] = totals[r] + dot_nt(act, w_ref[:, start : start + CHUNK])

    ahead = up(*units[0])
    behind = None
    for n, (r, j) in enumerate(units):
        u = ahead
        if n + 1 < len(units):
            ahead = up(*units[n + 1])
        if behind is not None:
            down(*behind)
        acts = []
        for k in range(0, size, 16):
            act, slope = gelu_parts(u[k : k + 16] + bias[:, j : j + CHUNK])
            slope_ref[r + k : r + k + 16, j : j + CHUNK] = slope
            acts.append(act.astype(BF16))
        act = jnp.concatenate(acts, 0)
        act_ref[r : r + size, j : j + CHUNK] = act
        behind = (r, j, act)
    down(*behind)
    total = jnp.concatenate([totals[r] for r in sorted(totals)], 0)
    if last:
        for i in range(PAIR):
            out_ref[i] = total[i * rows : i * rows + seq]
    else:
        out_ref[...] = total


def put_grads(core, first_of, second_of, keep_ref, send_ref):
    @pl.when(core == 0)
    def _():
        first_of(keep_ref)
        second_of(send_ref)

    @pl.when(core != 0)
    def _():
        first_of(send_ref)
        second_of(keep_ref)


def put_vectors(acc_ref, ref):
    size = acc_ref.shape[0]
    padded = jnp.concatenate(
        [acc_ref[...], jnp.zeros((TILE - size, acc_ref.shape[1]), F32)], 0
    )
    ref[:, ref.shape[1] - TILE :] = padded.T.astype(BF16)


def column_sum(values):
    return jnp.sum(values, 0, keepdims=True)


def mlp_backward(
    last, seq, rows, at, start, core_ref, place_ref, live_ref, g_ref, x1_ref, act_ref, slope_ref, vec_ref, *refs
):
    sources, refs = refs[:at], refs[at:]
    gx1_ref, keep_ref, send_ref, w_ref, up_ref, down_ref, acc_ref, bias_ref, gp_ref, sems = refs
    width = x1_ref.shape[1]
    step = pl.program_id(0)

    if at:

        @pl.when(step == 0)
        def _():
            load_weights(core_ref, place_ref, sources, start, w_ref, sems)
            for ref in (up_ref, down_ref, acc_ref, bias_ref):
                ref[...] = jnp.zeros_like(ref)

    if last:
        for i in range(PAIR):
            keep = (step * PAIR + i < live_ref[0]).astype(F32)
            gp_ref[i * rows : i * rows + seq, :] = g_ref[i].astype(F32) * keep
            gp_ref[i * rows + seq : (i + 1) * rows, :] = jnp.zeros((rows - seq, width), F32)
        g = gp_ref[...]
    else:
        g = g_ref[...]
    low = g.astype(BF16)
    size = CHUNK

    def back(j):
        start = width + FF + j
        return dot(low, w_ref[:, start : start + size])

    ahead = back(0)
    turned = low.T
    normed, scale = norm(x1_ref[...])
    hidden = (normed * vec_ref[5:6, :] + vec_ref[6:7, :]).astype(BF16)
    turned_h = hidden.T
    acc_ref[2:3, :] += column_sum(g)
    total = None

    def finish(total, j, gu):
        up_ref[:, j : j + size] += dot(turned_h, gu)
        part = dot_nt(gu, w_ref[:, width + j : width + j + size])
        return part if total is None else total + part

    behind = None
    for j in range(0, FF, size):
        ga = ahead
        if j + size < FF:
            ahead = back(j + size)
        down_ref[:, j : j + size] += dot(turned, act_ref[:, j : j + size])
        if behind is not None:
            total = finish(total, *behind)
        gus = []
        sums = jnp.zeros((8, size), F32)
        for r in range(0, ga.shape[0], 16):
            gu = ga[r : r + 16].astype(BF16).astype(F32) * slope_ref[r : r + 16, j : j + size]
            sums = sums + gu[:8] + gu[8:]
            gus.append(gu.astype(BF16))
        bias_ref[:, j : j + size] += sums
        behind = (j, jnp.concatenate(gus, 0))
    total = finish(total, *behind)
    gh2 = total.astype(BF16).astype(F32)
    acc_ref[0:1, :] += column_sum(gh2 * normed)
    acc_ref[1:2, :] += column_sum(gh2)
    gx1_ref[...] = g + norm_back(gh2, normed, scale, vec_ref[5:6, :])

    @pl.when(step == pl.num_programs(0) - 1)
    def _():
        sums = column_sum(bias_ref[...])
        for j in range(FF // width):
            acc_ref[3 + j : 4 + j, :] = sums[:, j * width : (j + 1) * width]

        def up(ref):
            ref[:, :FF] = up_ref[...].astype(BF16)
            put_vectors(acc_ref, ref)

        def down(ref):
            ref[:, :FF] = down_ref[...].astype(BF16)
            ref[:, FF:] = jnp.zeros((width, TILE), BF16)

        put_grads(core_ref[0], up, down, keep_ref, send_ref)


def last_layer(seq, rows, at, starts, core_ref, place_ref, live_ref, x_ref, g_ref, *refs):
    sources, refs = refs[:at], refs[at:]
    (qkv_ref, o_ref, lse_ref, vec_ref, out_ref, gx1_ref, keep_ref, send_ref,
     wq_ref, wr_ref, x1_ref, act_ref, slope_ref, up_ref, down_ref, acc_ref, bias_ref, gp_ref, sems, rsems) = refs
    step = pl.program_id(0)
    copies = weight_copies(core_ref, place_ref, sources, starts[1], wr_ref, rsems)

    @pl.when(step == 0)
    def _():
        for copy in copies:
            copy.start()
        for ref in (up_ref, down_ref, acc_ref, bias_ref):
            ref[...] = jnp.zeros_like(ref)

    attn_forward(
        False, seq, rows, at, starts[0], core_ref, place_ref, x_ref, *sources,
        qkv_ref, o_ref, lse_ref, vec_ref, wq_ref, sems,
    )

    @pl.when(step == 0)
    def _():
        for copy in copies:
            copy.wait()

    mlp_forward(
        True, seq, rows, 0, 0, core_ref, place_ref, x_ref, o_ref, vec_ref,
        x1_ref, act_ref, slope_ref, out_ref, wr_ref, rsems,
    )
    mlp_backward(
        True, seq, rows, 0, 0, core_ref, place_ref, live_ref, g_ref, x1_ref, act_ref, slope_ref, vec_ref,
        gx1_ref, keep_ref, send_ref, wr_ref, up_ref, down_ref, acc_ref, bias_ref, gp_ref, rsems,
    )


def attn_backward(
    first, seq, rows, ats, starts, core_ref, qplace_ref, place_ref, g_ref, x_ref, qkv_ref, lse_ref, o_ref,
    vec_ref, *refs
):
    qsources, refs = refs[: ats[0]], refs[ats[0] :]
    sources, refs = refs[: ats[1]], refs[ats[1] :]
    gx_ref, keep_ref, send_ref, w_ref, wout_ref, gw_ref, gout_ref, acc_ref, gqkv_ref, go_ref, sems, osems = refs
    width = x_ref.shape[1]
    heads = width // HEAD
    step = pl.program_id(0)

    copies = weight_copies(core_ref, qplace_ref, qsources, starts[0], w_ref, sems)

    @pl.when(step == 0)
    def _():
        for copy in copies:
            copy.start()
        load_first(core_ref, place_ref, sources, starts[1], wout_ref, osems)
        for ref in (gw_ref, gout_ref, acc_ref):
            ref[...] = jnp.zeros_like(ref)

    low = g_ref[...].astype(BF16)
    go_ref[...] = dot_nt(low, wout_ref[...]).astype(BF16)

    @pl.when(step == 0)
    def _():
        for copy in copies:
            copy.wait()

    edge = seq // 16 * 16
    alive = lax.broadcasted_iota(jnp.int32, (rows - edge, rows), 0) < seq - edge
    left = lax.broadcasted_iota(jnp.int32, (rows, TILE), 1) < HEAD
    zero = jnp.zeros((), BF16)
    work = [(i, h) for i in range(PAIR) for h in range(heads)]

    def tile_of(ref, part, i, h):
        at = part * width + h * HEAD // TILE * TILE
        return ref[i * rows : (i + 1) * rows, at : at + TILE]

    def start(i, h):
        mine = left if h * HEAD % TILE == 0 else ~left
        query = jnp.where(mine, tile_of(qkv_ref, 0, i, h), zero)
        go = jnp.where(mine, tile_of(go_ref, 0, i, h), zero)
        return dot_nt(tile_of(qkv_ref, 1, i, h), query), dot_nt(tile_of(qkv_ref, 2, i, h), go)

    def finish(i, h, probs, gs):
        gvs[i].append(dot(probs, tile_of(go_ref, 0, i, h)))
        gks[i].append(dot(gs, tile_of(qkv_ref, 0, i, h)))
        gqs[i].append((dot(turned_k[i][h * HEAD : (h + 1) * HEAD], gs) * 0.125).astype(BF16))
        span = slice(i * rows, (i + 1) * rows)
        if h % 2:
            for part, held in ((1, gks[i]), (2, gvs[i])):
                at = part * width + h * HEAD // TILE * TILE
                gqkv_ref[span, at : at + TILE] = jnp.where(left, held[h - 1], held[h]).astype(BF16)
        if h == heads - 1:
            gqkv_ref[span, :width] = jnp.concatenate(gqs[i], 0).T

    def post(i):
        span = slice(i * rows, (i + 1) * rows)
        gqkv = gqkv_ref[span, :]
        gw_ref[...] += dot(turned_h[i], gqkv)
        gh = dot_nt(gqkv, w_ref[:, : 3 * width]).astype(BF16).astype(F32)
        acc_ref[2:3, :] += column_sum(gqkv[:, :width].astype(F32))
        acc_ref[3:4, :] += column_sum(gqkv[:, 2 * width :].astype(F32))
        acc_ref[0:1, :] += column_sum(gh * normed[i])
        acc_ref[1:2, :] += column_sum(gh)
        gx = g_ref[span, :] + norm_back(gh, normed[i], scale[i], vec_ref[0:1, :])
        if first:
            gx_ref[i] = gx[:seq]
        else:
            gx_ref[span, :] = gx

    gks, gvs, gqs = ([[] for _ in range(PAIR)] for _ in range(3))
    turned_k = [qkv_ref[i * rows : (i + 1) * rows, width : 2 * width].T for i in range(PAIR)]
    ahead = [start(*item) for item in work[:2]]
    normed, scale, turned_h = [], [], []
    for i in range(PAIR):
        part, size = norm(x_ref[i * rows : (i + 1) * rows, :])
        normed.append(part)
        scale.append(size)
        turned_h.append((part * vec_ref[0:1, :] + vec_ref[1:2, :]).astype(BF16).T)
    behind = []
    for n, (i, h) in enumerate(work):
        if n + 2 < len(work):
            ahead.append(start(*work[n + 2]))
        scores, gp = ahead.pop(0)
        scores = scores - lse_ref[i, h : h + 1, :rows]
        p_low = jnp.exp(scores[:edge])
        p_high = jnp.where(alive, jnp.exp(scores[edge:]), 0.0)
        probs = jnp.concatenate([p_low.astype(BF16), p_high.astype(BF16)], 0)
        gp_low, gp_high = gp[:edge], gp[edge:]
        mean = column_sum(gp_low * p_low) + column_sum(gp_high * p_high)
        gs_low = (p_low * (gp_low - mean)).astype(BF16)
        gs_high = (p_high * (gp_high - mean)).astype(BF16)
        behind.append((i, h, probs, jnp.concatenate([gs_low, gs_high], 0)))
        if len(behind) > 1:
            finish(*behind.pop(0))
    for item in behind:
        finish(*item)
    gout_ref[...] += dot(o_ref[...].T, low)
    acc_ref[4:5, :] += column_sum(g_ref[...])
    for i in range(PAIR):
        post(i)
    @pl.when(step == pl.num_programs(0) - 1)
    def _():
        def one(ref):
            ref[:, : 2 * width] = gw_ref[:, : 2 * width].astype(BF16)
            put_vectors(acc_ref, ref)

        def two(ref):
            ref[:, :width] = gw_ref[:, 2 * width :].astype(BF16)
            ref[:, width : 2 * width] = gout_ref[...].astype(BF16)
            ref[:, 2 * width :] = jnp.zeros((width, TILE), BF16)

        put_grads(core_ref[0], one, two, keep_ref, send_ref)


def adamw(grad, first, second, old):
    first_new = 0.9 * first + 0.1 * grad
    second_new = 0.999 * second + 0.001 * grad * grad
    first_hat = first_new / (1.0 - 0.9**STEP)
    second_hat = second_new / (1.0 - 0.999**STEP)
    change = -0.01 * (first_hat / (jnp.sqrt(second_hat) + 1e-08) + 0.05 * old)
    return (first_new, second_new, change)


def step_kernel(start, core_ref, mine_ref, other_ref, one_ref, two_ref, old_ref, *refs):
    grad_ref, one_new_ref, two_new_ref, change_ref = refs[-4:]
    cols = slice(start, start + grad_ref.shape[2])

    def put(from_ref):
        grad = from_ref[:, cols].astype(F32)
        grad_ref[0] = grad
        one_new_ref[0], two_new_ref[0], change_ref[0] = adamw(grad, one_ref[0], two_ref[0], old_ref[0])

    @pl.when(core_ref[0] == pl.program_id(0))
    def _():
        put(mine_ref)

    @pl.when(core_ref[0] != pl.program_id(0))
    def _():
        put(other_ref)


def smem():
    return pl.BlockSpec(memory_space=pltpu.SMEM)


def whole(shape):
    zeros = (0,) * len(shape)
    return pl.BlockSpec(shape, lambda i: zeros)


def cost(flops, moved, exps):
    return pl.CostEstimate(flops=int(flops), bytes_accessed=int(moved), transcendentals=int(exps))


def params():
    return pltpu.CompilerParams(
        dimension_semantics=("arbitrary",), vmem_limit_bytes=VMEM_LIMIT
    )


def struct(shape, kind):
    return jax.ShapeDtypeStruct(shape, kind)


class Weights:
    def __init__(self, arrays, place, start, half):
        self.arrays, self.place, self.start, self.half = arrays, place, start, half

    def specs(self):
        return [pl.BlockSpec(memory_space=pl.ANY)] * len(self.arrays)

    def sems(self):
        return pltpu.SemaphoreType.DMA((sum(a.shape[0] for a in self.arrays),))


def call(kernel, after, in_specs, **rest):
    count = len(after)

    def run(*refs):
        kernel(*refs[count:])

    made = pl.pallas_call(
        run, in_specs=[pl.BlockSpec(memory_space=pl.ANY)] * count + in_specs, **rest
    )
    return lambda *args: made(*after, *args)


class Layers:
    def __init__(self, core, images, seq, width):
        self.core, self.images, self.seq, self.width = core, images, seq, width
        self.rows = -(-seq // 16) * 16
        self.grid = (images // PAIR,)
        self.total = images * self.rows
        self.block = PAIR * self.rows

    def tall(self, cols):
        return pl.BlockSpec((self.block, cols), lambda i: (i, 0))

    def images_spec(self):
        return pl.BlockSpec((PAIR, self.seq, self.width), lambda i: (i, 0, 0))

    def lse_spec(self):
        return pl.BlockSpec((PAIR, 8, 256), lambda i: (i, 0, 0))

    def attn_forward(self, x, wq, first, after):
        w, t = self.width, self.total
        outs = [
            (self.tall(3 * w), struct((t, 3 * w), BF16)),
            (self.tall(w), struct((t, w), BF16)),
            (self.lse_spec(), struct((self.images, 8, 256), F32)),
            (whole((16, w)), struct((16, w), F32)),
        ]
        if first:
            outs.append((self.tall(w), struct((t, w), F32)))
        return call(
            functools.partial(attn_forward, first, self.seq, self.rows, len(wq.arrays), wq.start),
            after,
            [smem(), smem(), self.images_spec() if first else self.tall(w)] + wq.specs(),
            grid=self.grid,
            out_specs=[o[0] for o in outs],
            out_shape=[o[1] for o in outs],
            scratch_shapes=[pltpu.VMEM((w, 2 * wq.half), BF16), wq.sems()],
            compiler_params=params(),
            cost_estimate=cost(1.7e10, 2e7, 3e6),
        )(self.core, wq.place, x, *wq.arrays)

    def mlp_forward(self, x, o, wr, vec, last, after):
        w, t = self.width, self.total
        outs = [
            (self.tall(w), struct((t, w), F32)),
            (self.tall(FF), struct((t, FF), BF16)),
            (self.tall(FF), struct((t, FF), F32)),
            (self.images_spec(), struct((self.images, self.seq, w), F32))
            if last
            else (self.tall(w), struct((t, w), F32)),
        ]
        return call(
            functools.partial(mlp_forward, last, self.seq, self.rows, len(wr.arrays), wr.start),
            after,
            [smem(), smem(), self.tall(w), self.tall(w), whole(vec.shape)] + wr.specs(),
            grid=self.grid,
            out_specs=[o[0] for o in outs],
            out_shape=[o[1] for o in outs],
            scratch_shapes=[pltpu.VMEM((w, 2 * wr.half), BF16), wr.sems()],
            compiler_params=params(),
            cost_estimate=cost(2.2e10, 3e7, 3e6),
        )(self.core, wr.place, x, o, vec, *wr.arrays)

    def mlp_backward(self, live, g, x1, act, slope, wr, vec, last, after):
        w, t = self.width, self.total
        return call(
            functools.partial(mlp_backward, last, self.seq, self.rows, len(wr.arrays), wr.start),
            after,
            [
                smem(), smem(), smem(),
                self.images_spec() if last else self.tall(w),
                self.tall(w), self.tall(FF), self.tall(FF), whole(vec.shape),
            ]
            + wr.specs(),
            grid=self.grid,
            out_specs=[self.tall(w), whole((w, FF + TILE)), whole((w, FF + TILE))],
            out_shape=[
                struct((t, w), F32), struct((w, FF + TILE), BF16), struct((w, FF + TILE), BF16),
            ],
            scratch_shapes=[
                pltpu.VMEM((w, 2 * wr.half), BF16),
                pltpu.VMEM((w, FF), F32),
                pltpu.VMEM((w, FF), F32),
                pltpu.VMEM((8, w), F32),
                pltpu.VMEM((8, FF), F32),
                pltpu.VMEM((self.block, w), F32),
                wr.sems(),
            ],
            compiler_params=params(),
            cost_estimate=cost(2.4e10, 3e7, 3e6),
        )(self.core, wr.place, live, g, x1, act, slope, vec, *wr.arrays)

    def last_layer(self, live, x, g, wq, wr):
        w, t = self.width, self.total
        outs = [
            (self.tall(3 * w), struct((t, 3 * w), BF16)),
            (self.tall(w), struct((t, w), BF16)),
            (self.lse_spec(), struct((self.images, 8, 256), F32)),
            (whole((16, w)), struct((16, w), F32)),
            (self.images_spec(), struct((self.images, self.seq, w), F32)),
            (self.tall(w), struct((t, w), F32)),
            (whole((w, FF + TILE)), struct((w, FF + TILE), BF16)),
            (whole((w, FF + TILE)), struct((w, FF + TILE), BF16)),
        ]
        return call(
            functools.partial(last_layer, self.seq, self.rows, len(wq.arrays), (wq.start, wr.start)),
            [],
            [smem(), smem(), smem(), self.tall(w), self.images_spec()] + wq.specs(),
            grid=self.grid,
            out_specs=[o[0] for o in outs],
            out_shape=[o[1] for o in outs],
            scratch_shapes=[
                pltpu.VMEM((w, 2 * wq.half), BF16),
                pltpu.VMEM((w, 2 * wr.half), BF16),
                pltpu.VMEM((self.block, w), F32),
                pltpu.VMEM((self.block, FF), BF16),
                pltpu.VMEM((self.block, FF), F32),
                pltpu.VMEM((w, FF), F32),
                pltpu.VMEM((w, FF), F32),
                pltpu.VMEM((8, w), F32),
                pltpu.VMEM((8, FF), F32),
                pltpu.VMEM((self.block, w), F32),
                wq.sems(),
                wr.sems(),
            ],
            compiler_params=params(),
            cost_estimate=cost(4.5e10, 3e7, 3e6),
        )(self.core, wq.place, live, x, g, *wq.arrays)

    def attn_backward(self, g, x, qkv, lse, o, wq, wr, vec, first, after):
        w, t = self.width, self.total
        return call(
            functools.partial(
                attn_backward, first, self.seq, self.rows,
                (len(wq.arrays), len(wr.arrays)), (wq.start, wr.start),
            ),
            after,
            [
                smem(), smem(), smem(), self.tall(w), self.tall(w), self.tall(3 * w),
                self.lse_spec(), self.tall(w), whole(vec.shape),
            ]
            + wq.specs()
            + wr.specs(),
            grid=self.grid,
            out_specs=[
                self.images_spec() if first else self.tall(w),
                whole((w, 2 * w + TILE)), whole((w, 2 * w + TILE)),
            ],
            out_shape=[
                struct((self.images, self.seq, w), F32) if first else struct((t, w), F32),
                struct((w, 2 * w + TILE), BF16), struct((w, 2 * w + TILE), BF16),
            ],
            scratch_shapes=[
                pltpu.VMEM((w, 2 * wq.half), BF16),
                pltpu.VMEM((w, w), BF16),
                pltpu.VMEM((w, 3 * w), F32),
                pltpu.VMEM((w, w), F32),
                pltpu.VMEM((8, w), F32),
                pltpu.VMEM((self.block, 3 * w), BF16),
                pltpu.VMEM((self.block, w), BF16),
                wq.sems(),
                wr.sems(),
            ],
            compiler_params=params(),
            cost_estimate=cost(3e10, 2e7, 3e6),
        )(self.core, wq.place, wr.place, g, x, qkv, lse, o, vec, *wq.arrays, *wr.arrays)


def flip(axis, bit):
    return [(i, i ^ bit) for i in range(lax.axis_size(axis))]


def swap_cores(value):
    return lax.ppermute(value, "rep", flip("rep", 1))


def own_half(packed, core):
    half = packed.shape[1] // 2
    return lax.dynamic_slice_in_dim(packed, core * half, half, 1)


class Gathering:
    def __init__(self, own):
        self.near = [own[None]]
        self.far = [self.neighbour(self.near[0])]
        self.ids = [0]

    @staticmethod
    def neighbour(piece):
        return lax.ppermute(piece, "shard", flip("shard", 1))

    def step(self, bit, anchor=None):
        have = self.near[0] if len(self.near) == 1 else jnp.concatenate(self.near, 0)
        have = have if anchor is None else after(have, anchor)
        self.near.append(lax.ppermute(have, "shard", flip("shard", bit)))
        self.ids += [i ^ bit for i in self.ids]

    def pass_on(self, *anchors):
        piece = after(self.near[-1], *anchors) if anchors else self.near[-1]
        self.far.append(self.neighbour(piece))

    def held(self, anchor=None):
        pieces = self.near + self.far
        if anchor is not None:
            pieces[-1] = after(pieces[-1], anchor)
        return pieces + [swap_cores(p) for p in pieces]

    def place(self):
        me = lax.axis_index("shard").astype(jnp.int32)
        return me ^ jnp.array(self.ids + [i ^ 1 for i in self.ids], jnp.int32)


def after(value, *others):
    return lax.optimization_barrier((value,) + others)[0]


def turn_kernel(in_ref, out_ref):
    for i in range(in_ref.shape[0]):
        out_ref[:, i, :] = in_ref[i]


def turn_images(value):
    images, seq, width = value.shape
    return pl.pallas_call(
        turn_kernel,
        grid=(width // TILE,),
        in_specs=[pl.BlockSpec((images, seq, TILE), lambda i: (0, 0, i))],
        out_specs=pl.BlockSpec((seq, images, TILE), lambda i: (0, 0, i)),
        out_shape=struct((seq, images, width), value.dtype),
        compiler_params=params(),
        cost_estimate=cost(1e6, 5e6, 0),
    )(value)


def join_cores(keep, send):
    other = swap_cores(send)
    return (keep.astype(F32) + other.astype(F32)).astype(BF16)


def exchange_shards(joined):
    count = lax.axis_size("shard")
    rows, cols = joined.shape
    return lax.all_to_all(joined.reshape(count, rows // count, cols), "shard", 0, 0, tiled=True)


def finish_groups(groups):
    mine = jnp.concatenate([jnp.sum(parts.astype(F32), 0).astype(BF16) for parts in groups], 1)
    bit = 2
    while bit < lax.axis_size("rep"):
        other = lax.ppermute(mine, "rep", flip("rep", bit))
        mine = (mine.astype(F32) + other.astype(F32)).astype(BF16)
        bit *= 2
    return mine, swap_cores(mine)


def update_group(core, pair, start, state, outs, layer, at, cols):
    mine, other = pair
    spec = pl.BlockSpec((1, mine.shape[0], cols), lambda j: (layer, 0, at + j))
    shape = struct(state[0].shape, F32)
    given = list(outs) if outs is not None else []
    return pl.pallas_call(
        functools.partial(step_kernel, start),
        grid=(2,),
        in_specs=[smem(), whole(mine.shape), whole(other.shape), spec, spec, spec]
        + [pl.BlockSpec(memory_space=pl.ANY)] * len(given),
        out_specs=[spec] * 4,
        out_shape=[shape] * 4,
        input_output_aliases={6 + i: i for i in range(len(given))},
        compiler_params=params(),
        cost_estimate=cost(1e6, 4e6, 0),
    )(core, mine, other, *state, *given)


def local(
    tokens, weights, vectors, moment_one, moment_two, vector_one, vector_two, images, cotangent
):
    count, seq, width = tokens.shape
    layers = weights.shape[0]
    core = lax.axis_index("rep") % 2
    core_arr = core.reshape(1).astype(jnp.int32)
    plan = Layers(core_arr, count, seq, width)
    packs = []
    for index in range(layers):
        low = weights[index].astype(BF16)
        turned = jnp.pad(vectors[index].T.astype(BF16), ((0, 0), (0, TILE - vectors.shape[1])))
        attn_pack = jnp.concatenate([low[:, : 3 * width], turned], 1)
        rest = low[:, 3 * width :]
        rest_pack = jnp.pad(rest, ((0, 0), (0, -rest.shape[1] % (2 * TILE))))
        packs.append((own_half(attn_pack, core), own_half(rest_pack, core)))
    bits = []
    bit = lax.axis_size("shard") // 2
    while bit > 1:
        bits.append(bit)
        bit //= 2
    attn_own, rest_own = packs[0]
    query = Gathering(attn_own)
    for bit in bits:
        query.step(bit)
        query.pass_on()
    rest = Gathering(after(rest_own, query.near[1]))
    for bit in bits:
        rest.step(bit)
        if bit != bits[-1]:
            rest.pass_on()
    gathered = [[Weights(query.held(), query.place(), 0, attn_own.shape[1]), None]]
    stored = []
    x = tokens
    for index in range(layers):
        first, last = index == 0, index == layers - 1
        if not last:
            ahead = Gathering(after(jnp.concatenate(packs[index + 1], 1), rest.near[1]))
            for bit in bits[:-1]:
                ahead.step(bit)
        if last and not first:
            qkv, o, lse, vec, output, *tail = plan.last_layer(images, x, cotangent, *gathered[index])
            stored.append((x, qkv, o, lse, vec, None, None, None))
            break
        qkv, o, lse, vec, *xp = plan.attn_forward(
            x, gathered[index][0], first, [rest.near[1]] if first else []
        )
        xp = xp[0] if first else x
        if first:
            rest.pass_on(o, rest.far[-1], ahead.far[0])
            gathered[0][1] = Weights(rest.held(o), rest.place(), 0, rest_own.shape[1])
        if not last:
            ahead.pass_on(o)
            ahead.step(bits[-1], o)
        x1, act, slope, x = plan.mlp_forward(
            xp, o, gathered[index][1], vec, last, [] if last else [ahead.near[-1]]
        )
        if not last:
            ahead.pass_on()
            held = ahead.held(x1)
            qhalf, half = (p.shape[1] for p in packs[index + 1])
            gathered.append(
                [Weights(held, ahead.place(), 0, qhalf), Weights(held, ahead.place(), qhalf, half)]
            )
        stored.append((xp, qkv, o, lse, vec, x1, act, slope))
    g = None
    state = (moment_one, moment_two, weights)
    outs, turned = None, None
    tails = {}

    def finish(done, outs):
        pair = finish_groups([parts for parts, _ in done])
        start = 0
        for _, spot in done:
            outs = update_group(core_arr, pair, start, state, outs, *spot)
            start += spot[2]
            mine, other = (p[:, start : start + TILE] for p in pair)
            tails[spot[:2]] = jnp.where(core == 0, mine, other).astype(F32).T
            start += TILE
        return outs

    groups, before = [], []
    for index in reversed(range(layers)):
        first, last = index == 0, index == layers - 1
        wq, wr = gathered[index]
        xp, qkv, o, lse, vec, x1, act, slope = stored[index]
        for half in range(2):
            if half == 0:
                gx1, keep, send = (
                    tail if last else plan.mlp_backward(images, g, x1, act, slope, wr, vec, last, before)
                )
                spot = (index, 1, FF)
            else:
                g, keep, send = plan.attn_backward(gx1, xp, qkv, lse, o, wq, wr, vec, first, before)
                spot = (index, 0, 2 * width)
                if last:
                    turned = turn_images(after(output, g))
                if first:
                    parts, at = groups.pop(0)
                    outs = finish([(after(parts, g), at)], outs)
            if groups:
                parts, at = groups[-1]
                keep, send, turned, outs, parts = lax.optimization_barrier((keep, send, turned, outs, parts))
                groups[-1] = parts, at
            joined = join_cores(keep, send)
            before = [joined]
            groups.append((exchange_shards(joined), spot))
    output = turned.swapaxes(0, 1)
    outs = finish(groups[:-1], outs)
    parts, spot = groups[-1]
    parts, outs = lax.optimization_barrier((parts, outs))
    outs = finish([(parts, spot)], outs)
    vec_grads = [
        jnp.concatenate([tails[index, 0][:5], tails[index, 1][:7]], 0) for index in range(layers)
    ]
    vector_grad = jnp.stack(vec_grads)
    weight_grad, moment_one_new, moment_two_new, update = outs
    vector_one_new, vector_two_new, vector_update = adamw(
        vector_grad, vector_one, vector_two, vectors
    )
    return (
        output,
        g,
        weight_grad,
        vector_grad,
        moment_one_new,
        moment_two_new,
        vector_one_new,
        vector_two_new,
        update,
        vector_update,
    )


def solution(mesh):
    in_specs = (
        P(("rep", "shard"), None, None),
        P(None, "shard", None),
        P(None, None, "shard"),
        P(None, "shard", None),
        P(None, "shard", None),
        P(None, None, "shard"),
        P(None, None, "shard"),
        P(("rep", "shard")),
        P(("rep", "shard"), None, None),
    )
    out_specs = (
        P(("rep", "shard"), None, None),
        P(("rep", "shard"), None, None),
        P(None, "shard", None),
        P(None, None, "shard"),
        P(None, "shard", None),
        P(None, "shard", None),
        P(None, None, "shard"),
        P(None, None, "shard"),
        P(None, "shard", None),
        P(None, None, "shard"),
    )
    return jax.shard_map(local, mesh=mesh, in_specs=in_specs, out_specs=out_specs, check_vma=False)
```

```python
import functools
import math

import jax
import jax.numpy as jnp
from jax import lax
from jax.experimental import pallas as pl
from jax.experimental.pallas import tpu as pltpu
from jax.sharding import PartitionSpec as P

HEAD = 64
FF = 1536
STEP = 10
PAIR = 2
TILE = 128
CHUNK = 768
NEG = -1e30
F32 = jnp.float32
BF16 = jnp.bfloat16
VMEM_LIMIT = 60 * 1024 * 1024


def dot(left, right):
    return jnp.dot(left, right, preferred_element_type=F32)


def dot_nt(left, right):
    return lax.dot_general(left, right, (((1,), (1,)), ((), ())), preferred_element_type=F32)


def dot_tn(left, right):
    return lax.dot_general(left, right, (((0,), (0,)), ((), ())), preferred_element_type=F32)


def norm(values):
    center = values - jnp.mean(values, -1, keepdims=True)
    scale = lax.rsqrt(jnp.mean(center * center, -1, keepdims=True) + 1e-06)
    return center * scale, scale


def norm_back(grad, normed, scale, gain):
    inner = grad * gain
    return scale * (
        inner
        - jnp.mean(inner, -1, keepdims=True)
        - normed * jnp.mean(inner * normed, -1, keepdims=True)
    )


def gelu_parts(u):
    phi = 0.5 + 0.5 * lax.erf(u * math.sqrt(0.5))
    slope = phi + u * (jnp.exp2((u * u) * (-0.5 * math.log2(math.e))) * (1.0 / math.sqrt(2.0 * math.pi)))
    return u * phi, slope


def bias_up(vec_ref, width):
    return jnp.concatenate([vec_ref[8 + j : 9 + j, :] for j in range(FF // width)], 1)


def weight_copies(core_ref, place_ref, sources, start, whole_ref, sems):
    half = whole_ref.shape[1] // 2
    per_core = len(sources) // 2
    copies = []
    for n, source in enumerate(sources):
        at = core_ref[0] if n < per_core else 1 - core_ref[0]
        cols = pl.ds(pl.multiple_of(at * half, TILE), half)
        base = sum(piece.shape[0] for piece in sources[: n % per_core])
        copies += row_copies(
            place_ref, source, base, slice(start, start + half), whole_ref, cols, sems, len(copies)
        )
    return copies


def load_weights(*args):
    copies = weight_copies(*args)
    for copy in copies:
        copy.start()
    for copy in copies:
        copy.wait()


def load_first(core_ref, place_ref, sources, start, whole_ref, sems):
    per_core = len(sources) // 2
    size = whole_ref.shape[1]

    def load(chosen):
        copies = []
        for n, source in enumerate(chosen):
            copies += row_copies(
                place_ref, source, len(copies), slice(start, start + size), whole_ref, slice(0, size), sems,
                len(copies),
            )
        for copy in copies:
            copy.start()
        for copy in copies:
            copy.wait()

    @pl.when(core_ref[0] == 0)
    def _():
        load(sources[:per_core])

    @pl.when(core_ref[0] != 0)
    def _():
        load(sources[per_core:])


def row_copies(place_ref, source, base, taken, whole_ref, cols, sems, at):
    count, rows = source.shape[:2]
    copies = []
    for k in range(count):
        row = pl.multiple_of(place_ref[base + k] * rows, rows)
        copies.append(
            pltpu.make_async_copy(
                source.at[k, :, taken], whole_ref.at[pl.ds(row, rows), cols], sems.at[at + k]
            )
        )
    return copies


def attn_forward(first, seq, rows, at, start, core_ref, place_ref, x_ref, *refs):
    sources, refs = refs[:at], refs[at:]
    if first:
        qkv_ref, o_ref, lse_ref, vec_ref, xp_ref, w_ref, sems = refs
    else:
        qkv_ref, o_ref, lse_ref, vec_ref, w_ref, sems = refs
        xp_ref = x_ref
    width = o_ref.shape[1]
    heads = width // HEAD

    copies = weight_copies(core_ref, place_ref, sources, start, w_ref, sems)

    @pl.when(pl.program_id(0) == 0)
    def _():
        for copy in copies:
            copy.start()

    if first:
        for i in range(PAIR):
            xp_ref[i * rows : i * rows + seq, :] = x_ref[i].astype(F32)
            xp_ref[i * rows + seq : (i + 1) * rows, :] = jnp.zeros((rows - seq, width), F32)

    normed, _ = norm(xp_ref[...])

    @pl.when(pl.program_id(0) == 0)
    def _():
        for copy in copies:
            copy.wait()
        turned = w_ref[:, 3 * width : 3 * width + TILE].astype(F32).T
        vec_ref[...] = turned[: vec_ref.shape[0]]

    hidden = (normed * vec_ref[0:1, :] + vec_ref[1:2, :]).astype(BF16)
    qkv = dot(hidden, w_ref[:, : 3 * width])
    qkv_ref[:, :width] = ((qkv[:, :width] + vec_ref[2:3, :]) * 0.125).astype(BF16)
    qkv_ref[:, width : 2 * width] = qkv[:, width : 2 * width].astype(BF16)
    qkv_ref[:, 2 * width :] = (qkv[:, 2 * width :] + vec_ref[3:4, :]).astype(BF16)

    edge = seq // 16 * 16
    alive = lax.broadcasted_iota(jnp.int32, (rows - edge, rows), 0) < seq - edge
    left = lax.broadcasted_iota(jnp.int32, (rows, TILE), 1) < HEAD
    work = [(i, h) for i in range(PAIR) for h in range(heads)]

    def scores_of(i, h):
        span = slice(i * rows, (i + 1) * rows)
        tile = h * HEAD // TILE * TILE
        mine = left if h * HEAD == tile else ~left
        query = jnp.where(mine, qkv_ref[span, tile : tile + TILE], jnp.zeros((), BF16))
        return dot_nt(qkv_ref[span, width + tile : width + tile + TILE], query)

    def finish(i, h, probs, total):
        out = dot(turned_v[i][h * HEAD : (h + 1) * HEAD], probs) * (1.0 / total)
        outs[i].append(out.astype(BF16))
        if h == heads - 1:
            o_ref[i * rows : (i + 1) * rows, :] = jnp.concatenate(outs[i], 0).T

    outs = [[] for _ in range(PAIR)]
    turned_v = [qkv_ref[i * rows : (i + 1) * rows, 2 * width :].T for i in range(PAIR)]
    ahead = [scores_of(*item) for item in work[:4]]
    behind = []
    for n, (i, h) in enumerate(work):
        if n + 4 < len(work):
            ahead.append(scores_of(*work[n + 4]))
        scores = ahead.pop(0)
        low = scores[:edge]
        high = jnp.where(alive, scores[edge:], NEG)
        top = jnp.maximum(jnp.max(low, 0, keepdims=True), jnp.max(high, 0, keepdims=True))
        low = jnp.exp(low - top)
        high = jnp.exp(high - top)
        total = jnp.sum(low, 0, keepdims=True) + jnp.sum(high, 0, keepdims=True)
        lse_ref[i, h : h + 1, :rows] = top + jnp.log(total)
        behind.append((i, h, jnp.concatenate([low.astype(BF16), high.astype(BF16)], 0), total))
        if len(behind) > 1:
            finish(*behind.pop(0))
    for item in behind:
        finish(*item)


def mlp_forward(last, seq, rows, at, start, core_ref, place_ref, x_ref, o_ref, vec_ref, *refs):
    sources, refs = refs[:at], refs[at:]
    x1_ref, act_ref, slope_ref, out_ref, w_ref, sems = refs
    width = x_ref.shape[1]

    if at:

        @pl.when(pl.program_id(0) == 0)
        def _():
            load_weights(core_ref, place_ref, sources, start, w_ref, sems)

    x1 = x_ref[...] + dot(o_ref[...], w_ref[:, :width]) + vec_ref[4:5, :]
    x1_ref[...] = x1
    normed, _ = norm(x1)
    hidden = (normed * vec_ref[5:6, :] + vec_ref[6:7, :]).astype(BF16)
    bias = bias_up(vec_ref, width)
    units = [(r, j) for r in range(0, x1.shape[0], x1.shape[0]) for j in range(0, FF, CHUNK)]
    size = x1.shape[0]

    def up(r, j):
        return dot(hidden[r : r + size], w_ref[:, width + j : width + j + CHUNK])

    totals = {r: x1[r : r + size] + vec_ref[7:8, :] for r, _ in units}

    def down(r, j, act):
        start = width + FF + j
        totals[r] = totals[r] + dot_nt(act, w_ref[:, start : start + CHUNK])

    ahead = up(*units[0])
    behind = None
    for n, (r, j) in enumerate(units):
        u = ahead
        if n + 1 < len(units):
            ahead = up(*units[n + 1])
        if behind is not None:
            down(*behind)
        acts = []
        for k in range(0, size, 16):
            act, slope = gelu_parts(u[k : k + 16] + bias[:, j : j + CHUNK])
            slope_ref[r + k : r + k + 16, j : j + CHUNK] = slope
            acts.append(act.astype(BF16))
        act = jnp.concatenate(acts, 0)
        act_ref[r : r + size, j : j + CHUNK] = act
        behind = (r, j, act)
    down(*behind)
    total = jnp.concatenate([totals[r] for r in sorted(totals)], 0)
    if last:
        for i in range(PAIR):
            out_ref[i] = total[i * rows : i * rows + seq]
    else:
        out_ref[...] = total


def put_grads(core, first_of, second_of, keep_ref, send_ref):
    @pl.when(core == 0)
    def _():
        first_of(keep_ref)
        second_of(send_ref)

    @pl.when(core != 0)
    def _():
        first_of(send_ref)
        second_of(keep_ref)


def put_vectors(acc_ref, ref):
    size = acc_ref.shape[0]
    padded = jnp.concatenate(
        [acc_ref[...], jnp.zeros((TILE - size, acc_ref.shape[1]), F32)], 0
    )
    ref[:, ref.shape[1] - TILE :] = padded.T.astype(BF16)


def column_sum(values):
    return jnp.sum(values, 0, keepdims=True)


def mlp_backward(
    last, seq, rows, at, start, core_ref, place_ref, live_ref, g_ref, x1_ref, act_ref, slope_ref, vec_ref, *refs
):
    sources, refs = refs[:at], refs[at:]
    gx1_ref, keep_ref, send_ref, w_ref, up_ref, down_ref, acc_ref, bias_ref, gp_ref, sems = refs
    width = x1_ref.shape[1]
    step = pl.program_id(0)

    if at:

        @pl.when(step == 0)
        def _():
            copies = weight_copies(core_ref, place_ref, sources, start, w_ref, sems)
            for copy in copies:
                copy.start()
            for ref in (up_ref, down_ref, acc_ref, bias_ref):
                ref[...] = jnp.zeros_like(ref)
            for copy in copies:
                copy.wait()

    if last:
        for i in range(PAIR):
            keep = (step * PAIR + i < live_ref[0]).astype(F32)
            gp_ref[i * rows : i * rows + seq, :] = g_ref[i].astype(F32) * keep
            gp_ref[i * rows + seq : (i + 1) * rows, :] = jnp.zeros((rows - seq, width), F32)
        g = gp_ref[...]
    else:
        g = g_ref[...]
    low = g.astype(BF16)
    size = CHUNK

    def back(j):
        start = width + FF + j
        return dot(low, w_ref[:, start : start + size])

    ahead = back(0)
    turned = low.T
    normed, scale = norm(x1_ref[...])
    hidden = (normed * vec_ref[5:6, :] + vec_ref[6:7, :]).astype(BF16)
    turned_h = hidden.T
    acc_ref[2:3, :] += column_sum(g)
    total = None

    def finish(total, j, gu):
        up_ref[:, j : j + size] += dot(turned_h, gu)
        part = dot_nt(gu, w_ref[:, width + j : width + j + size])
        return part if total is None else total + part

    behind = None
    for j in range(0, FF, size):
        ga = ahead
        if j + size < FF:
            ahead = back(j + size)
        down_ref[:, j : j + size] += dot(turned, act_ref[:, j : j + size])
        if behind is not None:
            total = finish(total, *behind)
        gus = []
        sums = jnp.zeros((8, size), F32)
        for r in range(0, ga.shape[0], 16):
            gu = ga[r : r + 16].astype(BF16).astype(F32) * slope_ref[r : r + 16, j : j + size]
            sums = sums + gu[:8] + gu[8:]
            gus.append(gu.astype(BF16))
        bias_ref[:, j : j + size] += sums
        behind = (j, jnp.concatenate(gus, 0))
    total = finish(total, *behind)
    gh2 = total.astype(BF16).astype(F32)
    acc_ref[0:1, :] += column_sum(gh2 * normed)
    acc_ref[1:2, :] += column_sum(gh2)
    gx1_ref[...] = g + norm_back(gh2, normed, scale, vec_ref[5:6, :])

    @pl.when(step == pl.num_programs(0) - 1)
    def _():
        sums = column_sum(bias_ref[...])
        for j in range(FF // width):
            acc_ref[3 + j : 4 + j, :] = sums[:, j * width : (j + 1) * width]

        def up(ref):
            ref[:, :FF] = up_ref[...].astype(BF16)
            put_vectors(acc_ref, ref)

        def down(ref):
            ref[:, :FF] = down_ref[...].astype(BF16)
            ref[:, FF:] = jnp.zeros((width, TILE), BF16)

        put_grads(core_ref[0], up, down, keep_ref, send_ref)


def last_layer(seq, rows, at, starts, core_ref, place_ref, live_ref, x_ref, g_ref, *refs):
    sources, refs = refs[:at], refs[at:]
    (qkv_ref, o_ref, lse_ref, vec_ref, out_ref, gx1_ref, keep_ref, send_ref,
     wq_ref, wr_ref, x1_ref, act_ref, slope_ref, up_ref, down_ref, acc_ref, bias_ref, gp_ref, sems, rsems) = refs
    step = pl.program_id(0)
    copies = weight_copies(core_ref, place_ref, sources, starts[1], wr_ref, rsems)

    @pl.when(step == 0)
    def _():
        for copy in copies:
            copy.start()
        for ref in (up_ref, down_ref, acc_ref, bias_ref):
            ref[...] = jnp.zeros_like(ref)

    attn_forward(
        False, seq, rows, at, starts[0], core_ref, place_ref, x_ref, *sources,
        qkv_ref, o_ref, lse_ref, vec_ref, wq_ref, sems,
    )

    @pl.when(step == 0)
    def _():
        for copy in copies:
            copy.wait()

    mlp_forward(
        True, seq, rows, 0, 0, core_ref, place_ref, x_ref, o_ref, vec_ref,
        x1_ref, act_ref, slope_ref, out_ref, wr_ref, rsems,
    )
    mlp_backward(
        True, seq, rows, 0, 0, core_ref, place_ref, live_ref, g_ref, x1_ref, act_ref, slope_ref, vec_ref,
        gx1_ref, keep_ref, send_ref, wr_ref, up_ref, down_ref, acc_ref, bias_ref, gp_ref, rsems,
    )


def attn_backward(
    first, seq, rows, ats, starts, core_ref, qplace_ref, place_ref, g_ref, x_ref, qkv_ref, lse_ref, o_ref,
    vec_ref, *refs
):
    qsources, refs = refs[: ats[0]], refs[ats[0] :]
    sources, refs = refs[: ats[1]], refs[ats[1] :]
    gx_ref, keep_ref, send_ref, w_ref, wout_ref, gw_ref, gout_ref, acc_ref, gqkv_ref, go_ref, sems, osems = refs
    width = x_ref.shape[1]
    heads = width // HEAD
    step = pl.program_id(0)

    copies = weight_copies(core_ref, qplace_ref, qsources, starts[0], w_ref, sems)

    @pl.when(step == 0)
    def _():
        for copy in copies:
            copy.start()
        load_first(core_ref, place_ref, sources, starts[1], wout_ref, osems)
        for ref in (gw_ref, gout_ref, acc_ref):
            ref[...] = jnp.zeros_like(ref)

    low = g_ref[...].astype(BF16)
    go_ref[...] = dot_nt(low, wout_ref[...]).astype(BF16)

    @pl.when(step == 0)
    def _():
        for copy in copies:
            copy.wait()

    edge = seq // 16 * 16
    alive = lax.broadcasted_iota(jnp.int32, (rows - edge, rows), 0) < seq - edge
    left = lax.broadcasted_iota(jnp.int32, (rows, TILE), 1) < HEAD
    zero = jnp.zeros((), BF16)
    work = [(i, h) for i in range(PAIR) for h in range(heads)]

    def tile_of(ref, part, i, h):
        at = part * width + h * HEAD // TILE * TILE
        return ref[i * rows : (i + 1) * rows, at : at + TILE]

    def start(i, h):
        mine = left if h * HEAD % TILE == 0 else ~left
        query = jnp.where(mine, tile_of(qkv_ref, 0, i, h), zero)
        go = jnp.where(mine, tile_of(go_ref, 0, i, h), zero)
        return dot_nt(tile_of(qkv_ref, 1, i, h), query), dot_nt(tile_of(qkv_ref, 2, i, h), go)

    def finish(i, h, probs, gs):
        gvs[i].append(dot(probs, tile_of(go_ref, 0, i, h)))
        gks[i].append(dot(gs, tile_of(qkv_ref, 0, i, h)))
        gqs[i].append((dot(turned_k[i][h * HEAD : (h + 1) * HEAD], gs) * 0.125).astype(BF16))
        span = slice(i * rows, (i + 1) * rows)
        if h % 2:
            for part, held in ((1, gks[i]), (2, gvs[i])):
                at = part * width + h * HEAD // TILE * TILE
                gqkv_ref[span, at : at + TILE] = jnp.where(left, held[h - 1], held[h]).astype(BF16)
        if h == heads - 1:
            gqkv_ref[span, :width] = jnp.concatenate(gqs[i], 0).T

    def post(i):
        span = slice(i * rows, (i + 1) * rows)
        gqkv = gqkv_ref[span, :]
        gw_ref[...] += dot(turned_h[i], gqkv)
        gh = dot_nt(gqkv, w_ref[:, : 3 * width]).astype(BF16).astype(F32)
        acc_ref[2:3, :] += column_sum(gqkv[:, :width].astype(F32))
        acc_ref[3:4, :] += column_sum(gqkv[:, 2 * width :].astype(F32))
        acc_ref[0:1, :] += column_sum(gh * normed[i])
        acc_ref[1:2, :] += column_sum(gh)
        gx = g_ref[span, :] + norm_back(gh, normed[i], scale[i], vec_ref[0:1, :])
        if first:
            gx_ref[i] = gx[:seq]
        else:
            gx_ref[span, :] = gx

    gks, gvs, gqs = ([[] for _ in range(PAIR)] for _ in range(3))
    turned_k = [qkv_ref[i * rows : (i + 1) * rows, width : 2 * width].T for i in range(PAIR)]
    ahead = [start(*item) for item in work[:2]]
    normed, scale, turned_h = [], [], []
    for i in range(PAIR):
        part, size = norm(x_ref[i * rows : (i + 1) * rows, :])
        normed.append(part)
        scale.append(size)
        turned_h.append((part * vec_ref[0:1, :] + vec_ref[1:2, :]).astype(BF16).T)
    behind = []
    for n, (i, h) in enumerate(work):
        if n + 2 < len(work):
            ahead.append(start(*work[n + 2]))
        scores, gp = ahead.pop(0)
        scores = scores - lse_ref[i, h : h + 1, :rows]
        p_low = jnp.exp(scores[:edge])
        p_high = jnp.where(alive, jnp.exp(scores[edge:]), 0.0)
        probs = jnp.concatenate([p_low.astype(BF16), p_high.astype(BF16)], 0)
        gp_low, gp_high = gp[:edge], gp[edge:]
        mean = column_sum(gp_low * p_low) + column_sum(gp_high * p_high)
        gs_low = (p_low * (gp_low - mean)).astype(BF16)
        gs_high = (p_high * (gp_high - mean)).astype(BF16)
        behind.append((i, h, probs, jnp.concatenate([gs_low, gs_high], 0)))
        if len(behind) > 1:
            finish(*behind.pop(0))
    for item in behind:
        finish(*item)
    gout_ref[...] += dot(o_ref[...].T, low)
    acc_ref[4:5, :] += column_sum(g_ref[...])
    for i in range(PAIR):
        post(i)
    @pl.when(step == pl.num_programs(0) - 1)
    def _():
        def one(ref):
            ref[:, : 2 * width] = gw_ref[:, : 2 * width].astype(BF16)
            put_vectors(acc_ref, ref)

        def two(ref):
            ref[:, :width] = gw_ref[:, 2 * width :].astype(BF16)
            ref[:, width : 2 * width] = gout_ref[...].astype(BF16)
            ref[:, 2 * width :] = jnp.zeros((width, TILE), BF16)

        put_grads(core_ref[0], one, two, keep_ref, send_ref)


def adamw(grad, first, second, old):
    first_new = 0.9 * first + 0.1 * grad
    second_new = 0.999 * second + 0.001 * grad * grad
    first_hat = first_new / (1.0 - 0.9**STEP)
    second_hat = second_new / (1.0 - 0.999**STEP)
    change = -0.01 * (first_hat / (jnp.sqrt(second_hat) + 1e-08) + 0.05 * old)
    return (first_new, second_new, change)


def step_kernel(start, core_ref, mine_ref, other_ref, one_ref, two_ref, old_ref, *refs):
    grad_ref, one_new_ref, two_new_ref, change_ref = refs[-4:]
    cols = slice(start, start + grad_ref.shape[2])

    def put(from_ref):
        grad = from_ref[:, cols].astype(F32)
        grad_ref[0] = grad
        one_new_ref[0], two_new_ref[0], change_ref[0] = adamw(grad, one_ref[0], two_ref[0], old_ref[0])

    @pl.when(core_ref[0] == pl.program_id(0))
    def _():
        put(mine_ref)

    @pl.when(core_ref[0] != pl.program_id(0))
    def _():
        put(other_ref)


def smem():
    return pl.BlockSpec(memory_space=pltpu.SMEM)


def whole(shape):
    zeros = (0,) * len(shape)
    return pl.BlockSpec(shape, lambda i: zeros)


def cost(flops, moved, exps):
    return pl.CostEstimate(flops=int(flops), bytes_accessed=int(moved), transcendentals=int(exps))


def params():
    return pltpu.CompilerParams(
        dimension_semantics=("arbitrary",), vmem_limit_bytes=VMEM_LIMIT
    )


def struct(shape, kind):
    return jax.ShapeDtypeStruct(shape, kind)


class Weights:
    def __init__(self, arrays, place, start, half):
        self.arrays, self.place, self.start, self.half = arrays, place, start, half

    def specs(self):
        return [pl.BlockSpec(memory_space=pl.ANY)] * len(self.arrays)

    def sems(self):
        return pltpu.SemaphoreType.DMA((sum(a.shape[0] for a in self.arrays),))


def call(kernel, after, in_specs, **rest):
    count = len(after)

    def run(*refs):
        kernel(*refs[count:])

    made = pl.pallas_call(
        run, in_specs=[pl.BlockSpec(memory_space=pl.ANY)] * count + in_specs, **rest
    )
    return lambda *args: made(*after, *args)


class Layers:
    def __init__(self, core, images, seq, width):
        self.core, self.images, self.seq, self.width = core, images, seq, width
        self.rows = -(-seq // 16) * 16
        self.grid = (images // PAIR,)
        self.total = images * self.rows
        self.block = PAIR * self.rows

    def tall(self, cols):
        return pl.BlockSpec((self.block, cols), lambda i: (i, 0))

    def images_spec(self):
        return pl.BlockSpec((PAIR, self.seq, self.width), lambda i: (i, 0, 0))

    def lse_spec(self):
        return pl.BlockSpec((PAIR, 8, 256), lambda i: (i, 0, 0))

    def attn_forward(self, x, wq, first, after):
        w, t = self.width, self.total
        outs = [
            (self.tall(3 * w), struct((t, 3 * w), BF16)),
            (self.tall(w), struct((t, w), BF16)),
            (self.lse_spec(), struct((self.images, 8, 256), F32)),
            (whole((16, w)), struct((16, w), F32)),
        ]
        if first:
            outs.append((self.tall(w), struct((t, w), F32)))
        return call(
            functools.partial(attn_forward, first, self.seq, self.rows, len(wq.arrays), wq.start),
            after,
            [smem(), smem(), self.images_spec() if first else self.tall(w)] + wq.specs(),
            grid=self.grid,
            out_specs=[o[0] for o in outs],
            out_shape=[o[1] for o in outs],
            scratch_shapes=[pltpu.VMEM((w, 2 * wq.half), BF16), wq.sems()],
            compiler_params=params(),
            cost_estimate=cost(1.7e10, 2e7, 3e6),
        )(self.core, wq.place, x, *wq.arrays)

    def mlp_forward(self, x, o, wr, vec, last, after):
        w, t = self.width, self.total
        outs = [
            (self.tall(w), struct((t, w), F32)),
            (self.tall(FF), struct((t, FF), BF16)),
            (self.tall(FF), struct((t, FF), F32)),
            (self.images_spec(), struct((self.images, self.seq, w), F32))
            if last
            else (self.tall(w), struct((t, w), F32)),
        ]
        return call(
            functools.partial(mlp_forward, last, self.seq, self.rows, len(wr.arrays), wr.start),
            after,
            [smem(), smem(), self.tall(w), self.tall(w), whole(vec.shape)] + wr.specs(),
            grid=self.grid,
            out_specs=[o[0] for o in outs],
            out_shape=[o[1] for o in outs],
            scratch_shapes=[pltpu.VMEM((w, 2 * wr.half), BF16), wr.sems()],
            compiler_params=params(),
            cost_estimate=cost(2.2e10, 3e7, 3e6),
        )(self.core, wr.place, x, o, vec, *wr.arrays)

    def mlp_backward(self, live, g, x1, act, slope, wr, vec, last, after):
        w, t = self.width, self.total
        return call(
            functools.partial(mlp_backward, last, self.seq, self.rows, len(wr.arrays), wr.start),
            after,
            [
                smem(), smem(), smem(),
                self.images_spec() if last else self.tall(w),
                self.tall(w), self.tall(FF), self.tall(FF), whole(vec.shape),
            ]
            + wr.specs(),
            grid=self.grid,
            out_specs=[self.tall(w), whole((w, FF + TILE)), whole((w, FF + TILE))],
            out_shape=[
                struct((t, w), F32), struct((w, FF + TILE), BF16), struct((w, FF + TILE), BF16),
            ],
            scratch_shapes=[
                pltpu.VMEM((w, 2 * wr.half), BF16),
                pltpu.VMEM((w, FF), F32),
                pltpu.VMEM((w, FF), F32),
                pltpu.VMEM((8, w), F32),
                pltpu.VMEM((8, FF), F32),
                pltpu.VMEM((self.block, w), F32),
                wr.sems(),
            ],
            compiler_params=params(),
            cost_estimate=cost(2.4e10, 3e7, 3e6),
        )(self.core, wr.place, live, g, x1, act, slope, vec, *wr.arrays)

    def last_layer(self, live, x, g, wq, wr):
        w, t = self.width, self.total
        outs = [
            (self.tall(3 * w), struct((t, 3 * w), BF16)),
            (self.tall(w), struct((t, w), BF16)),
            (self.lse_spec(), struct((self.images, 8, 256), F32)),
            (whole((16, w)), struct((16, w), F32)),
            (self.images_spec(), struct((self.images, self.seq, w), F32)),
            (self.tall(w), struct((t, w), F32)),
            (whole((w, FF + TILE)), struct((w, FF + TILE), BF16)),
            (whole((w, FF + TILE)), struct((w, FF + TILE), BF16)),
        ]
        return call(
            functools.partial(last_layer, self.seq, self.rows, len(wq.arrays), (wq.start, wr.start)),
            [],
            [smem(), smem(), smem(), self.tall(w), self.images_spec()] + wq.specs(),
            grid=self.grid,
            out_specs=[o[0] for o in outs],
            out_shape=[o[1] for o in outs],
            scratch_shapes=[
                pltpu.VMEM((w, 2 * wq.half), BF16),
                pltpu.VMEM((w, 2 * wr.half), BF16),
                pltpu.VMEM((self.block, w), F32),
                pltpu.VMEM((self.block, FF), BF16),
                pltpu.VMEM((self.block, FF), F32),
                pltpu.VMEM((w, FF), F32),
                pltpu.VMEM((w, FF), F32),
                pltpu.VMEM((8, w), F32),
                pltpu.VMEM((8, FF), F32),
                pltpu.VMEM((self.block, w), F32),
                wq.sems(),
                wr.sems(),
            ],
            compiler_params=params(),
            cost_estimate=cost(4.5e10, 3e7, 3e6),
        )(self.core, wq.place, live, x, g, *wq.arrays)

    def attn_backward(self, g, x, qkv, lse, o, wq, wr, vec, first, after):
        w, t = self.width, self.total
        return call(
            functools.partial(
                attn_backward, first, self.seq, self.rows,
                (len(wq.arrays), len(wr.arrays)), (wq.start, wr.start),
            ),
            after,
            [
                smem(), smem(), smem(), self.tall(w), self.tall(w), self.tall(3 * w),
                self.lse_spec(), self.tall(w), whole(vec.shape),
            ]
            + wq.specs()
            + wr.specs(),
            grid=self.grid,
            out_specs=[
                self.images_spec() if first else self.tall(w),
                whole((w, 2 * w + TILE)), whole((w, 2 * w + TILE)),
            ],
            out_shape=[
                struct((self.images, self.seq, w), F32) if first else struct((t, w), F32),
                struct((w, 2 * w + TILE), BF16), struct((w, 2 * w + TILE), BF16),
            ],
            scratch_shapes=[
                pltpu.VMEM((w, 2 * wq.half), BF16),
                pltpu.VMEM((w, w), BF16),
                pltpu.VMEM((w, 3 * w), F32),
                pltpu.VMEM((w, w), F32),
                pltpu.VMEM((8, w), F32),
                pltpu.VMEM((self.block, 3 * w), BF16),
                pltpu.VMEM((self.block, w), BF16),
                wq.sems(),
                wr.sems(),
            ],
            compiler_params=params(),
            cost_estimate=cost(3e10, 2e7, 3e6),
        )(self.core, wq.place, wr.place, g, x, qkv, lse, o, vec, *wq.arrays, *wr.arrays)


def flip(axis, bit):
    return [(i, i ^ bit) for i in range(lax.axis_size(axis))]


def swap_cores(value):
    return lax.ppermute(value, "rep", flip("rep", 1))


def own_half(packed, core):
    half = packed.shape[1] // 2
    return lax.dynamic_slice_in_dim(packed, core * half, half, 1)


class Gathering:
    def __init__(self, own):
        self.near = [own[None]]
        self.far = [self.neighbour(self.near[0])]
        self.ids = [0]

    @staticmethod
    def neighbour(piece):
        return lax.ppermute(piece, "shard", flip("shard", 1))

    def step(self, bit, anchor=None):
        have = self.near[0] if len(self.near) == 1 else jnp.concatenate(self.near, 0)
        have = have if anchor is None else after(have, anchor)
        self.near.append(lax.ppermute(have, "shard", flip("shard", bit)))
        self.ids += [i ^ bit for i in self.ids]

    def pass_on(self, *anchors):
        piece = after(self.near[-1], *anchors) if anchors else self.near[-1]
        self.far.append(self.neighbour(piece))

    def held(self, anchor=None):
        pieces = self.near + self.far
        if anchor is not None:
            pieces[-1] = after(pieces[-1], anchor)
        return pieces + [swap_cores(p) for p in pieces]

    def place(self):
        me = lax.axis_index("shard").astype(jnp.int32)
        return me ^ jnp.array(self.ids + [i ^ 1 for i in self.ids], jnp.int32)


def after(value, *others):
    return lax.optimization_barrier((value,) + others)[0]


def turn_kernel(in_ref, out_ref):
    for i in range(in_ref.shape[0]):
        out_ref[:, i, :] = in_ref[i]


def turn_images(value):
    images, seq, width = value.shape
    return pl.pallas_call(
        turn_kernel,
        grid=(width // TILE,),
        in_specs=[pl.BlockSpec((images, seq, TILE), lambda i: (0, 0, i))],
        out_specs=pl.BlockSpec((seq, images, TILE), lambda i: (0, 0, i)),
        out_shape=struct((seq, images, width), value.dtype),
        compiler_params=params(),
        cost_estimate=cost(1e6, 5e6, 0),
    )(value)


def join_cores(keep, send):
    other = swap_cores(send)
    return (keep.astype(F32) + other.astype(F32)).astype(BF16)


def exchange_shards(joined):
    count = lax.axis_size("shard")
    rows, cols = joined.shape
    return lax.all_to_all(joined.reshape(count, rows // count, cols), "shard", 0, 0, tiled=True)


def finish_groups(groups):
    mine = jnp.concatenate([jnp.sum(parts.astype(F32), 0).astype(BF16) for parts in groups], 1)
    bit = 2
    while bit < lax.axis_size("rep"):
        other = lax.ppermute(mine, "rep", flip("rep", bit))
        mine = (mine.astype(F32) + other.astype(F32)).astype(BF16)
        bit *= 2
    return mine, swap_cores(mine)


def update_group(core, pair, start, state, outs, layer, at, cols):
    mine, other = pair
    spec = pl.BlockSpec((1, mine.shape[0], cols), lambda j: (layer, 0, at + j))
    shape = struct(state[0].shape, F32)
    given = list(outs) if outs is not None else []
    return pl.pallas_call(
        functools.partial(step_kernel, start),
        grid=(2,),
        in_specs=[smem(), whole(mine.shape), whole(other.shape), spec, spec, spec]
        + [pl.BlockSpec(memory_space=pl.ANY)] * len(given),
        out_specs=[spec] * 4,
        out_shape=[shape] * 4,
        input_output_aliases={6 + i: i for i in range(len(given))},
        compiler_params=params(),
        cost_estimate=cost(1e6, 4e6, 0),
    )(core, mine, other, *state, *given)


def local(
    tokens, weights, vectors, moment_one, moment_two, vector_one, vector_two, images, cotangent
):
    count, seq, width = tokens.shape
    layers = weights.shape[0]
    core = lax.axis_index("rep") % 2
    core_arr = core.reshape(1).astype(jnp.int32)
    plan = Layers(core_arr, count, seq, width)
    packs = []
    for index in range(layers):
        low = weights[index].astype(BF16)
        turned = jnp.pad(vectors[index].T.astype(BF16), ((0, 0), (0, TILE - vectors.shape[1])))
        attn_pack = jnp.concatenate([low[:, : 3 * width], turned], 1)
        rest = low[:, 3 * width :]
        rest_pack = jnp.pad(rest, ((0, 0), (0, -rest.shape[1] % (2 * TILE))))
        packs.append((own_half(attn_pack, core), own_half(rest_pack, core)))
    bits = []
    bit = lax.axis_size("shard") // 2
    while bit > 1:
        bits.append(bit)
        bit //= 2
    attn_own, rest_own = packs[0]
    query = Gathering(attn_own)
    for bit in bits:
        query.step(bit)
        query.pass_on()
    rest = Gathering(after(rest_own, query.near[1]))
    for bit in bits:
        rest.step(bit)
        if bit != bits[-1]:
            rest.pass_on()
    gathered = [[Weights(query.held(), query.place(), 0, attn_own.shape[1]), None]]
    stored = []
    x = tokens
    for index in range(layers):
        first, last = index == 0, index == layers - 1
        if not last:
            ahead = Gathering(after(jnp.concatenate(packs[index + 1], 1), rest.near[1]))
            for bit in bits[:-1]:
                ahead.step(bit)
        if last and not first:
            qkv, o, lse, vec, output, *tail = plan.last_layer(images, x, cotangent, *gathered[index])
            stored.append((x, qkv, o, lse, vec, None, None, None))
            break
        qkv, o, lse, vec, *xp = plan.attn_forward(
            x, gathered[index][0], first, [rest.near[1]] if first else []
        )
        xp = xp[0] if first else x
        if first:
            rest.pass_on(o, rest.far[-1], ahead.far[0])
            gathered[0][1] = Weights(rest.held(o), rest.place(), 0, rest_own.shape[1])
        if not last:
            ahead.pass_on(o)
            ahead.step(bits[-1], o)
        x1, act, slope, x = plan.mlp_forward(
            xp, o, gathered[index][1], vec, last, [] if last else [ahead.near[-1]]
        )
        if not last:
            ahead.pass_on()
            held = ahead.held(x1)
            qhalf, half = (p.shape[1] for p in packs[index + 1])
            gathered.append(
                [Weights(held, ahead.place(), 0, qhalf), Weights(held, ahead.place(), qhalf, half)]
            )
        stored.append((xp, qkv, o, lse, vec, x1, act, slope))
    g = None
    state = (moment_one, moment_two, weights)
    outs, turned = None, None
    tails = {}

    def finish(done, outs):
        pair = finish_groups([parts for parts, _ in done])
        start = 0
        for _, spot in done:
            outs = update_group(core_arr, pair, start, state, outs, *spot)
            start += spot[2]
            mine, other = (p[:, start : start + TILE] for p in pair)
            tails[spot[:2]] = jnp.where(core == 0, mine, other).astype(F32).T
            start += TILE
        return outs

    groups, before = [], []
    for index in reversed(range(layers)):
        first, last = index == 0, index == layers - 1
        wq, wr = gathered[index]
        xp, qkv, o, lse, vec, x1, act, slope = stored[index]
        for half in range(2):
            if half == 0:
                gx1, keep, send = (
                    tail if last else plan.mlp_backward(images, g, x1, act, slope, wr, vec, last, before)
                )
                spot = (index, 1, FF)
            else:
                g, keep, send = plan.attn_backward(gx1, xp, qkv, lse, o, wq, wr, vec, first, before)
                spot = (index, 0, 2 * width)
                if last:
                    turned = turn_images(after(output, g))
                if first:
                    parts, at = groups.pop(0)
                    outs = finish([(after(parts, g), at)], outs)
            if groups and half == 0:
                parts, at = groups[-1]
                keep, send, parts = lax.optimization_barrier((keep, send, parts))
                groups[-1] = parts, at
            joined = join_cores(keep, send)
            if groups and half == 1:
                parts, at = groups[-1]
                joined, turned, outs, parts = lax.optimization_barrier((joined, turned, outs, parts))
                groups[-1] = parts, at
            before = [joined]
            groups.append((exchange_shards(joined), spot))
    output = turned.swapaxes(0, 1)
    outs = finish(groups[:-1], outs)
    parts, spot = groups[-1]
    parts, outs = lax.optimization_barrier((parts, outs))
    outs = finish([(parts, spot)], outs)
    vec_grads = [
        jnp.concatenate([tails[index, 0][:5], tails[index, 1][:7]], 0) for index in range(layers)
    ]
    vector_grad = jnp.stack(vec_grads)
    weight_grad, moment_one_new, moment_two_new, update = outs
    vector_one_new, vector_two_new, vector_update = adamw(
        vector_grad, vector_one, vector_two, vectors
    )
    return (
        output,
        g,
        weight_grad,
        vector_grad,
        moment_one_new,
        moment_two_new,
        vector_one_new,
        vector_two_new,
        update,
        vector_update,
    )


def solution(mesh):
    in_specs = (
        P(("rep", "shard"), None, None),
        P(None, "shard", None),
        P(None, None, "shard"),
        P(None, "shard", None),
        P(None, "shard", None),
        P(None, None, "shard"),
        P(None, None, "shard"),
        P(("rep", "shard")),
        P(("rep", "shard"), None, None),
    )
    out_specs = (
        P(("rep", "shard"), None, None),
        P(("rep", "shard"), None, None),
        P(None, "shard", None),
        P(None, None, "shard"),
        P(None, "shard", None),
        P(None, "shard", None),
        P(None, None, "shard"),
        P(None, None, "shard"),
        P(None, "shard", None),
        P(None, None, "shard"),
    )
    return jax.shard_map(local, mesh=mesh, in_specs=in_specs, out_specs=out_specs, check_vma=False)
```

```python
import functools
import math

import jax
import jax.numpy as jnp
from jax import lax
from jax.experimental import pallas as pl
from jax.experimental.pallas import tpu as pltpu
from jax.sharding import PartitionSpec as P

HEAD = 64
FF = 1536
STEP = 10
PAIR = 2
TILE = 128
CHUNK = 768
NEG = -1e30
F32 = jnp.float32
BF16 = jnp.bfloat16
VMEM_LIMIT = 60 * 1024 * 1024


def dot(left, right):
    return jnp.dot(left, right, preferred_element_type=F32)


def dot_nt(left, right):
    return lax.dot_general(left, right, (((1,), (1,)), ((), ())), preferred_element_type=F32)


def dot_tn(left, right):
    return lax.dot_general(left, right, (((0,), (0,)), ((), ())), preferred_element_type=F32)


def norm(values):
    center = values - jnp.mean(values, -1, keepdims=True)
    scale = lax.rsqrt(jnp.mean(center * center, -1, keepdims=True) + 1e-06)
    return center * scale, scale


def norm_back(grad, normed, scale, gain):
    inner = grad * gain
    return scale * (
        inner
        - jnp.mean(inner, -1, keepdims=True)
        - normed * jnp.mean(inner * normed, -1, keepdims=True)
    )


def gelu_parts(u):
    phi = 0.5 + 0.5 * lax.erf(u * math.sqrt(0.5))
    slope = phi + u * (jnp.exp2((u * u) * (-0.5 * math.log2(math.e))) * (1.0 / math.sqrt(2.0 * math.pi)))
    return u * phi, slope


def bias_up(vec_ref, width):
    return jnp.concatenate([vec_ref[8 + j : 9 + j, :] for j in range(FF // width)], 1)


def weight_copies(core_ref, place_ref, sources, start, whole_ref, sems):
    half = whole_ref.shape[1] // 2
    per_core = len(sources) // 2
    copies = []
    for n, source in enumerate(sources):
        at = core_ref[0] if n < per_core else 1 - core_ref[0]
        cols = pl.ds(pl.multiple_of(at * half, TILE), half)
        base = sum(piece.shape[0] for piece in sources[: n % per_core])
        copies += row_copies(
            place_ref, source, base, slice(start, start + half), whole_ref, cols, sems, len(copies)
        )
    return copies


def load_weights(*args):
    copies = weight_copies(*args)
    for copy in copies:
        copy.start()
    for copy in copies:
        copy.wait()


def load_first(core_ref, place_ref, sources, start, whole_ref, sems):
    per_core = len(sources) // 2
    size = whole_ref.shape[1]

    def load(chosen):
        copies = []
        for n, source in enumerate(chosen):
            copies += row_copies(
                place_ref, source, len(copies), slice(start, start + size), whole_ref, slice(0, size), sems,
                len(copies),
            )
        for copy in copies:
            copy.start()
        for copy in copies:
            copy.wait()

    @pl.when(core_ref[0] == 0)
    def _():
        load(sources[:per_core])

    @pl.when(core_ref[0] != 0)
    def _():
        load(sources[per_core:])


def row_copies(place_ref, source, base, taken, whole_ref, cols, sems, at):
    count, rows = source.shape[:2]
    copies = []
    for k in range(count):
        row = pl.multiple_of(place_ref[base + k] * rows, rows)
        copies.append(
            pltpu.make_async_copy(
                source.at[k, :, taken], whole_ref.at[pl.ds(row, rows), cols], sems.at[at + k]
            )
        )
    return copies


def attn_forward(first, seq, rows, at, start, core_ref, place_ref, x_ref, *refs):
    sources, refs = refs[:at], refs[at:]
    if first:
        qkv_ref, o_ref, lse_ref, vec_ref, xp_ref, w_ref, sems = refs
    else:
        qkv_ref, o_ref, lse_ref, vec_ref, w_ref, sems = refs
        xp_ref = x_ref
    width = o_ref.shape[1]
    heads = width // HEAD

    copies = weight_copies(core_ref, place_ref, sources, start, w_ref, sems)

    @pl.when(pl.program_id(0) == 0)
    def _():
        for copy in copies:
            copy.start()

    if first:
        for i in range(PAIR):
            xp_ref[i * rows : i * rows + seq, :] = x_ref[i].astype(F32)
            xp_ref[i * rows + seq : (i + 1) * rows, :] = jnp.zeros((rows - seq, width), F32)

    normed, _ = norm(xp_ref[...])

    @pl.when(pl.program_id(0) == 0)
    def _():
        for copy in copies:
            copy.wait()
        turned = w_ref[:, 3 * width : 3 * width + TILE].astype(F32).T
        vec_ref[...] = turned[: vec_ref.shape[0]]

    hidden = (normed * vec_ref[0:1, :] + vec_ref[1:2, :]).astype(BF16)
    qkv = dot(hidden, w_ref[:, : 3 * width])
    qkv_ref[:, :width] = ((qkv[:, :width] + vec_ref[2:3, :]) * 0.125).astype(BF16)
    qkv_ref[:, width : 2 * width] = qkv[:, width : 2 * width].astype(BF16)
    qkv_ref[:, 2 * width :] = (qkv[:, 2 * width :] + vec_ref[3:4, :]).astype(BF16)

    edge = seq // 16 * 16
    alive = lax.broadcasted_iota(jnp.int32, (rows - edge, rows), 0) < seq - edge
    left = lax.broadcasted_iota(jnp.int32, (rows, TILE), 1) < HEAD
    work = [(i, h) for i in range(PAIR) for h in range(heads)]

    def scores_of(i, h):
        span = slice(i * rows, (i + 1) * rows)
        tile = h * HEAD // TILE * TILE
        mine = left if h * HEAD == tile else ~left
        query = jnp.where(mine, qkv_ref[span, tile : tile + TILE], jnp.zeros((), BF16))
        return dot_nt(qkv_ref[span, width + tile : width + tile + TILE], query)

    def finish(i, h, probs, total):
        out = dot(turned_v[i][h * HEAD : (h + 1) * HEAD], probs) * (1.0 / total)
        outs[i].append(out.astype(BF16))
        if h == heads - 1:
            o_ref[i * rows : (i + 1) * rows, :] = jnp.concatenate(outs[i], 0).T

    outs = [[] for _ in range(PAIR)]
    turned_v = [qkv_ref[i * rows : (i + 1) * rows, 2 * width :].T for i in range(PAIR)]
    ahead = [scores_of(*item) for item in work[:4]]
    behind = []
    for n, (i, h) in enumerate(work):
        if n + 4 < len(work):
            ahead.append(scores_of(*work[n + 4]))
        scores = ahead.pop(0)
        low = scores[:edge]
        high = jnp.where(alive, scores[edge:], NEG)
        top = jnp.maximum(jnp.max(low, 0, keepdims=True), jnp.max(high, 0, keepdims=True))
        low = jnp.exp(low - top)
        high = jnp.exp(high - top)
        total = jnp.sum(low, 0, keepdims=True) + jnp.sum(high, 0, keepdims=True)
        lse_ref[i, h : h + 1, :rows] = top + jnp.log(total)
        behind.append((i, h, jnp.concatenate([low.astype(BF16), high.astype(BF16)], 0), total))
        if len(behind) > 1:
            finish(*behind.pop(0))
    for item in behind:
        finish(*item)


def mlp_forward(last, seq, rows, at, start, core_ref, place_ref, x_ref, o_ref, vec_ref, *refs):
    sources, refs = refs[:at], refs[at:]
    x1_ref, act_ref, slope_ref, out_ref, w_ref, sems = refs
    width = x_ref.shape[1]

    if at:

        @pl.when(pl.program_id(0) == 0)
        def _():
            load_weights(core_ref, place_ref, sources, start, w_ref, sems)

    x1 = x_ref[...] + dot(o_ref[...], w_ref[:, :width]) + vec_ref[4:5, :]
    x1_ref[...] = x1
    normed, _ = norm(x1)
    hidden = (normed * vec_ref[5:6, :] + vec_ref[6:7, :]).astype(BF16)
    bias = bias_up(vec_ref, width)
    units = [(r, j) for r in range(0, x1.shape[0], x1.shape[0]) for j in range(0, FF, CHUNK)]
    size = x1.shape[0]

    def up(r, j):
        return dot(hidden[r : r + size], w_ref[:, width + j : width + j + CHUNK])

    totals = {r: x1[r : r + size] + vec_ref[7:8, :] for r, _ in units}

    def down(r, j, act):
        start = width + FF + j
        totals[r] = totals[r] + dot_nt(act, w_ref[:, start : start + CHUNK])

    ahead = up(*units[0])
    behind = None
    for n, (r, j) in enumerate(units):
        u = ahead
        if n + 1 < len(units):
            ahead = up(*units[n + 1])
        if behind is not None:
            down(*behind)
        acts = []
        for k in range(0, size, 16):
            act, slope = gelu_parts(u[k : k + 16] + bias[:, j : j + CHUNK])
            slope_ref[r + k : r + k + 16, j : j + CHUNK] = slope
            acts.append(act.astype(BF16))
        act = jnp.concatenate(acts, 0)
        act_ref[r : r + size, j : j + CHUNK] = act
        behind = (r, j, act)
    down(*behind)
    total = jnp.concatenate([totals[r] for r in sorted(totals)], 0)
    if last:
        for i in range(PAIR):
            out_ref[i] = total[i * rows : i * rows + seq]
    else:
        out_ref[...] = total


def put_grads(core, first_of, second_of, keep_ref, send_ref):
    @pl.when(core == 0)
    def _():
        first_of(keep_ref)
        second_of(send_ref)

    @pl.when(core != 0)
    def _():
        first_of(send_ref)
        second_of(keep_ref)


def put_vectors(acc_ref, ref):
    size = acc_ref.shape[0]
    padded = jnp.concatenate(
        [acc_ref[...], jnp.zeros((TILE - size, acc_ref.shape[1]), F32)], 0
    )
    ref[:, ref.shape[1] - TILE :] = padded.T.astype(BF16)


def column_sum(values):
    return jnp.sum(values, 0, keepdims=True)


def mlp_backward(
    last, seq, rows, at, start, core_ref, place_ref, live_ref, g_ref, x1_ref, act_ref, slope_ref, vec_ref, *refs
):
    sources, refs = refs[:at], refs[at:]
    gx1_ref, keep_ref, send_ref, w_ref, up_ref, down_ref, acc_ref, bias_ref, gp_ref, sems = refs
    width = x1_ref.shape[1]
    step = pl.program_id(0)

    if at:

        @pl.when(step == 0)
        def _():
            copies = weight_copies(core_ref, place_ref, sources, start, w_ref, sems)
            for copy in copies:
                copy.start()
            for ref in (up_ref, down_ref, acc_ref, bias_ref):
                ref[...] = jnp.zeros_like(ref)
            for copy in copies:
                copy.wait()

    if last:
        for i in range(PAIR):
            keep = (step * PAIR + i < live_ref[0]).astype(F32)
            gp_ref[i * rows : i * rows + seq, :] = g_ref[i].astype(F32) * keep
            gp_ref[i * rows + seq : (i + 1) * rows, :] = jnp.zeros((rows - seq, width), F32)
        g = gp_ref[...]
    else:
        g = g_ref[...]
    low = g.astype(BF16)
    size = CHUNK

    def back(j):
        start = width + FF + j
        return dot(low, w_ref[:, start : start + size])

    ahead = back(0)
    turned = low.T
    normed, scale = norm(x1_ref[...])
    hidden = (normed * vec_ref[5:6, :] + vec_ref[6:7, :]).astype(BF16)
    turned_h = hidden.T
    acc_ref[2:3, :] += column_sum(g)
    total = None

    def finish(total, j, gu):
        up_ref[:, j : j + size] += dot(turned_h, gu)
        part = dot_nt(gu, w_ref[:, width + j : width + j + size])
        return part if total is None else total + part

    behind = None
    for j in range(0, FF, size):
        ga = ahead
        if j + size < FF:
            ahead = back(j + size)
        down_ref[:, j : j + size] += dot(turned, act_ref[:, j : j + size])
        if behind is not None:
            total = finish(total, *behind)
        gus = []
        sums = jnp.zeros((8, size), F32)
        for r in range(0, ga.shape[0], 16):
            gu = ga[r : r + 16].astype(BF16).astype(F32) * slope_ref[r : r + 16, j : j + size]
            sums = sums + gu[:8] + gu[8:]
            gus.append(gu.astype(BF16))
        bias_ref[:, j : j + size] += sums
        behind = (j, jnp.concatenate(gus, 0))
    total = finish(total, *behind)
    gh2 = total.astype(BF16).astype(F32)
    acc_ref[0:1, :] += column_sum(gh2 * normed)
    acc_ref[1:2, :] += column_sum(gh2)
    gx1_ref[...] = g + norm_back(gh2, normed, scale, vec_ref[5:6, :])

    @pl.when(step == pl.num_programs(0) - 1)
    def _():
        sums = column_sum(bias_ref[...])
        for j in range(FF // width):
            acc_ref[3 + j : 4 + j, :] = sums[:, j * width : (j + 1) * width]

        def up(ref):
            ref[:, :FF] = up_ref[...].astype(BF16)
            put_vectors(acc_ref, ref)

        def down(ref):
            ref[:, :FF] = down_ref[...].astype(BF16)
            ref[:, FF:] = jnp.zeros((width, TILE), BF16)

        put_grads(core_ref[0], up, down, keep_ref, send_ref)


def last_layer(seq, rows, at, starts, core_ref, place_ref, live_ref, x_ref, g_ref, *refs):
    sources, refs = refs[:at], refs[at:]
    (qkv_ref, o_ref, lse_ref, vec_ref, out_ref, gx1_ref, keep_ref, send_ref,
     wq_ref, wr_ref, x1_ref, act_ref, slope_ref, up_ref, down_ref, acc_ref, bias_ref, gp_ref, sems, rsems) = refs
    step = pl.program_id(0)
    copies = weight_copies(core_ref, place_ref, sources, starts[1], wr_ref, rsems)

    @pl.when(step == 0)
    def _():
        for copy in copies:
            copy.start()
        for ref in (up_ref, down_ref, acc_ref, bias_ref):
            ref[...] = jnp.zeros_like(ref)

    attn_forward(
        False, seq, rows, at, starts[0], core_ref, place_ref, x_ref, *sources,
        qkv_ref, o_ref, lse_ref, vec_ref, wq_ref, sems,
    )

    @pl.when(step == 0)
    def _():
        for copy in copies:
            copy.wait()

    mlp_forward(
        True, seq, rows, 0, 0, core_ref, place_ref, x_ref, o_ref, vec_ref,
        x1_ref, act_ref, slope_ref, out_ref, wr_ref, rsems,
    )
    mlp_backward(
        True, seq, rows, 0, 0, core_ref, place_ref, live_ref, g_ref, x1_ref, act_ref, slope_ref, vec_ref,
        gx1_ref, keep_ref, send_ref, wr_ref, up_ref, down_ref, acc_ref, bias_ref, gp_ref, rsems,
    )


def attn_backward(
    first, seq, rows, ats, starts, core_ref, qplace_ref, place_ref, g_ref, x_ref, qkv_ref, lse_ref, o_ref,
    vec_ref, *refs
):
    qsources, refs = refs[: ats[0]], refs[ats[0] :]
    sources, refs = refs[: ats[1]], refs[ats[1] :]
    gx_ref, keep_ref, send_ref, w_ref, wout_ref, gw_ref, gout_ref, acc_ref, gqkv_ref, go_ref, sems, osems = refs
    width = x_ref.shape[1]
    heads = width // HEAD
    step = pl.program_id(0)

    copies = weight_copies(core_ref, qplace_ref, qsources, starts[0], w_ref, sems)

    @pl.when(step == 0)
    def _():
        for copy in copies:
            copy.start()
        load_first(core_ref, place_ref, sources, starts[1], wout_ref, osems)
        for ref in (gw_ref, gout_ref, acc_ref):
            ref[...] = jnp.zeros_like(ref)

    low = g_ref[...].astype(BF16)
    go_ref[...] = dot_nt(low, wout_ref[...]).astype(BF16)

    @pl.when(step == 0)
    def _():
        for copy in copies:
            copy.wait()

    edge = seq // 16 * 16
    alive = lax.broadcasted_iota(jnp.int32, (rows - edge, rows), 0) < seq - edge
    left = lax.broadcasted_iota(jnp.int32, (rows, TILE), 1) < HEAD
    zero = jnp.zeros((), BF16)
    work = [(i, h) for i in range(PAIR) for h in range(heads)]

    def tile_of(ref, part, i, h):
        at = part * width + h * HEAD // TILE * TILE
        return ref[i * rows : (i + 1) * rows, at : at + TILE]

    def start(i, h):
        mine = left if h * HEAD % TILE == 0 else ~left
        query = jnp.where(mine, tile_of(qkv_ref, 0, i, h), zero)
        go = jnp.where(mine, tile_of(go_ref, 0, i, h), zero)
        return dot_nt(tile_of(qkv_ref, 1, i, h), query), dot_nt(tile_of(qkv_ref, 2, i, h), go)

    def finish(i, h, probs, gs):
        gvs[i].append(dot(probs, tile_of(go_ref, 0, i, h)))
        gks[i].append(dot(gs, tile_of(qkv_ref, 0, i, h)))
        gqs[i].append((dot(turned_k[i][h * HEAD : (h + 1) * HEAD], gs) * 0.125).astype(BF16))
        span = slice(i * rows, (i + 1) * rows)
        if h % 2:
            for part, held in ((1, gks[i]), (2, gvs[i])):
                at = part * width + h * HEAD // TILE * TILE
                gqkv_ref[span, at : at + TILE] = jnp.where(left, held[h - 1], held[h]).astype(BF16)
        if h == heads - 1:
            gqkv_ref[span, :width] = jnp.concatenate(gqs[i], 0).T

    def post(i):
        span = slice(i * rows, (i + 1) * rows)
        gqkv = gqkv_ref[span, :]
        gw_ref[...] += dot(turned_h[i], gqkv)
        gh = dot_nt(gqkv, w_ref[:, : 3 * width]).astype(BF16).astype(F32)
        acc_ref[2:3, :] += column_sum(gqkv[:, :width].astype(F32))
        acc_ref[3:4, :] += column_sum(gqkv[:, 2 * width :].astype(F32))
        acc_ref[0:1, :] += column_sum(gh * normed[i])
        acc_ref[1:2, :] += column_sum(gh)
        gx = g_ref[span, :] + norm_back(gh, normed[i], scale[i], vec_ref[0:1, :])
        if first:
            gx_ref[i] = gx[:seq]
        else:
            gx_ref[span, :] = gx

    gks, gvs, gqs = ([[] for _ in range(PAIR)] for _ in range(3))
    turned_k = [qkv_ref[i * rows : (i + 1) * rows, width : 2 * width].T for i in range(PAIR)]
    ahead = [start(*item) for item in work[:2]]
    normed, scale, turned_h = [], [], []
    for i in range(PAIR):
        part, size = norm(x_ref[i * rows : (i + 1) * rows, :])
        normed.append(part)
        scale.append(size)
        turned_h.append((part * vec_ref[0:1, :] + vec_ref[1:2, :]).astype(BF16).T)
    behind = []
    for n, (i, h) in enumerate(work):
        if n + 2 < len(work):
            ahead.append(start(*work[n + 2]))
        scores, gp = ahead.pop(0)
        scores = scores - lse_ref[i, h : h + 1, :rows]
        p_low = jnp.exp(scores[:edge])
        p_high = jnp.where(alive, jnp.exp(scores[edge:]), 0.0)
        probs = jnp.concatenate([p_low.astype(BF16), p_high.astype(BF16)], 0)
        gp_low, gp_high = gp[:edge], gp[edge:]
        mean = column_sum(gp_low * p_low) + column_sum(gp_high * p_high)
        gs_low = (p_low * (gp_low - mean)).astype(BF16)
        gs_high = (p_high * (gp_high - mean)).astype(BF16)
        behind.append((i, h, probs, jnp.concatenate([gs_low, gs_high], 0)))
        if len(behind) > 1:
            finish(*behind.pop(0))
    for item in behind:
        finish(*item)
    gout_ref[...] += dot(o_ref[...].T, low)
    acc_ref[4:5, :] += column_sum(g_ref[...])
    for i in range(PAIR):
        post(i)
    @pl.when(step == pl.num_programs(0) - 1)
    def _():
        def one(ref):
            ref[:, : 2 * width] = gw_ref[:, : 2 * width].astype(BF16)
            put_vectors(acc_ref, ref)

        def two(ref):
            ref[:, :width] = gw_ref[:, 2 * width :].astype(BF16)
            ref[:, width : 2 * width] = gout_ref[...].astype(BF16)
            ref[:, 2 * width :] = jnp.zeros((width, TILE), BF16)

        put_grads(core_ref[0], one, two, keep_ref, send_ref)


def adamw(grad, first, second, old):
    first_new = 0.9 * first + 0.1 * grad
    second_new = 0.999 * second + 0.001 * grad * grad
    first_hat = first_new / (1.0 - 0.9**STEP)
    second_hat = second_new / (1.0 - 0.999**STEP)
    change = -0.01 * (first_hat / (jnp.sqrt(second_hat) + 1e-08) + 0.05 * old)
    return (first_new, second_new, change)


def step_kernel(start, core_ref, mine_ref, other_ref, one_ref, two_ref, old_ref, *refs):
    grad_ref, one_new_ref, two_new_ref, change_ref = refs[-4:]
    cols = slice(start, start + grad_ref.shape[2])

    def put(from_ref):
        grad = from_ref[:, cols].astype(F32)
        grad_ref[0] = grad
        one_new_ref[0], two_new_ref[0], change_ref[0] = adamw(grad, one_ref[0], two_ref[0], old_ref[0])

    @pl.when(core_ref[0] == pl.program_id(0))
    def _():
        put(mine_ref)

    @pl.when(core_ref[0] != pl.program_id(0))
    def _():
        put(other_ref)


def smem():
    return pl.BlockSpec(memory_space=pltpu.SMEM)


def whole(shape):
    zeros = (0,) * len(shape)
    return pl.BlockSpec(shape, lambda i: zeros)


def cost(flops, moved, exps):
    return pl.CostEstimate(flops=int(flops), bytes_accessed=int(moved), transcendentals=int(exps))


def params():
    return pltpu.CompilerParams(
        dimension_semantics=("arbitrary",), vmem_limit_bytes=VMEM_LIMIT
    )


def struct(shape, kind):
    return jax.ShapeDtypeStruct(shape, kind)


class Weights:
    def __init__(self, arrays, place, start, half):
        self.arrays, self.place, self.start, self.half = arrays, place, start, half

    def specs(self):
        return [pl.BlockSpec(memory_space=pl.ANY)] * len(self.arrays)

    def sems(self):
        return pltpu.SemaphoreType.DMA((sum(a.shape[0] for a in self.arrays),))


def call(kernel, after, in_specs, **rest):
    count = len(after)

    def run(*refs):
        kernel(*refs[count:])

    made = pl.pallas_call(
        run, in_specs=[pl.BlockSpec(memory_space=pl.ANY)] * count + in_specs, **rest
    )
    return lambda *args: made(*after, *args)


class Layers:
    def __init__(self, core, images, seq, width):
        self.core, self.images, self.seq, self.width = core, images, seq, width
        self.rows = -(-seq // 16) * 16
        self.grid = (images // PAIR,)
        self.total = images * self.rows
        self.block = PAIR * self.rows

    def tall(self, cols):
        return pl.BlockSpec((self.block, cols), lambda i: (i, 0))

    def images_spec(self):
        return pl.BlockSpec((PAIR, self.seq, self.width), lambda i: (i, 0, 0))

    def lse_spec(self):
        return pl.BlockSpec((PAIR, 8, 256), lambda i: (i, 0, 0))

    def attn_forward(self, x, wq, first, after):
        w, t = self.width, self.total
        outs = [
            (self.tall(3 * w), struct((t, 3 * w), BF16)),
            (self.tall(w), struct((t, w), BF16)),
            (self.lse_spec(), struct((self.images, 8, 256), F32)),
            (whole((16, w)), struct((16, w), F32)),
        ]
        if first:
            outs.append((self.tall(w), struct((t, w), F32)))
        return call(
            functools.partial(attn_forward, first, self.seq, self.rows, len(wq.arrays), wq.start),
            after,
            [smem(), smem(), self.images_spec() if first else self.tall(w)] + wq.specs(),
            grid=self.grid,
            out_specs=[o[0] for o in outs],
            out_shape=[o[1] for o in outs],
            scratch_shapes=[pltpu.VMEM((w, 2 * wq.half), BF16), wq.sems()],
            compiler_params=params(),
            cost_estimate=cost(1.7e10, 2e7, 3e6),
        )(self.core, wq.place, x, *wq.arrays)

    def mlp_forward(self, x, o, wr, vec, last, after):
        w, t = self.width, self.total
        outs = [
            (self.tall(w), struct((t, w), F32)),
            (self.tall(FF), struct((t, FF), BF16)),
            (self.tall(FF), struct((t, FF), F32)),
            (self.images_spec(), struct((self.images, self.seq, w), F32))
            if last
            else (self.tall(w), struct((t, w), F32)),
        ]
        return call(
            functools.partial(mlp_forward, last, self.seq, self.rows, len(wr.arrays), wr.start),
            after,
            [smem(), smem(), self.tall(w), self.tall(w), whole(vec.shape)] + wr.specs(),
            grid=self.grid,
            out_specs=[o[0] for o in outs],
            out_shape=[o[1] for o in outs],
            scratch_shapes=[pltpu.VMEM((w, 2 * wr.half), BF16), wr.sems()],
            compiler_params=params(),
            cost_estimate=cost(2.2e10, 3e7, 3e6),
        )(self.core, wr.place, x, o, vec, *wr.arrays)

    def mlp_backward(self, live, g, x1, act, slope, wr, vec, last, after):
        w, t = self.width, self.total
        return call(
            functools.partial(mlp_backward, last, self.seq, self.rows, len(wr.arrays), wr.start),
            after,
            [
                smem(), smem(), smem(),
                self.images_spec() if last else self.tall(w),
                self.tall(w), self.tall(FF), self.tall(FF), whole(vec.shape),
            ]
            + wr.specs(),
            grid=self.grid,
            out_specs=[self.tall(w), whole((w, FF + TILE)), whole((w, FF + TILE))],
            out_shape=[
                struct((t, w), F32), struct((w, FF + TILE), BF16), struct((w, FF + TILE), BF16),
            ],
            scratch_shapes=[
                pltpu.VMEM((w, 2 * wr.half), BF16),
                pltpu.VMEM((w, FF), F32),
                pltpu.VMEM((w, FF), F32),
                pltpu.VMEM((8, w), F32),
                pltpu.VMEM((8, FF), F32),
                pltpu.VMEM((self.block, w), F32),
                wr.sems(),
            ],
            compiler_params=params(),
            cost_estimate=cost(2.4e10, 3e7, 3e6),
        )(self.core, wr.place, live, g, x1, act, slope, vec, *wr.arrays)

    def last_layer(self, live, x, g, wq, wr):
        w, t = self.width, self.total
        outs = [
            (self.tall(3 * w), struct((t, 3 * w), BF16)),
            (self.tall(w), struct((t, w), BF16)),
            (self.lse_spec(), struct((self.images, 8, 256), F32)),
            (whole((16, w)), struct((16, w), F32)),
            (self.images_spec(), struct((self.images, self.seq, w), F32)),
            (self.tall(w), struct((t, w), F32)),
            (whole((w, FF + TILE)), struct((w, FF + TILE), BF16)),
            (whole((w, FF + TILE)), struct((w, FF + TILE), BF16)),
        ]
        return call(
            functools.partial(last_layer, self.seq, self.rows, len(wq.arrays), (wq.start, wr.start)),
            [],
            [smem(), smem(), smem(), self.tall(w), self.images_spec()] + wq.specs(),
            grid=self.grid,
            out_specs=[o[0] for o in outs],
            out_shape=[o[1] for o in outs],
            scratch_shapes=[
                pltpu.VMEM((w, 2 * wq.half), BF16),
                pltpu.VMEM((w, 2 * wr.half), BF16),
                pltpu.VMEM((self.block, w), F32),
                pltpu.VMEM((self.block, FF), BF16),
                pltpu.VMEM((self.block, FF), F32),
                pltpu.VMEM((w, FF), F32),
                pltpu.VMEM((w, FF), F32),
                pltpu.VMEM((8, w), F32),
                pltpu.VMEM((8, FF), F32),
                pltpu.VMEM((self.block, w), F32),
                wq.sems(),
                wr.sems(),
            ],
            compiler_params=params(),
            cost_estimate=cost(4.5e10, 3e7, 3e6),
        )(self.core, wq.place, live, x, g, *wq.arrays)

    def attn_backward(self, g, x, qkv, lse, o, wq, wr, vec, first, after):
        w, t = self.width, self.total
        return call(
            functools.partial(
                attn_backward, first, self.seq, self.rows,
                (len(wq.arrays), len(wr.arrays)), (wq.start, wr.start),
            ),
            after,
            [
                smem(), smem(), smem(), self.tall(w), self.tall(w), self.tall(3 * w),
                self.lse_spec(), self.tall(w), whole(vec.shape),
            ]
            + wq.specs()
            + wr.specs(),
            grid=self.grid,
            out_specs=[
                self.images_spec() if first else self.tall(w),
                whole((w, 2 * w + TILE)), whole((w, 2 * w + TILE)),
            ],
            out_shape=[
                struct((self.images, self.seq, w), F32) if first else struct((t, w), F32),
                struct((w, 2 * w + TILE), BF16), struct((w, 2 * w + TILE), BF16),
            ],
            scratch_shapes=[
                pltpu.VMEM((w, 2 * wq.half), BF16),
                pltpu.VMEM((w, w), BF16),
                pltpu.VMEM((w, 3 * w), F32),
                pltpu.VMEM((w, w), F32),
                pltpu.VMEM((8, w), F32),
                pltpu.VMEM((self.block, 3 * w), BF16),
                pltpu.VMEM((self.block, w), BF16),
                wq.sems(),
                wr.sems(),
            ],
            compiler_params=params(),
            cost_estimate=cost(3e10, 2e7, 3e6),
        )(self.core, wq.place, wr.place, g, x, qkv, lse, o, vec, *wq.arrays, *wr.arrays)


def flip(axis, bit):
    return [(i, i ^ bit) for i in range(lax.axis_size(axis))]


def swap_cores(value):
    return lax.ppermute(value, "rep", flip("rep", 1))


def own_half(packed, core):
    half = packed.shape[1] // 2
    return lax.dynamic_slice_in_dim(packed, core * half, half, 1)


class Gathering:
    def __init__(self, own):
        self.near = [own[None]]
        self.far = [self.neighbour(self.near[0])]
        self.ids = [0]

    @staticmethod
    def neighbour(piece):
        return lax.ppermute(piece, "shard", flip("shard", 1))

    def step(self, bit, anchor=None):
        have = self.near[0] if len(self.near) == 1 else jnp.concatenate(self.near, 0)
        have = have if anchor is None else after(have, anchor)
        self.near.append(lax.ppermute(have, "shard", flip("shard", bit)))
        self.ids += [i ^ bit for i in self.ids]

    def pass_on(self, *anchors):
        piece = after(self.near[-1], *anchors) if anchors else self.near[-1]
        self.far.append(self.neighbour(piece))

    def held(self, anchor=None):
        pieces = self.near + self.far
        if anchor is not None:
            pieces[-1] = after(pieces[-1], anchor)
        return pieces + [swap_cores(p) for p in pieces]

    def place(self):
        me = lax.axis_index("shard").astype(jnp.int32)
        return me ^ jnp.array(self.ids + [i ^ 1 for i in self.ids], jnp.int32)


def after(value, *others):
    return lax.optimization_barrier((value,) + others)[0]


def turn_kernel(in_ref, out_ref):
    for i in range(in_ref.shape[0]):
        out_ref[:, i, :] = in_ref[i]


def turn_images(value):
    images, seq, width = value.shape
    return pl.pallas_call(
        turn_kernel,
        grid=(width // TILE,),
        in_specs=[pl.BlockSpec((images, seq, TILE), lambda i: (0, 0, i))],
        out_specs=pl.BlockSpec((seq, images, TILE), lambda i: (0, 0, i)),
        out_shape=struct((seq, images, width), value.dtype),
        compiler_params=params(),
        cost_estimate=cost(1e6, 5e6, 0),
    )(value)


def join_cores(keep, send):
    other = swap_cores(send)
    return (keep.astype(F32) + other.astype(F32)).astype(BF16)


def exchange_shards(joined):
    count = lax.axis_size("shard")
    rows, cols = joined.shape
    return lax.all_to_all(joined.reshape(count, rows // count, cols), "shard", 0, 0, tiled=True)


def finish_groups(groups):
    mine = jnp.concatenate([jnp.sum(parts.astype(F32), 0).astype(BF16) for parts in groups], 1)
    bit = 2
    while bit < lax.axis_size("rep"):
        other = lax.ppermute(mine, "rep", flip("rep", bit))
        mine = (mine.astype(F32) + other.astype(F32)).astype(BF16)
        bit *= 2
    return mine, swap_cores(mine)


def update_group(core, pair, start, state, outs, layer, at, cols):
    mine, other = pair
    spec = pl.BlockSpec((1, mine.shape[0], cols), lambda j: (layer, 0, at + j))
    shape = struct(state[0].shape, F32)
    given = list(outs) if outs is not None else []
    return pl.pallas_call(
        functools.partial(step_kernel, start),
        grid=(2,),
        in_specs=[smem(), whole(mine.shape), whole(other.shape), spec, spec, spec]
        + [pl.BlockSpec(memory_space=pl.ANY)] * len(given),
        out_specs=[spec] * 4,
        out_shape=[shape] * 4,
        input_output_aliases={6 + i: i for i in range(len(given))},
        compiler_params=params(),
        cost_estimate=cost(1e6, 4e6, 0),
    )(core, mine, other, *state, *given)


def local(
    tokens, weights, vectors, moment_one, moment_two, vector_one, vector_two, images, cotangent
):
    count, seq, width = tokens.shape
    layers = weights.shape[0]
    core = lax.axis_index("rep") % 2
    core_arr = core.reshape(1).astype(jnp.int32)
    plan = Layers(core_arr, count, seq, width)
    packs = []
    whole_weights = weights
    for index in range(layers):
        turned = jnp.pad(vectors[index].T, ((0, 0), (0, TILE - vectors.shape[1])))
        attn_pack = jnp.concatenate([whole_weights[index, :, : 3 * width], turned], 1)
        attn_own = own_half(attn_pack, core).astype(BF16)
        if index == 0:
            whole_weights = after(weights, attn_own)
        rest = whole_weights[index, :, 3 * width :].astype(BF16)
        rest_pack = jnp.pad(rest, ((0, 0), (0, -rest.shape[1] % (2 * TILE))))
        packs.append((attn_own, own_half(rest_pack, core)))
    bits = []
    bit = lax.axis_size("shard") // 2
    while bit > 1:
        bits.append(bit)
        bit //= 2
    attn_own, rest_own = packs[0]
    query = Gathering(attn_own)
    for bit in bits:
        query.step(bit)
        query.pass_on()
    rest = Gathering(after(rest_own, query.near[1]))
    for bit in bits:
        rest.step(bit)
        if bit != bits[-1]:
            rest.pass_on()
    gathered = [[Weights(query.held(), query.place(), 0, attn_own.shape[1]), None]]
    stored = []
    x = tokens
    for index in range(layers):
        first, last = index == 0, index == layers - 1
        if not last:
            ahead = Gathering(after(jnp.concatenate(packs[index + 1], 1), rest.near[1]))
            for bit in bits[:-1]:
                ahead.step(bit)
        if last and not first:
            qkv, o, lse, vec, output, *tail = plan.last_layer(images, x, cotangent, *gathered[index])
            stored.append((x, qkv, o, lse, vec, None, None, None))
            break
        qkv, o, lse, vec, *xp = plan.attn_forward(
            x, gathered[index][0], first, [rest.near[1]] if first else []
        )
        xp = xp[0] if first else x
        if first:
            rest.pass_on(o, rest.far[-1], ahead.far[0])
            gathered[0][1] = Weights(rest.held(o), rest.place(), 0, rest_own.shape[1])
        if not last:
            ahead.pass_on(o)
            ahead.step(bits[-1], o)
        x1, act, slope, x = plan.mlp_forward(
            xp, o, gathered[index][1], vec, last, [] if last else [ahead.near[-1]]
        )
        if not last:
            ahead.pass_on()
            held = ahead.held(x1)
            qhalf, half = (p.shape[1] for p in packs[index + 1])
            gathered.append(
                [Weights(held, ahead.place(), 0, qhalf), Weights(held, ahead.place(), qhalf, half)]
            )
        stored.append((xp, qkv, o, lse, vec, x1, act, slope))
    g = None
    state = (moment_one, moment_two, weights)
    outs, turned = None, None
    tails = {}

    def finish(done, outs):
        pair = finish_groups([parts for parts, _ in done])
        start = 0
        for _, spot in done:
            outs = update_group(core_arr, pair, start, state, outs, *spot)
            start += spot[2]
            mine, other = (p[:, start : start + TILE] for p in pair)
            tails[spot[:2]] = jnp.where(core == 0, mine, other).astype(F32).T
            start += TILE
        return outs

    groups, before = [], []
    for index in reversed(range(layers)):
        first, last = index == 0, index == layers - 1
        wq, wr = gathered[index]
        xp, qkv, o, lse, vec, x1, act, slope = stored[index]
        for half in range(2):
            if half == 0:
                gx1, keep, send = (
                    tail if last else plan.mlp_backward(images, g, x1, act, slope, wr, vec, last, before)
                )
                spot = (index, 1, FF)
            else:
                g, keep, send = plan.attn_backward(gx1, xp, qkv, lse, o, wq, wr, vec, first, before)
                spot = (index, 0, 2 * width)
                if last:
                    turned = turn_images(after(output, g))
                if first:
                    parts, at = groups.pop(0)
                    outs = finish([(after(parts, g), at)], outs)
            if groups and half == 0:
                parts, at = groups[-1]
                keep, send, parts = lax.optimization_barrier((keep, send, parts))
                groups[-1] = parts, at
            joined = join_cores(keep, send)
            if groups and half == 1:
                parts, at = groups[-1]
                joined, turned, outs, parts = lax.optimization_barrier((joined, turned, outs, parts))
                groups[-1] = parts, at
            before = [joined]
            groups.append((exchange_shards(joined), spot))
    output = turned.swapaxes(0, 1)
    outs = finish(groups[:-1], outs)
    parts, spot = groups[-1]
    parts, outs = lax.optimization_barrier((parts, outs))
    outs = finish([(parts, spot)], outs)
    vec_grads = [
        jnp.concatenate([tails[index, 0][:5], tails[index, 1][:7]], 0) for index in range(layers)
    ]
    vector_grad = jnp.stack(vec_grads)
    weight_grad, moment_one_new, moment_two_new, update = outs
    vector_one_new, vector_two_new, vector_update = adamw(
        vector_grad, vector_one, vector_two, vectors
    )
    return (
        output,
        g,
        weight_grad,
        vector_grad,
        moment_one_new,
        moment_two_new,
        vector_one_new,
        vector_two_new,
        update,
        vector_update,
    )


def solution(mesh):
    in_specs = (
        P(("rep", "shard"), None, None),
        P(None, "shard", None),
        P(None, None, "shard"),
        P(None, "shard", None),
        P(None, "shard", None),
        P(None, None, "shard"),
        P(None, None, "shard"),
        P(("rep", "shard")),
        P(("rep", "shard"), None, None),
    )
    out_specs = (
        P(("rep", "shard"), None, None),
        P(("rep", "shard"), None, None),
        P(None, "shard", None),
        P(None, None, "shard"),
        P(None, "shard", None),
        P(None, "shard", None),
        P(None, None, "shard"),
        P(None, None, "shard"),
        P(None, "shard", None),
        P(None, None, "shard"),
    )
    return jax.shard_map(local, mesh=mesh, in_specs=in_specs, out_specs=out_specs, check_vma=False)
```
